32 devices in a mesh: dp: 8 (over y, x, core), prefix: 4 (over z).
Axes of the slice: x: 2, y: 2, z: 4, core: 2. Of those that a mesh axis runs over, the one named last changes fastest.
Arguments:
- hidden_in: bfloat16 [24, 1024, 1024], P('dp'), may hold values from -6 to 6
- cotangent: bfloat16 [24, 1024, 1024], P('dp'), may hold values from -6 to 6
- segment_ids: int32 [24, 1024], P('dp'), may hold values from 0 to 7, never falling along the last dimension, each value on 1 to 512 neighbouring positions
- key_mask: int32 [24, 1024], P('dp'), may hold values 0 or 1
- prefix_keys: bfloat16 [96, 1024], P('prefix'), may hold values from -6 to 6
- prefix_values: bfloat16 [96, 1024], P('prefix'), may hold values from -6 to 6
- w_query: bfloat16 [1024, 1024], P('dp', 'prefix'), may hold values from -0.1875 to 0.1875
- b_query: float32 [1024], P('prefix'), may hold values from -3 to 3
- w_key: bfloat16 [1024, 1024], P('dp', 'prefix'), may hold values from -0.1875 to 0.1875
- b_key: float32 [1024], P('prefix'), may hold values from -3 to 3
- w_value: bfloat16 [1024, 1024], P('dp', 'prefix'), may hold values from -0.1875 to 0.1875
- b_value: float32 [1024], P('prefix'), may hold values from -3 to 3
- w_attn_out: bfloat16 [1024, 1024], P('prefix', 'dp'), may hold values from -1 to 1
- b_attn_out: float32 [1024], replicated, may hold values from -3 to 3
- gain_attn: float32 [1024], replicated, may hold values from 0.1 to 1.9
- shift_attn: float32 [1024], replicated, may hold values from -3 to 3
- w_ffn_in: bfloat16 [1024, 4096], P('dp', 'prefix'), may hold values from -0.1875 to 0.1875
- b_ffn_in: float32 [4096], P('prefix'), may hold values from -3 to 3
- w_ffn_out: bfloat16 [4096, 1024], P('prefix', 'dp'), may hold values from -0.09375 to 0.09375
- b_ffn_out: float32 [1024], replicated, may hold values from -3 to 3
- gain_ffn: float32 [1024], replicated, may hold values from 0.1 to 1.9
- shift_ffn: float32 [1024], replicated, may hold values from -3 to 3
Outputs:
- output: bfloat16 [24, 1024, 1024], P('dp')
- input_grad: bfloat16 [24, 1024, 1024], P('dp')
- prefix_key_grad: float32 [96, 1024], P('prefix')
- prefix_value_grad: float32 [96, 1024], P('prefix')
The draws below stay inside these ranges and needn't reach their ends.
Inputs may be any that keep to these rules, and one draw needn't show every extreme that they name: `segment_ids`: within a row segment numbers never fall; each segment holds 1 to 512 positions, and some segment of each row exactly that many.
All inputs are finite; a program needn't handle non-finite values. No bound on the sum of `key_mask` on one device may be relied on, other than what follows from the above.
Results may differ from the reference program's by a relative error of at most 0.015.
Values may be sent and summed in bfloat16 or wider, within the bound.
A program may use at most 256 MiB of HBM per device.

```python
import math
import jax
import jax.numpy as jnp
import numpy as np
from jax import lax

D = 1024
HEADS = 16
FF = 4096
HEAD_DIM = 64
ROW_LEN = 1024
PREFIX = 96
SEGMENTS = 8
ROWS = 24


def set_ends(values, key, least, high):
    extent = values.shape
    place = [jax.random.randint(jax.random.fold_in(key, axis), (), 0, extent[axis]) for axis in range(len(extent))]
    values = values.at[tuple(place)].set(least)
    longest = extent.index(max(extent))
    place[longest] = (place[longest] + 1) % extent[longest]
    return values.at[tuple(place)].set(high)


def level_of(rng, shape, shards, smallest, largest):
    def one(axis_at, parts):
        heights = jax.random.uniform(jax.random.fold_in(jax.random.fold_in(rng, 6), axis_at), (parts,), jnp.float32, smallest / len(shards), largest / len(shards))
        return jnp.repeat(jnp.exp(heights), shape[axis_at] // parts).reshape((-1,) + (1,) * (len(shape) - axis_at - 1))

    level = one(*shards[0])
    for cut in shards[1:]:
        level = level * one(*cut)
    return level


def profile(amount, total, reach, skew):
    portions = [(1 << 20) // math.isqrt(grade ** skew) + 1 for grade in range(2, amount + 1)]
    rest, given = total - reach - (amount - 1), [1] * (amount - 1)
    while rest > 0:
        candidates = [i for i in range(amount - 1) if given[i] < reach]
        pool, remaining = sum([portions[i] for i in candidates]), rest
        for i in candidates:
            addition = min(reach - given[i], max(1, remaining * portions[i] // pool), rest)
            given[i] = given[i] + addition
            rest = rest - addition
    return np.array([reach] + given)


def uneven(stream_key, number_of, total, bound, skew):
    if number_of == 2:
        one = jax.random.randint(stream_key, (), max(1, total - bound), min(bound, total - 1) + 1)
        return jnp.stack([one, total - one])
    lengths = jnp.asarray(profile(number_of, total, bound, skew), jnp.int32)
    couples = (number_of - 1) // 2
    donor, sink = lengths[1:1 + 2 * couples:2], lengths[2:2 + 2 * couples:2]
    margin = jnp.minimum(donor - 1, bound - sink)
    shifted = jax.random.randint(jax.random.fold_in(stream_key, 1), (couples,), 0, 1 << 20) % (margin + 1)
    lengths = lengths.at[1:1 + 2 * couples:2].set(donor - shifted).at[2:2 + 2 * couples:2].set(sink + shifted)
    return lengths[jax.random.permutation(jax.random.fold_in(stream_key, 2), number_of)]


def centred(stream_key, shape, width, reach, split=(), kind=jnp.bfloat16):
    entries = jax.random.normal(stream_key, shape, jnp.float32) * width
    if len(split) > 0:
        entries = level_of(stream_key, shape, split, -0.22, 0.18) * entries
    return jnp.clip(entries, min=-reach, max=reach).astype(kind)


def setup_inputs(seed: int = 0) -> dict:
    streams_of = jax.random.split(jax.random.key(seed), 23)
    hidden_in = centred(streams_of[0], (ROWS, ROW_LEN, D), 1.0, 6.0, ((0, 8),))
    cotangent = centred(streams_of[1], (ROWS, ROW_LEN, D), 1.0, 6.0, ((0, 8),))
    segment_ids = jax.vmap(lambda own: jnp.searchsorted(jnp.cumsum(uneven(own, SEGMENTS, ROW_LEN, ROW_LEN // 2, 1)), jnp.arange(ROW_LEN), side="right"))(jax.random.split(streams_of[2], ROWS)).reshape((ROWS, ROW_LEN)).astype(jnp.int32)
    key_mask = set_ends((jax.random.randint(streams_of[3], (ROWS, ROW_LEN), 0, 8) < 7).astype(jnp.int32), jax.random.fold_in(streams_of[3], 1), 0, 1)
    prefix_keys = centred(streams_of[4], (PREFIX, D), 1.0, 6.0, ((0, 4),))
    prefix_values = centred(streams_of[5], (PREFIX, D), 1.0, 6.0, ((0, 4),))
    w_query = centred(streams_of[6], (D, D), D ** -0.5, 0.1875, ((0, 8), (1, 4)))
    b_query = centred(streams_of[7], (D,), 0.5, 3.0, ((0, 4),), jnp.float32)
    w_key = centred(streams_of[8], (D, D), D ** -0.5, 0.1875, ((0, 8), (1, 4)))
    b_key = centred(streams_of[9], (D,), 0.5, 3.0, ((0, 4),), jnp.float32)
    w_value = centred(streams_of[10], (D, D), D ** -0.5, 0.1875, ((0, 8), (1, 4)))
    b_value = centred(streams_of[11], (D,), 0.5, 3.0, ((0, 4),), jnp.float32)
    w_attn_out = centred(streams_of[12], (D, D), (D // 32) ** -0.5, 1.0, ((0, 4), (1, 8)))
    b_attn_out = centred(streams_of[13], (D,), 0.5, 3.0, (), jnp.float32)
    gain_attn = jnp.clip(1.0 + 0.18 * jax.random.normal(streams_of[14], (D,), jnp.float32), 0.1, 1.9)
    shift_attn = centred(streams_of[15], (D,), 0.5, 3.0, (), jnp.float32)
    w_ffn_in = centred(streams_of[16], (D, FF), D ** -0.5, 0.1875, ((0, 8), (1, 4)))
    b_ffn_in = centred(streams_of[17], (FF,), 0.5, 3.0, ((0, 4),), jnp.float32)
    w_ffn_out = centred(streams_of[18], (FF, D), FF ** -0.5, 0.09375, ((0, 4), (1, 8)))
    b_ffn_out = centred(streams_of[19], (D,), 0.5, 3.0, (), jnp.float32)
    gain_ffn = jnp.clip(1.0 + 0.18 * jax.random.normal(streams_of[20], (D,), jnp.float32), 0.1, 1.9)
    shift_ffn = centred(streams_of[21], (D,), 0.5, 3.0, (), jnp.float32)
    return {"hidden_in": hidden_in, "cotangent": cotangent, "segment_ids": segment_ids, "key_mask": key_mask, "prefix_keys": prefix_keys, "prefix_values": prefix_values, "w_query": w_query, "b_query": b_query, "w_key": w_key, "b_key": b_key, "w_value": w_value, "b_value": b_value, "w_attn_out": w_attn_out, "b_attn_out": b_attn_out, "gain_attn": gain_attn, "shift_attn": shift_attn, "w_ffn_in": w_ffn_in, "b_ffn_in": b_ffn_in, "w_ffn_out": w_ffn_out, "b_ffn_out": b_ffn_out, "gain_ffn": gain_ffn, "shift_ffn": shift_ffn}


@jax.custom_vjp
def low(v):
    return lax.optimization_barrier(v.astype(jnp.bfloat16)).astype(jnp.float32)

@jax.custom_vjp
def low_back(v):
    return v

def low_keep(v):
    return (low(v), None)

def low_pass(kept, grad):
    return (grad,)

def back_keep(v):
    return (v, None)

def back_low(kept, grad):
    return (low(grad),)
low.defvjp(low_keep, low_pass)
low_back.defvjp(back_keep, back_low)
EPSILON = 1e-05
NEGATIVE = -1e+30

def dense(left, right):
    return jnp.dot(left, right, precision=lax.Precision.HIGHEST)

def layer_norm(values, gain, shift):
    center = values - lax.optimization_barrier(jnp.mean(values, axis=-1, keepdims=True))
    spread = lax.optimization_barrier(jnp.mean(center * center, axis=-1, keepdims=True))
    return center * lax.rsqrt(spread + EPSILON) * gain + shift

def layer_row(row_in, seg_row, pad_row, pre_keys, pre_values, params):
    w_query, b_query, w_key, b_key, w_value, b_value, w_attn_out, b_attn_out, gain_attn, shift_attn, w_ffn_in, b_ffn_in, w_ffn_out, b_ffn_out, gain_ffn, shift_ffn = params
    queries = low(low_back(dense(row_in, w_query) + b_query))
    key_rows = low(low_back(dense(row_in, w_key) + b_key))
    value_rows = low(low_back(dense(row_in, w_value) + b_value))
    all_keys = jnp.concatenate([key_rows, pre_keys], axis=0).reshape(ROW_LEN + PREFIX, HEADS, HEAD_DIM)
    all_values = jnp.concatenate([value_rows, pre_values], axis=0).reshape(ROW_LEN + PREFIX, HEADS, HEAD_DIM)
    heads_query = queries.reshape(ROW_LEN, HEADS, HEAD_DIM)
    scores = jnp.einsum('qhd,khd->hqk', heads_query, all_keys, precision=lax.Precision.HIGHEST) * HEAD_DIM ** (-0.5)
    scores = low_back(scores)
    same_doc = (seg_row[:, None] == seg_row[None, :]) & (pad_row[None, :] == 1)
    allowed = jnp.concatenate([same_doc, jnp.ones((ROW_LEN, PREFIX), jnp.bool_)], axis=1)
    masked = jnp.where(allowed[None], scores, NEGATIVE)
    weights_low = low(jax.nn.softmax(masked, axis=-1))
    context = jnp.einsum('hqk,khd->qhd', weights_low, all_values, precision=lax.Precision.HIGHEST)
    context = low(low_back(context.reshape(ROW_LEN, D)))
    attended = low_back(dense(context, w_attn_out) + b_attn_out)
    normed = layer_norm(row_in + attended, gain_attn, shift_attn)
    hidden_pre = low_back(dense(low(normed), w_ffn_in) + b_ffn_in)
    activated = low(jax.nn.gelu(hidden_pre, approximate=False))
    branch = low_back(dense(activated, w_ffn_out) + b_ffn_out)
    return layer_norm(normed + branch, gain_ffn, shift_ffn)

def reference(hidden_in, cotangent, segment_ids, key_mask, prefix_keys, prefix_values, w_query, b_query, w_key, b_key, w_value, b_value, w_attn_out, b_attn_out, gain_attn, shift_attn, w_ffn_in, b_ffn_in, w_ffn_out, b_ffn_out, gain_ffn, shift_ffn):
    params = tuple((item.astype(jnp.float32) for item in (w_query, b_query, w_key, b_key, w_value, b_value, w_attn_out, b_attn_out, gain_attn, shift_attn, w_ffn_in, b_ffn_in, w_ffn_out, b_ffn_out, gain_ffn, shift_ffn)))
    row_step = jax.checkpoint(layer_row)

    def forward(rows_in, pre_keys, pre_values):

        def one_row(packed):
            row_in, seg_row, pad_row = packed
            return row_step(row_in, seg_row, pad_row, pre_keys, pre_values, params)
        return lax.map(one_row, (rows_in, segment_ids, key_mask))
    outputs, pullback = jax.vjp(forward, hidden_in.astype(jnp.float32), prefix_keys.astype(jnp.float32), prefix_values.astype(jnp.float32))
    input_grad, key_grad, value_grad = pullback(cotangent.astype(jnp.float32))
    return (outputs.astype(jnp.bfloat16), input_grad.astype(jnp.bfloat16), key_grad, value_grad)
```

```python
import functools
import jax
import jax.numpy as jnp
from jax import lax
from jax.experimental import pallas as pl
from jax.experimental.pallas import tpu as pltpu
from jax.sharding import PartitionSpec as P

L = 1024
D = 1024
PRE = 96
BLK = 128
NEG = -1e30
CLASSES = (2, 3, 4, 5, 6, 8)
bf16 = jnp.bfloat16
f32 = jnp.float32


def nt(a, b):
    return lax.dot_general(a, b, (((1,), (1,)), ((), ())), preferred_element_type=f32)


def nn(a, b):
    return jnp.dot(a, b, preferred_element_type=f32)


def stack_heads(tile):
    lane = lax.broadcasted_iota(jnp.int32, tile.shape, 1)
    zero = jnp.zeros_like(tile)
    return jnp.concatenate([jnp.where(lane < 64, tile, zero), jnp.where(lane >= 64, tile, zero)], axis=0)


def windows(seg):
    tiles = seg.shape[-1] // BLK
    first = seg[..., ::BLK]
    last = seg[..., BLK - 1 :: BLK]
    start = jnp.sum((seg[..., None, :] < first[..., :, None]).astype(jnp.int32), axis=-1) // BLK
    stop = (jnp.sum((seg[..., None, :] <= last[..., :, None]).astype(jnp.int32), axis=-1) + BLK - 1) // BLK
    need = stop - start
    size = jnp.full_like(need, CLASSES[-1])
    for n in reversed(CLASSES[:-1]):
        size = jnp.where(need <= n, n, size)
    start = jnp.minimum(start, tiles - size)
    return jnp.stack([start, size], axis=-1)


def attn_fwd_kernel(rows, win, x, w, b, pk, pv, segk, segq, qkv, ctx, lse, kx, vt):
    row = pl.program_id(0)
    y = nn(x[0], w[0]) + b[0]
    q = (y[:, :256].astype(bf16) * 0.125).astype(bf16)
    qkv[0, 0, :, :256] = q
    kv = y[:, 256:].astype(bf16)
    qkv[0, 0, :, 256:] = kv
    kx[:L] = kv[:, :256]
    kx[L:] = pk[0]
    vt[:, :L] = kv[:, 256:].T
    vt[:, L:] = pv[0].T

    def tile(t, carry):
        start = win[row, t, 0]
        size = win[row, t, 1]
        q0 = pl.multiple_of(t * BLK, BLK)
        k0 = pl.multiple_of(start * BLK, BLK)

        def run(n):
            W = n * BLK
            mask = segk[0, pl.ds(k0, W), :] == segq[0, :, pl.ds(q0, BLK)]
            for p in range(2):
                lanes = slice(128 * p, 128 * p + 128)
                q2 = stack_heads(qkv[0, 0, pl.ds(q0, BLK), lanes])
                s = nt(kx[pl.ds(k0, W), lanes], q2)
                s = jnp.concatenate([jnp.where(mask, s[:, :128], NEG), jnp.where(mask, s[:, 128:], NEG)], axis=1)
                sp = nt(kx[L : L + PRE, lanes], q2)
                top = jnp.maximum(jnp.max(s, axis=0, keepdims=True), jnp.max(sp, axis=0, keepdims=True))
                e = jnp.exp(s - top)
                ep = jnp.exp(sp - top)
                total = jnp.sum(e, axis=0, keepdims=True) + jnp.sum(ep, axis=0, keepdims=True)
                o = nn(vt[lanes, pl.ds(k0, W)], e.astype(bf16)) + nn(vt[lanes, L : L + PRE], ep.astype(bf16))
                o = o * (1.0 / total)
                o = jnp.concatenate([o[:64, :128], o[64:, 128:]], axis=0)
                ctx[0, pl.ds(q0, BLK), lanes] = o.T.astype(bf16)
                lt = top + jnp.log(total)
                lse[0, 0, 2 * p : 2 * p + 1, pl.ds(q0, BLK)] = lt[:, :128]
                lse[0, 0, 2 * p + 1 : 2 * p + 2, pl.ds(q0, BLK)] = lt[:, 128:]

        for n in CLASSES:
            pl.when(size == n)(functools.partial(run, n))
        return carry

    lax.fori_loop(0, L // BLK, tile, 0)


def attn_fwd(rows, win, x, w, b, pk, pv, segk, segq):
    R = rows.shape[0]
    row = lambda r, g, *_: (r, 0, 0)
    grp = lambda r, g, *_: (g, 0, 0)
    return pl.pallas_call(
        attn_fwd_kernel,
        grid_spec=pltpu.PrefetchScalarGridSpec(
            num_scalar_prefetch=2,
            grid=(R, 4),
            in_specs=[
                pl.BlockSpec((1, L, D), lambda r, g, rows, win: (rows[r], 0, 0)),
                pl.BlockSpec((1, D, 768), grp),
                pl.BlockSpec((1, 1, 768), grp),
                pl.BlockSpec((1, 128, 256), grp),
                pl.BlockSpec((1, 128, 256), grp),
                pl.BlockSpec((1, L, 128), row),
                pl.BlockSpec((1, 1, L), row),
            ],
            out_specs=[
                pl.BlockSpec((1, 1, L, 768), lambda r, g, *_: (r, g, 0, 0)),
                pl.BlockSpec((1, L, 256), lambda r, g, *_: (r, 0, g)),
                pl.BlockSpec((1, 1, 4, L), lambda r, g, *_: (r, g, 0, 0)),
            ],
            scratch_shapes=[pltpu.VMEM((L + 128, 256), bf16), pltpu.VMEM((256, L + 128), bf16)],
        ),
        out_shape=[
            jax.ShapeDtypeStruct((R, 4, L, 768), bf16),
            jax.ShapeDtypeStruct((R, L, D), bf16),
            jax.ShapeDtypeStruct((R, 4, 4, L), f32),
        ],
        compiler_params=pltpu.CompilerParams(vmem_limit_bytes=48 << 20),
        name="attn_fwd",
    )(rows, win, x, w, b, pk, pv, segk, segq)


def attn_bwd_kernel(r, rows, win, qkv, ctx, gctx, lse, pk, pv, segk, segq, gfirst, w, *rest):
    gin, pkg, pvg, dqt, dall, delta = rest[-6:]
    row = r
    g = pl.program_id(0)
    prod = gctx[0].astype(f32) * ctx[0].astype(f32)
    head = lax.broadcasted_iota(jnp.int32, (8, 256), 0)
    lane = lax.broadcasted_iota(jnp.int32, (8, 256), 1)
    pick = (lane // 64 == head).astype(f32)
    delta[...] = lax.dot_general(
        pick, prod, (((1,), (1,)), ((), ())), precision=lax.Precision.HIGHEST, preferred_element_type=f32
    )

    def block(kt, vt, mask, p, q0, W, first):
        n = kt.shape[0]
        lanes = slice(128 * p, 128 * p + 128)
        k2 = stack_heads(kt)
        v2 = stack_heads(vt)
        qw = qkv[0, 0, pl.ds(q0, W), lanes]
        dow = gctx[0, pl.ds(q0, W), lanes]
        s = nt(k2, qw)
        dp = nt(v2, dow)
        ps, ds = [], []
        for h in range(2):
            lrow = lse[0, 0, 2 * p + h : 2 * p + h + 1, pl.ds(q0, W)]
            drow = delta[2 * p + h : 2 * p + h + 1, pl.ds(q0, W)]
            sh = s[h * n : h * n + n] - lrow
            if mask is not None:
                sh = jnp.where(mask, sh, NEG)
            ph = jnp.exp(sh)
            ps.append(ph.astype(bf16))
            ds.append((ph * (dp[h * n : h * n + n] - drow)).astype(bf16))
        pb = jnp.concatenate(ps, axis=0)
        db = jnp.concatenate(ds, axis=0)
        dv = nn(pb, dow)
        dk = nn(db, qw)
        part = nn(k2.T, db)
        if first:
            dqt[lanes, pl.ds(q0, W)] = part
        else:
            dqt[lanes, pl.ds(q0, W)] += part
        lane = lax.broadcasted_iota(jnp.int32, (n, 128), 1)
        return jnp.where(lane < 64, dk[:n], dk[n:]), jnp.where(lane < 64, dv[:n], dv[n:])

    for p in range(2):
        lanes = slice(128 * p, 128 * p + 128)
        sk = jnp.zeros((PRE, 128), f32)
        sv = jnp.zeros((PRE, 128), f32)
        for c in range(2):
            dk, dv = block(pk[0, :PRE, lanes], pv[0, :PRE, lanes], None, p, c * 512, 512, True)
            sk = sk + dk
            sv = sv + dv
        pkg[:, lanes] = sk
        pvg[:, lanes] = sv

    def tile(t, carry):
        start = win[row, t, 0]
        size = win[row, t, 1]
        k0 = pl.multiple_of(t * BLK, BLK)
        q0 = pl.multiple_of(start * BLK, BLK)

        def run(n):
            W = n * BLK
            sk = segk[0, pl.ds(k0, BLK), :]
            sq = segq[0, :, pl.ds(q0, W)]
            mask = jnp.concatenate([sk] * n, axis=1) == sq
            for p in range(2):
                kt = qkv[0, 0, pl.ds(k0, BLK), 256 + 128 * p : 384 + 128 * p]
                vt = qkv[0, 0, pl.ds(k0, BLK), 512 + 128 * p : 640 + 128 * p]
                dk, dv = block(kt, vt, mask, p, q0, W, False)
                dall[g, pl.ds(k0, BLK), 256 + 128 * p : 384 + 128 * p] = dk.astype(bf16)
                dall[g, pl.ds(k0, BLK), 512 + 128 * p : 640 + 128 * p] = dv.astype(bf16)

        for n in CLASSES:
            pl.when(size == n)(functools.partial(run, n))
        return carry

    lax.fori_loop(0, L // BLK, tile, 0)
    dall[g, :, :256] = (dqt[...].T * 0.125).astype(bf16)

    @pl.when(g == 3)
    def _():
        def cols(c, carry):
            c0 = pl.multiple_of(c * 256, 256)
            acc = gfirst[0, :, pl.ds(c0, 256)].astype(f32)
            for i in range(4):
                acc = acc + nt(dall[i], w[i, pl.ds(c0, 256), :])
            gin[0, :, pl.ds(c0, 256)] = acc.astype(bf16)
            return carry

        lax.fori_loop(0, 4, cols, 0)


def attn_bwd(r, rows, win, qkv, ctx, gctx, lse, pk, pv, segk, segq, gfirst, w, into=None):
    row = lambda g, *_: (r, 0, 0)
    grp = lambda g, *_: (g, 0, 0)
    rg = lambda g, *_: (r, g, 0, 0)
    cg = lambda g, *_: (r, 0, g)
    extra = [] if into is None else [into]
    return pl.pallas_call(
        functools.partial(attn_bwd_kernel, r),
        grid_spec=pltpu.PrefetchScalarGridSpec(
            num_scalar_prefetch=2,
            grid=(4,),
            in_specs=[
                pl.BlockSpec((1, 1, L, 768), rg),
                pl.BlockSpec((1, L, 256), cg),
                pl.BlockSpec((1, L, 256), cg),
                pl.BlockSpec((1, 1, 4, L), rg),
                pl.BlockSpec((1, 128, 256), grp),
                pl.BlockSpec((1, 128, 256), grp),
                pl.BlockSpec((1, L, 128), row),
                pl.BlockSpec((1, 1, L), row),
                pl.BlockSpec((1, L, D), row),
                pl.BlockSpec((4, D, 768), lambda g, *_: (0, 0, 0)),
            ]
            + [pl.BlockSpec(memory_space=pl.ANY) for _ in extra],
            out_specs=[
                pl.BlockSpec((1, L, D), lambda g, rows, win: (rows[r], 0, 0)),
                pl.BlockSpec((PRE, 256), lambda g, *_: (0, g)),
                pl.BlockSpec((PRE, 256), lambda g, *_: (0, g)),
            ],
            scratch_shapes=[
                pltpu.VMEM((256, L), f32),
                pltpu.VMEM((4, L, 768), bf16),
                pltpu.VMEM((8, L), f32),
            ],
        ),
        out_shape=[
            jax.ShapeDtypeStruct((3, L, D), bf16),
            jax.ShapeDtypeStruct((PRE, D), f32),
            jax.ShapeDtypeStruct((PRE, D), f32),
        ],
        input_output_aliases={12: 0} if extra else {},
        compiler_params=pltpu.CompilerParams(vmem_limit_bytes=56 << 20),
        name="attn_bwd",
    )(rows, win, qkv, ctx, gctx, lse, pk, pv, segk, segq, gfirst, w, *extra)


HC = 512
TM = 512
EPS = 1e-5


ERF = (0.7978849414895208, 0.03633308441063725, -3.2594747109729314e-05, -5.5306315505082965e-05,
       3.964772884359942e-06, -1.3226625462816106e-07, 1.7562766828961903e-09)


def gelu_parts(v):
    u = v * v
    w = jnp.minimum(u, 31.36)
    p = ERF[6] * w + ERF[5]
    for c in ERF[4::-1]:
        p = p * w + c
    phi = 0.5 * jnp.tanh(v * p) + 0.5
    return v * phi, phi


def norm_stats(z):
    mean = jnp.mean(z, axis=1, keepdims=True)
    c = z - mean
    var = jnp.mean(c * c, axis=1, keepdims=True)
    r = lax.rsqrt(var + EPS)
    return c * r, r


RC = 512


def tokens_kernel(rows, ctx, x, cot, wo, win, wout, bo, g1, s1, bi, b2, g2, s2, out, gf, gc, xhat, zbuf, low, act, gp, rs, vb):
    M = TM

    def dot_cols(i, carry):
        c0 = pl.multiple_of(i * 256, 256)
        zbuf[:, pl.ds(c0, 256)] = nn(ctx[...], wo[:, pl.ds(c0, 256)]) + x[:, pl.ds(c0, 256)].astype(f32)
        return carry

    lax.fori_loop(0, 4, dot_cols, 0, unroll=4)

    def ln1(i, carry):
        r0 = pl.multiple_of(i * RC, RC)
        n, r = norm_stats(zbuf[pl.ds(r0, RC), :] + bo[...])
        xhat[pl.ds(r0, RC), :] = n
        rs[pl.ds(r0, RC), :] = jnp.broadcast_to(r, (RC, 128))
        y = n * g1[...] + s1[...]
        zbuf[pl.ds(r0, RC), :] = y
        low[pl.ds(r0, RC), :] = y.astype(bf16)
        return carry

    lax.fori_loop(0, M // RC, ln1, 0)

    def up(i, carry):
        z, c = i // 2, i % 2
        c0 = pl.multiple_of(c * HC, HC)
        h0 = pl.multiple_of(i * HC, HC)
        h = nn(low[...], win[z, :, pl.ds(c0, HC)]) + bi[:, pl.ds(h0, HC)]
        a, d = gelu_parts(h)
        act[:, pl.ds(h0, HC)] = a.astype(bf16)
        gp[:, pl.ds(h0, HC)] = d.astype(bf16)
        vb[:, pl.ds(h0, HC)] = h.astype(bf16)
        return carry

    lax.fori_loop(0, 8, up, 0, unroll=8)

    def down(i, carry):
        c0 = pl.multiple_of(i * 256, 256)
        zbuf[:, pl.ds(c0, 256)] += nn(act[...], wout[:, pl.ds(c0, 256)])
        return carry

    lax.fori_loop(0, 4, down, 0, unroll=4)

    def ln2(i, carry):
        r0 = pl.multiple_of(i * RC, RC)
        n, r = norm_stats(zbuf[pl.ds(r0, RC), :] + b2[...])
        out[pl.ds(r0, RC), :] = (n * g2[...] + s2[...]).astype(bf16)
        g = cot[pl.ds(r0, RC), :].astype(f32) * g2[...]
        m1 = jnp.mean(g, axis=1, keepdims=True)
        m2 = jnp.mean(g * n, axis=1, keepdims=True)
        d = (g - m1 - n * m2) * r
        zbuf[pl.ds(r0, RC), :] = d
        low[pl.ds(r0, RC), :] = d.astype(bf16)
        return carry

    lax.fori_loop(0, M // RC, ln2, 0)

    def back(i, carry):
        h0 = pl.multiple_of(i * HC, HC)
        d = nt(low[...], wout[pl.ds(h0, HC), :])
        v = vb[:, pl.ds(h0, HC)].astype(f32)
        slope = gp[:, pl.ds(h0, HC)].astype(f32) + v * (jnp.exp(-0.5 * v * v) * 0.3989422804014327)
        act[:, pl.ds(h0, HC)] = (d * slope).astype(bf16)
        return carry

    lax.fori_loop(0, 8, back, 0, unroll=8)

    def back2(i, carry):
        c0 = pl.multiple_of(i * 256, 256)
        acc = zbuf[:, pl.ds(c0, 256)]
        for z in range(4):
            acc = acc + nt(act[:, 1024 * z : 1024 * z + 1024], win[z, pl.ds(c0, 256), :])
        zbuf[:, pl.ds(c0, 256)] = acc
        return carry

    lax.fori_loop(0, 4, back2, 0, unroll=4)

    def ln1b(i, carry):
        r0 = pl.multiple_of(i * RC, RC)
        n = xhat[pl.ds(r0, RC), :]
        g = zbuf[pl.ds(r0, RC), :] * g1[...]
        m1 = jnp.mean(g, axis=1, keepdims=True)
        m2 = jnp.mean(g * n, axis=1, keepdims=True)
        d = (g - m1 - n * m2) * rs[pl.ds(r0, RC), 0:1]
        gf[pl.ds(r0, RC), :] = d.astype(bf16)
        return carry

    lax.fori_loop(0, M // RC, ln1b, 0)

    def gcols(i, carry):
        c0 = pl.multiple_of(i * 256, 256)
        gc[:, pl.ds(c0, 256)] = nt(gf[...], wo[pl.ds(c0, 256), :]).astype(bf16)
        return carry

    lax.fori_loop(0, 4, gcols, 0, unroll=4)


def tokens(rows, ctx, x, cot, wo, win, wout, bo, g1, s1, bi, b2, g2, s2):
    R = ctx.shape[0]
    per = L // TM
    own = pl.BlockSpec((None, TM, D), lambda i, rows: (i // per, i % per, 0))
    pick = pl.BlockSpec((None, TM, D), lambda i, rows: (rows[i // per], i % per, 0))
    whole = lambda a: pl.BlockSpec(a.shape, lambda i, rows: (0,) * a.ndim, pipeline_mode=pl.Buffered(1))
    consts = (wo, win, wout, bo, g1, s1, bi, b2, g2, s2)
    return pl.pallas_call(
        tokens_kernel,
        grid_spec=pltpu.PrefetchScalarGridSpec(
            num_scalar_prefetch=1,
            grid=(R * per,),
            in_specs=[own, pick, pick] + [whole(a) for a in consts],
            out_specs=[pick, own, own],
            scratch_shapes=[
                pltpu.VMEM((TM, D), f32),
                pltpu.VMEM((TM, D), f32),
                pltpu.VMEM((TM, D), bf16),
                pltpu.VMEM((TM, 4 * D), bf16),
                pltpu.VMEM((TM, 4 * D), bf16),
                pltpu.VMEM((TM, 128), f32),
                pltpu.VMEM((TM, 4 * D), bf16),
            ],
        ),
        out_shape=[
            jax.ShapeDtypeStruct((3, L, D), bf16),
            jax.ShapeDtypeStruct((R, L, D), bf16),
            jax.ShapeDtypeStruct((R, L, D), bf16),
        ],
        compiler_params=pltpu.CompilerParams(vmem_limit_bytes=60 << 20),
        name="tokens",
    )(rows, ctx, x, cot, *consts)


KINDS = 10
STEPS = ((0, 0), (1, -1), (1, 1), (2, -1), (2, 1), (3, -1), (3, 1))


def gather_kernel(pre_s, vec_s, wq, wk, wv, wo_s, wi_s, wu_s, pre, vec, qkv, wo, wi, wu, lsem, ssem, rsem):
    d = lax.axis_index("dp")
    z = lax.axis_index("prefix")
    core, xx, yy = d % 2, (d // 2) % 2, d // 4
    dc = d + 1 - 2 * core
    dx = d + 2 - 4 * xx
    dy = d + 4 - 8 * yy
    dxy = dx + dy - d

    def region(pay, zz, dd, half=None):
        if pay >= 4:
            return (pre, vec)[pay - 4].at[zz]
        if pay == 0:
            n, ref = 128, lambda o, s: qkv.at[zz, pl.ds(128 * dd + o, s), :]
        elif pay == 1:
            n, ref = 256, lambda o, s: wo.at[pl.ds(256 * zz + o, s), pl.ds(128 * dd, 128)]
        elif pay == 2:
            n, ref = 128, lambda o, s: wi.at[zz, pl.ds(128 * dd + o, s), :]
        else:
            n, ref = 1024, lambda o, s: wu.at[pl.ds(1024 * zz + o, s), pl.ds(128 * dd, 128)]
        return ref(0, n) if half is None else ref(half * (n // 2), n // 2)

    local = [
        pltpu.make_async_copy(src, dst, lsem.at[i])
        for i, (src, dst) in enumerate(
            [
                (wq, qkv.at[z, pl.ds(128 * d, 128), 0:256]),
                (wk, qkv.at[z, pl.ds(128 * d, 128), 256:512]),
                (wv, qkv.at[z, pl.ds(128 * d, 128), 512:768]),
                (wo_s, region(1, z, d)),
                (wi_s, region(2, z, d)),
                (wu_s, region(3, z, d)),
                (pre_s, pre.at[z]),
                (vec_s, vec.at[z]),
            ]
        )
    ]
    for c in local:
        c.start()
    bar = pltpu.get_barrier_semaphore()

    def hello(dev):
        pl.semaphore_signal(bar, inc=1, device_id=dev, device_id_type=pl.DeviceIdType.MESH)

    for dd in (dc, dx, dy):
        hello((dd, z))

    @pl.when(z > 0)
    def _():
        hello((d, z - 1))

    @pl.when(z < 3)
    def _():
        hello((d, z + 1))

    peers = jnp.where(z > 0, 1, 0) + jnp.where(z < 3, 1, 0)
    pl.semaphore_wait(bar, 3 + peers)
    for c in local:
        c.wait()

    def copy(kind, pay, zz, dd, half, dev, skind):
        r = region(pay, zz, dd, half)
        return pltpu.make_async_remote_copy(
            src_ref=r, dst_ref=r, send_sem=ssem.at[pay * 4 + zz, skind], recv_sem=rsem.at[pay * 4 + zz, kind],
            device_id=dev, device_id_type=pl.DeviceIdType.MESH,
        )

    def guard(step, fn):
        delta, side = step
        zz = z + delta * side
        if delta == 0:
            fn(zz)
        elif side < 0:
            pl.when(z >= delta)(lambda: fn(zz))
        else:
            pl.when(z + delta <= 3)(lambda: fn(zz))

    def stage1(pay, step):
        def run(zz):
            delta, side = step
            if delta:
                copy(0, pay, zz, d, None, (d, z), 0).wait_recv()
            if side <= 0:
                pl.when(z < 3)(lambda: copy(0, pay, zz, d, None, (d, z + 1), 10).start())
            if side >= 0:
                pl.when(z > 0)(lambda: copy(0, pay, zz, d, None, (d, z - 1), 0).start())
            if pay >= 4:
                return
            copy(1, pay, zz, d, None, (dx, z), 1).start()
            copy(2, pay, zz, d, None, (dy, z), 2).start()
            copy(5, pay, zz, d, None, (dc, z), 5).start()
        guard(step, run)

    def stage2(pay, step):
        def run(zz):
            copy(1, pay, zz, dx, None, (dx, z), 1).wait_recv()
            copy(3, pay, zz, dx, 0, (dy, z), 3).start()
            copy(6, pay, zz, dx, None, (dc, z), 6).start()
            copy(2, pay, zz, dy, None, (dy, z), 2).wait_recv()
            copy(4, pay, zz, dy, 1, (dx, z), 4).start()
            copy(7, pay, zz, dy, None, (dc, z), 7).start()
        guard(step, run)

    def stage3(pay, step):
        def run(zz):
            copy(3, pay, zz, dxy, 0, (dy, z), 3).wait_recv()
            copy(8, pay, zz, dxy, 0, (dc, z), 8).start()
            copy(4, pay, zz, dxy, 1, (dx, z), 4).wait_recv()
            copy(9, pay, zz, dxy, 1, (dc, z), 9).start()
        guard(step, run)

    def stage4(pay, step):
        o = dc - d
        def run(zz):
            copy(5, pay, zz, d + o, None, (dc, z), 5).wait_recv()
            copy(6, pay, zz, dx + o, None, (dc, z), 6).wait_recv()
            copy(7, pay, zz, dy + o, None, (dc, z), 7).wait_recv()
            copy(8, pay, zz, dxy + o, 0, (dc, z), 8).wait_recv()
            copy(9, pay, zz, dxy + o, 1, (dc, z), 9).wait_recv()
        guard(step, run)

    def drain(pay, step):
        def run(zz):
            delta, side = step
            if side <= 0:
                pl.when(z < 3)(lambda: copy(0, pay, zz, d, None, (d, z + 1), 10).wait_send())
            if side >= 0:
                pl.when(z > 0)(lambda: copy(0, pay, zz, d, None, (d, z - 1), 0).wait_send())
            if pay >= 4:
                return
            copy(1, pay, zz, d, None, (dx, z), 1).wait_send()
            copy(2, pay, zz, d, None, (dy, z), 2).wait_send()
            copy(3, pay, zz, dx, 0, (dy, z), 3).wait_send()
            copy(4, pay, zz, dy, 1, (dx, z), 4).wait_send()
            copy(5, pay, zz, d, None, (dc, z), 5).wait_send()
            copy(6, pay, zz, dx, None, (dc, z), 6).wait_send()
            copy(7, pay, zz, dy, None, (dc, z), 7).wait_send()
            copy(8, pay, zz, dxy, 0, (dc, z), 8).wait_send()
            copy(9, pay, zz, dxy, 1, (dc, z), 9).wait_send()
        guard(step, run)

    items = [(pay, step) for pay in range(4) for step in STEPS]
    small = [(pay, step) for pay in (4, 5) for step in STEPS]
    n = len(items)
    for i in range(n + 6):
        if i < n:
            stage1(*items[i])
        if i < len(small):
            stage1(*small[i])
        if 0 <= i - 3 < n:
            stage2(*items[i - 3])
        if 0 <= i - 6 < n:
            stage3(*items[i - 6])
    for it in items:
        stage4(*it)
    for it in items + small:
        drain(*it)


def gather(pre, vec, wq, wk, wv, wo, wi, wu):
    any_ = pl.BlockSpec(memory_space=pl.ANY)
    return pl.pallas_call(
        gather_kernel,
        in_specs=[any_] * 8,
        out_specs=[any_] * 6,
        out_shape=[
            jax.ShapeDtypeStruct((4,) + pre.shape, pre.dtype),
            jax.ShapeDtypeStruct((4,) + vec.shape, vec.dtype),
            jax.ShapeDtypeStruct((4, D, 768), bf16),
            jax.ShapeDtypeStruct((D, D), bf16),
            jax.ShapeDtypeStruct((4, D, D), bf16),
            jax.ShapeDtypeStruct((4 * D, D), bf16),
        ],
        scratch_shapes=[
            pltpu.SemaphoreType.DMA((8,)),
            pltpu.SemaphoreType.DMA((24, KINDS + 1)),
            pltpu.SemaphoreType.DMA((24, KINDS)),
        ],
        compiler_params=pltpu.CompilerParams(collective_id=0, has_side_effects=True),
        name="gather",
    )(pre, vec, wq, wk, wv, wo, wi, wu)


def gather_plain(pre, vec, wq, wk, wv, wo, wi, wu):
    over = lambda v, axis, at: lax.all_gather(v, axis, axis=at, tiled=True)
    qkv = jnp.concatenate([over(w, "dp", 0) for w in (wq, wk, wv)], axis=1)
    up = over(wi, "dp", 0)
    return (
        lax.all_gather(pre, "prefix"),
        lax.all_gather(vec, "prefix"),
        lax.all_gather(qkv, "prefix"),
        over(over(wo, "dp", 1), "prefix", 0),
        lax.all_gather(up, "prefix"),
        over(over(wu, "dp", 1), "prefix", 0),
    )


def body(
    hidden_in, cotangent, segment_ids, key_mask, prefix_keys, prefix_values,
    w_query, b_query, w_key, b_key, w_value, b_value, w_attn_out, b_attn_out, gain_attn, shift_attn,
    w_ffn_in, b_ffn_in, w_ffn_out, b_ffn_out, gain_ffn, shift_ffn,
):
    z = lax.axis_index("prefix")
    side = z % 2
    rows = jnp.stack([2 * side, jnp.ones_like(side)]).astype(jnp.int32)
    pre = jnp.concatenate([prefix_keys, prefix_values], axis=0)
    vec = jnp.concatenate([b_query, b_key, b_value, b_ffn_in, jnp.zeros((256,), f32)]).reshape(8, 256)
    whole = gather if lax.axis_size("dp") == 8 and lax.axis_size("prefix") == 4 else gather_plain
    pre, vec, w_qkv, w_out, w_up, w_down = whole(
        pre, vec, w_query, w_key, w_value, w_attn_out, w_ffn_in, w_ffn_out
    )
    by_group = lambda p: jnp.pad(p.reshape(PRE, 4, 256).transpose(1, 0, 2), ((0, 0), (0, 128 - PRE), (0, 0)))
    pk, pv = by_group(pre[:, :24]), by_group(pre[:, 24:])
    b_qkv = vec[:, :3].reshape(4, 1, 768)
    b_up = vec[:, 3:7].reshape(1, 4 * D)
    line = lambda v: v.reshape(1, -1)

    seg = jnp.stack([jnp.where(side == 0, segment_ids[0], segment_ids[2]), segment_ids[1]])
    mask = jnp.stack([jnp.where(side == 0, key_mask[0], key_mask[2]), key_mask[1]])
    win = windows(seg)
    segk = jnp.broadcast_to(jnp.where(mask == 1, seg, -1)[:, :, None], (2, L, 128))
    segq = seg[:, None, :]

    qkv, ctx, lse = attn_fwd(rows, win, hidden_in, w_qkv, b_qkv, pk, pv, segk, segq)
    out, gfirst, gctx = tokens(
        rows, ctx, hidden_in, cotangent, w_out, w_up, w_down, line(b_attn_out), line(gain_attn), line(shift_attn),
        b_up, line(b_ffn_out), line(gain_ffn), line(shift_ffn),
    )
    pairs = [(i, i + 1 - 2 * (i % 2)) for i in range(lax.axis_size("prefix"))]
    swap = lambda v: lax.ppermute(lax.dynamic_slice_in_dim(v, rows[0], 1, 0), "prefix", pairs)
    put = lambda v, r: lax.dynamic_update_slice_in_dim(v, r, 2 - rows[0], 0)
    out_other = swap(out)
    args = (rows, win, qkv, ctx, gctx, lse, pk, pv, segk, segq, gfirst, w_qkv)
    gin, ku, vu = attn_bwd(0, *args)
    gin_other = swap(gin)
    gin, ks, vs = attn_bwd(1, *args, into=gin)
    unique = (z < 2).astype(f32)
    shared = (z == 0).astype(f32)
    both = jnp.stack([ku * unique + ks * shared, vu * unique + vs * shared])
    both = lax.psum(lax.psum_scatter(both, "prefix", scatter_dimension=1, tiled=True), "dp")
    return put(out, out_other), put(gin, gin_other), both[0], both[1]


def solution(mesh):
    return jax.shard_map(
        body,
        mesh=mesh,
        in_specs=(
            P("dp", None, None), P("dp", None, None), P("dp", None), P("dp", None),
            P("prefix", None), P("prefix", None),
            P("dp", "prefix"), P("prefix"), P("dp", "prefix"), P("prefix"), P("dp", "prefix"), P("prefix"),
            P("prefix", "dp"), P(), P(), P(),
            P("dp", "prefix"), P("prefix"), P("prefix", "dp"), P(), P(), P(),
        ),
        out_specs=(P("dp", None, None), P("dp", None, None), P("prefix", None), P("prefix", None)),
        check_vma=False,
    )
```

```python
import functools
import jax
import jax.numpy as jnp
from jax import lax
from jax.experimental import pallas as pl
from jax.experimental.pallas import tpu as pltpu
from jax.sharding import PartitionSpec as P

L = 1024
D = 1024
PRE = 96
BLK = 128
NEG = -1e30
CLASSES = (2, 3, 4, 5, 6, 8)
bf16 = jnp.bfloat16
f32 = jnp.float32


def nt(a, b):
    return lax.dot_general(a, b, (((1,), (1,)), ((), ())), preferred_element_type=f32)


def nn(a, b):
    return jnp.dot(a, b, preferred_element_type=f32)


def stack_heads(tile):
    lane = lax.broadcasted_iota(jnp.int32, tile.shape, 1)
    zero = jnp.zeros_like(tile)
    return jnp.concatenate([jnp.where(lane < 64, tile, zero), jnp.where(lane >= 64, tile, zero)], axis=0)


def windows(seg):
    tiles = seg.shape[-1] // BLK
    first = seg[..., ::BLK]
    last = seg[..., BLK - 1 :: BLK]
    start = jnp.sum((seg[..., None, :] < first[..., :, None]).astype(jnp.int32), axis=-1) // BLK
    stop = (jnp.sum((seg[..., None, :] <= last[..., :, None]).astype(jnp.int32), axis=-1) + BLK - 1) // BLK
    need = stop - start
    size = jnp.full_like(need, CLASSES[-1])
    for n in reversed(CLASSES[:-1]):
        size = jnp.where(need <= n, n, size)
    start = jnp.minimum(start, tiles - size)
    return jnp.stack([start, size], axis=-1)


NP = 8


def attn_fwd_kernel(rows, win, x, w, b, pk, pv, segk, segq, qkv, ctx, lse, vt):
    row = pl.program_id(0)
    for g in range(4):
        y = nn(x[0], w[g]) + b[g]
        q = (y[:, :256].astype(bf16) * 0.125).astype(bf16)
        qkv[0, g, :, :256] = q
        kv = y[:, 256:].astype(bf16)
        qkv[0, g, :, 256:] = kv
        vt[256 * g : 256 * g + 256, :L] = kv[:, 256:].T
        vt[256 * g : 256 * g + 256, L:] = pv[g].T

    def tile(t, carry):
        start = win[row, t, 0]
        size = win[row, t, 1]
        q0 = pl.multiple_of(t * BLK, BLK)
        k0 = pl.multiple_of(start * BLK, BLK)

        def run(n):
            W = n * BLK
            mask = segk[0, pl.ds(k0, W), :] == segq[0, :, pl.ds(q0, BLK)]

            def batch(i, carry):
                jobs = []
                for j in range(NP):
                    p = i * NP + j
                    g, half = p // 2, j % 2
                    lanes = slice(128 * half, 128 * half + 128)
                    klanes = slice(256 + 128 * half, 384 + 128 * half)
                    q2 = stack_heads(qkv[0, g, pl.ds(q0, BLK), lanes])
                    jobs.append((p, g, half, nt(qkv[0, g, pl.ds(k0, W), klanes], q2), nt(pk[g, :PRE, lanes], q2)))
                stage = []
                for p, g, half, s, sp in jobs:
                    s = jnp.concatenate([jnp.where(mask, s[:, :128], NEG), jnp.where(mask, s[:, 128:], NEG)], axis=1)
                    top = jnp.maximum(jnp.max(s, axis=0, keepdims=True), jnp.max(sp, axis=0, keepdims=True))
                    stage.append((s, sp, top))
                probs = []
                for s, sp, top in stage:
                    e = jnp.exp(s - top)
                    ep = jnp.exp(sp - top)
                    total = jnp.sum(e, axis=0, keepdims=True) + jnp.sum(ep, axis=0, keepdims=True)
                    probs.append((e.astype(bf16), ep.astype(bf16), total, top))
                outs = []
                for (p, g, half, _, _), (e, ep, total, top) in zip(jobs, probs):
                    r0 = pl.multiple_of(p * 128, 128)
                    outs.append(nn(vt[pl.ds(r0, 128), pl.ds(k0, W)], e) + nn(vt[pl.ds(r0, 128), L : L + PRE], ep))
                for (p, g, half, _, _), (e, ep, total, top), o in zip(jobs, probs, outs):
                    o = o * (1.0 / total)
                    o = jnp.concatenate([o[:64, :128], o[64:, 128:]], axis=0)
                    r0 = pl.multiple_of(p * 128, 128)
                    ctx[0, pl.ds(q0, BLK), pl.ds(r0, 128)] = o.T.astype(bf16)
                    lt = top + jnp.log(total)
                    lse[0, g, 2 * half : 2 * half + 1, pl.ds(q0, BLK)] = lt[:, :128]
                    lse[0, g, 2 * half + 1 : 2 * half + 2, pl.ds(q0, BLK)] = lt[:, 128:]
                return carry

            lax.fori_loop(0, 8 // NP, batch, 0)

        for n in CLASSES:
            pl.when(size == n)(functools.partial(run, n))
        return carry

    lax.fori_loop(0, L // BLK, tile, 0)


def attn_fwd(rows, win, x, w, b, pk, pv, segk, segq):
    R = rows.shape[0]
    row = lambda r, *_: (r, 0, 0)
    all_ = lambda r, *_: (0, 0, 0)
    return pl.pallas_call(
        attn_fwd_kernel,
        grid_spec=pltpu.PrefetchScalarGridSpec(
            num_scalar_prefetch=2,
            grid=(R,),
            in_specs=[
                pl.BlockSpec((1, L, D), lambda r, rows, win: (rows[r], 0, 0)),
                pl.BlockSpec((4, D, 768), all_),
                pl.BlockSpec((4, 1, 768), all_),
                pl.BlockSpec((4, 128, 256), all_),
                pl.BlockSpec((4, 128, 256), all_),
                pl.BlockSpec((1, L, 128), row),
                pl.BlockSpec((1, 1, L), row),
            ],
            out_specs=[
                pl.BlockSpec((1, 4, L, 768), lambda r, *_: (r, 0, 0, 0)),
                pl.BlockSpec((1, L, D), row),
                pl.BlockSpec((1, 4, 4, L), lambda r, *_: (r, 0, 0, 0)),
            ],
            scratch_shapes=[pltpu.VMEM((D, L + 128), bf16)],
        ),
        out_shape=[
            jax.ShapeDtypeStruct((R, 4, L, 768), bf16),
            jax.ShapeDtypeStruct((R, L, D), bf16),
            jax.ShapeDtypeStruct((R, 4, 4, L), f32),
        ],
        compiler_params=pltpu.CompilerParams(vmem_limit_bytes=60 << 20),
        name="attn_fwd",
    )(rows, win, x, w, b, pk, pv, segk, segq)


NB = 4


def attn_bwd_kernel(row, rows, win, qkv, gctx, lse, delta, pk, pv, segk, segq, gfirst_h, w_h, *rest):
    gin, own, pgrad, dqt, dall, gfirst, w, sem = rest[-8:]
    late = [
        pltpu.make_async_copy(gfirst_h.at[row], gfirst, sem.at[0]),
        pltpu.make_async_copy(w_h, w, sem.at[1]),
    ]
    for c in late:
        c.start()

    def blocks(jobs, mask, q0, W, first):
        n = jobs[0][3].shape[0]
        stage = []
        for p, g, half, kt, vt in jobs:
            lanes = slice(128 * half, 128 * half + 128)
            k2 = stack_heads(kt)
            qw = qkv[0, g, pl.ds(q0, W), lanes]
            dow = gctx[0, pl.ds(q0, W), pl.ds(pl.multiple_of(p * 128, 128), 128)]
            stage.append((k2, qw, dow, nt(k2, qw), nt(stack_heads(vt), dow)))
        probs = []
        for (p, g, half, _, _), (k2, qw, dow, s, dp) in zip(jobs, stage):
            ps, ds = [], []
            for h in range(2):
                r = 2 * half + h
                sh = s[h * n : h * n + n] - lse[0, g, r : r + 1, pl.ds(q0, W)]
                if mask is not None:
                    sh = jnp.where(mask, sh, NEG)
                ph = jnp.exp(sh)
                ps.append(ph.astype(bf16))
                ds.append((ph * (dp[h * n : h * n + n] - delta[0, g, r : r + 1, pl.ds(q0, W)])).astype(bf16))
            probs.append((jnp.concatenate(ps, axis=0), jnp.concatenate(ds, axis=0)))
        lane = lax.broadcasted_iota(jnp.int32, (n, 128), 1)
        res = []
        for (p, g, half, _, _), (k2, qw, dow, _, _), (pb, db) in zip(jobs, stage, probs):
            dv = nn(pb, dow)
            dk = nn(db, qw)
            res.append((jnp.where(lane < 64, dk[:n], dk[n:]), jnp.where(lane < 64, dv[:n], dv[n:])))
        for (p, g, half, _, _), (k2, _, _, _, _), (pb, db) in zip(jobs, stage, probs):
            part = nn(k2.T, db)
            r0 = pl.multiple_of(p * 128, 128)
            if first:
                dqt[pl.ds(r0, 128), pl.ds(q0, W)] = part
            else:
                dqt[pl.ds(r0, 128), pl.ds(q0, W)] += part
        return res

    def prefix(i, carry):
        jobs = []
        for j in range(NB):
            p = i * NB + j
            g, half = p // 2, j % 2
            lanes = slice(128 * half, 128 * half + 128)
            jobs.append((p, g, half, pk[g, :PRE, lanes], pv[g, :PRE, lanes]))
        total = None
        for c in range(2):
            part = blocks(jobs, None, c * 512, 512, True)
            total = part if total is None else [(a + c_, b + d) for (a, b), (c_, d) in zip(total, part)]
        for (p, g, half, _, _), (dk, dv) in zip(jobs, total):
            cols = pl.ds(pl.multiple_of(p * 128, 128), 128)
            pgrad[0, :, cols] = dk
            pgrad[1, :, cols] = dv
        return carry

    lax.fori_loop(0, 8 // NB, prefix, 0)

    def tile(t, carry):
        start = win[row, t, 0]
        size = win[row, t, 1]
        k0 = pl.multiple_of(t * BLK, BLK)
        q0 = pl.multiple_of(start * BLK, BLK)

        def run(n):
            W = n * BLK
            sk = segk[0, pl.ds(k0, BLK), :]
            sq = segq[0, :, pl.ds(q0, W)]
            mask = jnp.concatenate([sk] * n, axis=1) == sq

            def batch(i, carry):
                jobs = []
                for j in range(NB):
                    p = i * NB + j
                    g, half = p // 2, j % 2
                    kt = qkv[0, g, pl.ds(k0, BLK), 256 + 128 * half : 384 + 128 * half]
                    vt = qkv[0, g, pl.ds(k0, BLK), 512 + 128 * half : 640 + 128 * half]
                    jobs.append((p, g, half, kt, vt))
                for (p, g, half, _, _), (dk, dv) in zip(jobs, blocks(jobs, mask, q0, W, False)):
                    dall[g, pl.ds(k0, BLK), 256 + 128 * half : 384 + 128 * half] = dk.astype(bf16)
                    dall[g, pl.ds(k0, BLK), 512 + 128 * half : 640 + 128 * half] = dv.astype(bf16)
                return carry

            lax.fori_loop(0, 8 // NB, batch, 0)

        for n in CLASSES:
            pl.when(size == n)(functools.partial(run, n))
        return carry

    lax.fori_loop(0, L // BLK, tile, 0)
    for c in late:
        c.wait()
    for g in range(4):
        dall[g, :, :256] = (dqt[256 * g : 256 * g + 256, :].T * 0.125).astype(bf16)
    for c in range(2):
        cols = slice(512 * c, 512 * c + 512)
        acc = gfirst[:, cols].astype(f32)
        for i in range(4):
            acc = acc + nt(dall[i], w[i, cols, :])
        low = acc.astype(bf16)
        gin[0, :, cols] = low
        own[:, cols] = low


def attn_bwd(r, rows, win, qkv, gctx, lse, delta, pk, pv, segk, segq, gfirst, w, into=None):
    row = lambda i, *_: (r, 0, 0)
    row4 = lambda i, *_: (r, 0, 0, 0)
    all_ = lambda i, *_: (0, 0, 0)
    extra = [] if into is None else [into]
    return pl.pallas_call(
        functools.partial(attn_bwd_kernel, r),
        grid_spec=pltpu.PrefetchScalarGridSpec(
            num_scalar_prefetch=2,
            grid=(1,),
            in_specs=[
                pl.BlockSpec((1, 4, L, 768), row4),
                pl.BlockSpec((1, L, D), row),
                pl.BlockSpec((1, 4, 4, L), row4),
                pl.BlockSpec((1, 4, 4, L), row4),
                pl.BlockSpec((4, 128, 256), all_),
                pl.BlockSpec((4, 128, 256), all_),
                pl.BlockSpec((1, L, 128), row),
                pl.BlockSpec((1, 1, L), row),
                pl.BlockSpec(memory_space=pl.ANY),
                pl.BlockSpec(memory_space=pl.ANY),
            ]
            + [pl.BlockSpec(memory_space=pl.ANY) for _ in extra],
            out_specs=[
                pl.BlockSpec((1, L, D), lambda i, rows, win: (rows[r], 0, 0)),
                pl.BlockSpec((L, D), lambda i, *_: (0, 0)),
                pl.BlockSpec((2, PRE, D), all_),
            ],
            scratch_shapes=[
                pltpu.VMEM((D, L), f32),
                pltpu.VMEM((4, L, 768), bf16),
                pltpu.VMEM((L, D), bf16),
                pltpu.VMEM((4, D, 768), bf16),
                pltpu.SemaphoreType.DMA((2,)),
            ],
        ),
        out_shape=[
            jax.ShapeDtypeStruct((3, L, D), bf16),
            jax.ShapeDtypeStruct((L, D), bf16),
            jax.ShapeDtypeStruct((2, PRE, D), f32),
        ],
        input_output_aliases={12: 0} if extra else {},
        compiler_params=pltpu.CompilerParams(vmem_limit_bytes=60 << 20),
        name="attn_bwd",
    )(rows, win, qkv, gctx, lse, delta, pk, pv, segk, segq, gfirst, w, *extra)


HC = 512
TM = 512
EPS = 1e-5


ERF = (0.7978849414895208, 0.03633308441063725, -3.2594747109729314e-05, -5.5306315505082965e-05,
       3.964772884359942e-06, -1.3226625462816106e-07, 1.7562766828961903e-09)


def gelu_parts(v):
    u = v * v
    w = jnp.minimum(u, 31.36)
    p = ERF[6] * w + ERF[5]
    for c in ERF[4::-1]:
        p = p * w + c
    phi = 0.5 * jnp.tanh(v * p) + 0.5
    return v * phi, phi


def norm_stats(z):
    mean = jnp.mean(z, axis=1, keepdims=True)
    c = z - mean
    var = jnp.mean(c * c, axis=1, keepdims=True)
    r = lax.rsqrt(var + EPS)
    return c * r, r


RC = 512


def tokens_kernel(rows, ctx, x, cot, wo, win, wout, bo, g1, s1, bi, b2, g2, s2, out, own, gf, gc, delta, xhat, zbuf, low, act, gp, rs, vb):
    M = TM

    def dot_cols(i, carry):
        c0 = pl.multiple_of(i * 256, 256)
        zbuf[:, pl.ds(c0, 256)] = nn(ctx[...], wo[:, pl.ds(c0, 256)]) + x[:, pl.ds(c0, 256)].astype(f32)
        return carry

    lax.fori_loop(0, 4, dot_cols, 0, unroll=4)

    def ln1(i, carry):
        r0 = pl.multiple_of(i * RC, RC)
        n, r = norm_stats(zbuf[pl.ds(r0, RC), :] + bo[...])
        xhat[pl.ds(r0, RC), :] = n
        rs[pl.ds(r0, RC), :] = jnp.broadcast_to(r, (RC, 128))
        y = n * g1[...] + s1[...]
        zbuf[pl.ds(r0, RC), :] = y
        low[pl.ds(r0, RC), :] = y.astype(bf16)
        return carry

    lax.fori_loop(0, M // RC, ln1, 0)

    def up(i, carry):
        z, c = i // 2, i % 2
        c0 = pl.multiple_of(c * HC, HC)
        h0 = pl.multiple_of(i * HC, HC)
        h = nn(low[...], win[z, :, pl.ds(c0, HC)]) + bi[:, pl.ds(h0, HC)]
        a, d = gelu_parts(h)
        act[:, pl.ds(h0, HC)] = a.astype(bf16)
        gp[:, pl.ds(h0, HC)] = d.astype(bf16)
        vb[:, pl.ds(h0, HC)] = h.astype(bf16)
        return carry

    lax.fori_loop(0, 8, up, 0, unroll=8)

    def down(i, carry):
        c0 = pl.multiple_of(i * 256, 256)
        zbuf[:, pl.ds(c0, 256)] += nn(act[...], wout[:, pl.ds(c0, 256)])
        return carry

    lax.fori_loop(0, 4, down, 0, unroll=4)

    def ln2(i, carry):
        r0 = pl.multiple_of(i * RC, RC)
        n, r = norm_stats(zbuf[pl.ds(r0, RC), :] + b2[...])
        result = (n * g2[...] + s2[...]).astype(bf16)
        out[pl.ds(r0, RC), :] = result
        own[pl.ds(r0, RC), :] = result
        g = cot[pl.ds(r0, RC), :].astype(f32) * g2[...]
        m1 = jnp.mean(g, axis=1, keepdims=True)
        m2 = jnp.mean(g * n, axis=1, keepdims=True)
        d = (g - m1 - n * m2) * r
        zbuf[pl.ds(r0, RC), :] = d
        low[pl.ds(r0, RC), :] = d.astype(bf16)
        return carry

    lax.fori_loop(0, M // RC, ln2, 0)

    def back(i, carry):
        h0 = pl.multiple_of(i * HC, HC)
        d = nt(low[...], wout[pl.ds(h0, HC), :])
        v = vb[:, pl.ds(h0, HC)].astype(f32)
        slope = gp[:, pl.ds(h0, HC)].astype(f32) + v * (jnp.exp(-0.5 * v * v) * 0.3989422804014327)
        act[:, pl.ds(h0, HC)] = (d * slope).astype(bf16)
        return carry

    lax.fori_loop(0, 8, back, 0, unroll=8)

    def back2(i, carry):
        c0 = pl.multiple_of(i * 256, 256)
        acc = zbuf[:, pl.ds(c0, 256)]
        for z in range(4):
            acc = acc + nt(act[:, 1024 * z : 1024 * z + 1024], win[z, pl.ds(c0, 256), :])
        zbuf[:, pl.ds(c0, 256)] = acc
        return carry

    lax.fori_loop(0, 4, back2, 0, unroll=4)

    def ln1b(i, carry):
        r0 = pl.multiple_of(i * RC, RC)
        n = xhat[pl.ds(r0, RC), :]
        g = zbuf[pl.ds(r0, RC), :] * g1[...]
        m1 = jnp.mean(g, axis=1, keepdims=True)
        m2 = jnp.mean(g * n, axis=1, keepdims=True)
        d = (g - m1 - n * m2) * rs[pl.ds(r0, RC), 0:1]
        gf[pl.ds(r0, RC), :] = d.astype(bf16)
        return carry

    lax.fori_loop(0, M // RC, ln1b, 0)

    def gcols(i, carry):
        c0 = pl.multiple_of(i * 256, 256)
        part = nt(gf[...], wo[pl.ds(c0, 256), :]).astype(bf16)
        gc[:, pl.ds(c0, 256)] = part
        prod = part.astype(f32) * ctx[:, pl.ds(c0, 256)].astype(f32)
        high = prod.astype(bf16)
        rest = (prod - high.astype(f32)).astype(bf16)
        head = lax.broadcasted_iota(jnp.int32, (16, 256), 0)
        lane = lax.broadcasted_iota(jnp.int32, (16, 256), 1)
        pick = jnp.where(lane // 64 == head, 1.0, 0.0).astype(bf16)
        delta[i] = (nt(pick, high) + nt(pick, rest))[:4]
        return carry

    lax.fori_loop(0, 4, gcols, 0, unroll=4)


def tokens(rows, ctx, x, cot, wo, win, wout, bo, g1, s1, bi, b2, g2, s2):
    R = ctx.shape[0]
    per = L // TM
    own = pl.BlockSpec((None, TM, D), lambda i, rows: (i // per, i % per, 0))
    pick = pl.BlockSpec((None, TM, D), lambda i, rows: (rows[i // per], i % per, 0))
    whole = lambda a: pl.BlockSpec(a.shape, lambda i, rows: (0,) * a.ndim, pipeline_mode=pl.Buffered(1))
    consts = (wo, win, wout, bo, g1, s1, bi, b2, g2, s2)
    return pl.pallas_call(
        tokens_kernel,
        grid_spec=pltpu.PrefetchScalarGridSpec(
            num_scalar_prefetch=1,
            grid=(R * per,),
            in_specs=[own, pick, pick] + [whole(a) for a in consts],
            out_specs=[pick, own, own, own, pl.BlockSpec((None, 4, 4, TM), lambda i, rows: (i // per, 0, 0, i % per))],
            scratch_shapes=[
                pltpu.VMEM((TM, D), f32),
                pltpu.VMEM((TM, D), f32),
                pltpu.VMEM((TM, D), bf16),
                pltpu.VMEM((TM, 4 * D), bf16),
                pltpu.VMEM((TM, 4 * D), bf16),
                pltpu.VMEM((TM, 128), f32),
                pltpu.VMEM((TM, 4 * D), bf16),
            ],
        ),
        out_shape=[
            jax.ShapeDtypeStruct((3, L, D), bf16),
            jax.ShapeDtypeStruct((R, L, D), bf16),
            jax.ShapeDtypeStruct((R, L, D), bf16),
            jax.ShapeDtypeStruct((R, L, D), bf16),
            jax.ShapeDtypeStruct((R, 4, 4, L), f32),
        ],
        compiler_params=pltpu.CompilerParams(vmem_limit_bytes=60 << 20),
        name="tokens",
    )(rows, ctx, x, cot, *consts)


KINDS = 10
STEPS = ((0, 0), (1, -1), (1, 1), (2, -1), (2, 1), (3, -1), (3, 1))


def gather_kernel(pre_s, vec_s, wq, wk, wv, wo_s, wi_s, wu_s, pre, vec, qkv, wo, wi, wu, lsem, ssem, rsem):
    d = lax.axis_index("dp")
    z = lax.axis_index("prefix")
    core, xx, yy = d % 2, (d // 2) % 2, d // 4
    dc = d + 1 - 2 * core
    dx = d + 2 - 4 * xx
    dy = d + 4 - 8 * yy
    dxy = dx + dy - d

    def region(pay, zz, dd, half=None):
        if pay >= 4:
            return (pre, vec)[pay - 4].at[zz]
        if pay == 0:
            n, ref = 128, lambda o, s: qkv.at[zz, pl.ds(128 * dd + o, s), :]
        elif pay == 1:
            n, ref = 256, lambda o, s: wo.at[pl.ds(256 * zz + o, s), pl.ds(128 * dd, 128)]
        elif pay == 2:
            n, ref = 128, lambda o, s: wi.at[zz, pl.ds(128 * dd + o, s), :]
        else:
            n, ref = 1024, lambda o, s: wu.at[pl.ds(1024 * zz + o, s), pl.ds(128 * dd, 128)]
        return ref(0, n) if half is None else ref(half * (n // 2), n // 2)

    local = [
        pltpu.make_async_copy(src, dst, lsem.at[i])
        for i, (src, dst) in enumerate(
            [
                (wq, qkv.at[z, pl.ds(128 * d, 128), 0:256]),
                (wk, qkv.at[z, pl.ds(128 * d, 128), 256:512]),
                (wv, qkv.at[z, pl.ds(128 * d, 128), 512:768]),
                (wo_s, region(1, z, d)),
                (wi_s, region(2, z, d)),
                (wu_s, region(3, z, d)),
                (pre_s, pre.at[z]),
                (vec_s, vec.at[z]),
            ]
        )
    ]
    for c in local:
        c.start()
    bar = pltpu.get_barrier_semaphore()

    def hello(dev):
        pl.semaphore_signal(bar, inc=1, device_id=dev, device_id_type=pl.DeviceIdType.MESH)

    for dd in (dc, dx, dy):
        hello((dd, z))

    @pl.when(z > 0)
    def _():
        hello((d, z - 1))

    @pl.when(z < 3)
    def _():
        hello((d, z + 1))

    peers = jnp.where(z > 0, 1, 0) + jnp.where(z < 3, 1, 0)
    pl.semaphore_wait(bar, 3 + peers)
    for c in local:
        c.wait()

    def copy(kind, pay, zz, dd, half, dev, skind):
        r = region(pay, zz, dd, half)
        return pltpu.make_async_remote_copy(
            src_ref=r, dst_ref=r, send_sem=ssem.at[pay * 4 + zz, skind], recv_sem=rsem.at[pay * 4 + zz, kind],
            device_id=dev, device_id_type=pl.DeviceIdType.MESH,
        )

    def guard(step, fn):
        delta, side = step
        zz = z + delta * side
        if delta == 0:
            fn(zz)
        elif side < 0:
            pl.when(z >= delta)(lambda: fn(zz))
        else:
            pl.when(z + delta <= 3)(lambda: fn(zz))

    def stage1(pay, step):
        def run(zz):
            delta, side = step
            if delta:
                copy(0, pay, zz, d, None, (d, z), 0).wait_recv()
            if side <= 0:
                pl.when(z < 3)(lambda: copy(0, pay, zz, d, None, (d, z + 1), 10).start())
            if side >= 0:
                pl.when(z > 0)(lambda: copy(0, pay, zz, d, None, (d, z - 1), 0).start())
            if pay >= 4:
                return
            copy(1, pay, zz, d, None, (dx, z), 1).start()
            copy(2, pay, zz, d, None, (dy, z), 2).start()
            copy(5, pay, zz, d, None, (dc, z), 5).start()
        guard(step, run)

    def stage2(pay, step):
        def run(zz):
            copy(1, pay, zz, dx, None, (dx, z), 1).wait_recv()
            copy(3, pay, zz, dx, 0, (dy, z), 3).start()
            copy(6, pay, zz, dx, None, (dc, z), 6).start()
            copy(2, pay, zz, dy, None, (dy, z), 2).wait_recv()
            copy(4, pay, zz, dy, 1, (dx, z), 4).start()
            copy(7, pay, zz, dy, None, (dc, z), 7).start()
        guard(step, run)

    def stage3(pay, step):
        def run(zz):
            copy(3, pay, zz, dxy, 0, (dy, z), 3).wait_recv()
            copy(8, pay, zz, dxy, 0, (dc, z), 8).start()
            copy(4, pay, zz, dxy, 1, (dx, z), 4).wait_recv()
            copy(9, pay, zz, dxy, 1, (dc, z), 9).start()
        guard(step, run)

    def stage4(pay, step):
        o = dc - d
        def run(zz):
            copy(5, pay, zz, d + o, None, (dc, z), 5).wait_recv()
            copy(6, pay, zz, dx + o, None, (dc, z), 6).wait_recv()
            copy(7, pay, zz, dy + o, None, (dc, z), 7).wait_recv()
            copy(8, pay, zz, dxy + o, 0, (dc, z), 8).wait_recv()
            copy(9, pay, zz, dxy + o, 1, (dc, z), 9).wait_recv()
        guard(step, run)

    def drain(pay, step):
        def run(zz):
            delta, side = step
            if side <= 0:
                pl.when(z < 3)(lambda: copy(0, pay, zz, d, None, (d, z + 1), 10).wait_send())
            if side >= 0:
                pl.when(z > 0)(lambda: copy(0, pay, zz, d, None, (d, z - 1), 0).wait_send())
            if pay >= 4:
                return
            copy(1, pay, zz, d, None, (dx, z), 1).wait_send()
            copy(2, pay, zz, d, None, (dy, z), 2).wait_send()
            copy(3, pay, zz, dx, 0, (dy, z), 3).wait_send()
            copy(4, pay, zz, dy, 1, (dx, z), 4).wait_send()
            copy(5, pay, zz, d, None, (dc, z), 5).wait_send()
            copy(6, pay, zz, dx, None, (dc, z), 6).wait_send()
            copy(7, pay, zz, dy, None, (dc, z), 7).wait_send()
            copy(8, pay, zz, dxy, 0, (dc, z), 8).wait_send()
            copy(9, pay, zz, dxy, 1, (dc, z), 9).wait_send()
        guard(step, run)

    items = [(pay, step) for pay in range(4) for step in STEPS]
    small = [(pay, step) for pay in (4, 5) for step in STEPS]
    n = len(items)
    for i in range(n + 6):
        if i < n:
            stage1(*items[i])
        if i < len(small):
            stage1(*small[i])
        if 0 <= i - 3 < n:
            stage2(*items[i - 3])
        if 0 <= i - 6 < n:
            stage3(*items[i - 6])
    for it in items:
        stage4(*it)
    for it in items + small:
        drain(*it)


def gather(pre, vec, wq, wk, wv, wo, wi, wu):
    any_ = pl.BlockSpec(memory_space=pl.ANY)
    return pl.pallas_call(
        gather_kernel,
        in_specs=[any_] * 8,
        out_specs=[any_] * 6,
        out_shape=[
            jax.ShapeDtypeStruct((4,) + pre.shape, pre.dtype),
            jax.ShapeDtypeStruct((4,) + vec.shape, vec.dtype),
            jax.ShapeDtypeStruct((4, D, 768), bf16),
            jax.ShapeDtypeStruct((D, D), bf16),
            jax.ShapeDtypeStruct((4, D, D), bf16),
            jax.ShapeDtypeStruct((4 * D, D), bf16),
        ],
        scratch_shapes=[
            pltpu.SemaphoreType.DMA((8,)),
            pltpu.SemaphoreType.DMA((24, KINDS + 1)),
            pltpu.SemaphoreType.DMA((24, KINDS)),
        ],
        compiler_params=pltpu.CompilerParams(collective_id=0, has_side_effects=True),
        name="gather",
    )(pre, vec, wq, wk, wv, wo, wi, wu)


def gather_plain(pre, vec, wq, wk, wv, wo, wi, wu):
    over = lambda v, axis, at: lax.all_gather(v, axis, axis=at, tiled=True)
    qkv = jnp.concatenate([over(w, "dp", 0) for w in (wq, wk, wv)], axis=1)
    up = over(wi, "dp", 0)
    return (
        lax.all_gather(pre, "prefix"),
        lax.all_gather(vec, "prefix"),
        lax.all_gather(qkv, "prefix"),
        over(over(wo, "dp", 1), "prefix", 0),
        lax.all_gather(up, "prefix"),
        over(over(wu, "dp", 1), "prefix", 0),
    )


def total_kernel(uniq, shared, other, key, value, mine, half, slots, ssem, rsem):
    d = lax.axis_index("dp")
    z = lax.axis_index("prefix")
    core, chip = d % 2, d // 2
    xx, yy = chip % 2, chip // 2
    dc = d + 1 - 2 * core
    peers = [((d + 2 - 4 * xx), chip + 1 - 2 * xx), ((d + 4 - 8 * yy), chip + 2 - 4 * yy)]
    peers.append((peers[0][0] + peers[1][0] - d, 3 - chip))
    bar = pltpu.get_barrier_semaphore()
    for dd in (dc, *(p for p, _ in peers)):
        pl.semaphore_signal(bar, inc=1, device_id=(dd, z), device_id_type=pl.DeviceIdType.MESH)
    n = key.shape[0]
    r0 = pl.multiple_of(z * n, 8)
    mine[...] = uniq[:, pl.ds(r0, n), :] + shared[:, pl.ds(r0, n), :] + other[...]
    pl.semaphore_wait(bar, 4)

    def send(src, dst, i, dd):
        return pltpu.make_async_remote_copy(
            src_ref=src, dst_ref=dst, send_sem=ssem.at[i], recv_sem=rsem.at[i],
            device_id=(dd, z), device_id_type=pl.DeviceIdType.MESH,
        )

    first = send(mine.at[1 - core], half, 0, dc)
    first.start()
    first.wait()
    slots[chip] = mine[core] + half[...]
    copies = [send(slots.at[chip], slots.at[chip], 1 + i, dd) for i, (dd, _) in enumerate(peers)]
    for c in copies:
        c.start()
    for c in copies:
        c.wait()
    total = (slots[0] + slots[1]) + (slots[2] + slots[3])

    @pl.when(core == 0)
    def _():
        key[...] = total
        last = send(key, key, 4, dc)
        last.start()
        last.wait_send()
        send(value, value, 5, dc).wait_recv()

    @pl.when(core == 1)
    def _():
        value[...] = total
        last = send(value, value, 5, dc)
        last.start()
        last.wait_send()
        send(key, key, 4, dc).wait_recv()


def total_grads(uniq, shared, other):
    n = other.shape[1]
    vmem = pl.BlockSpec(memory_space=pltpu.VMEM)
    return pl.pallas_call(
        total_kernel,
        in_specs=[vmem] * 3,
        out_specs=[vmem] * 2,
        out_shape=[jax.ShapeDtypeStruct((n, D), f32)] * 2,
        scratch_shapes=[
            pltpu.VMEM((2, n, D), f32),
            pltpu.VMEM((n, D), f32),
            pltpu.VMEM((4, n, D), f32),
            pltpu.SemaphoreType.DMA((6,)),
            pltpu.SemaphoreType.DMA((6,)),
        ],
        compiler_params=pltpu.CompilerParams(collective_id=1, has_side_effects=True),
        name="total_grads",
    )(uniq, shared, other)


def body(
    hidden_in, cotangent, segment_ids, key_mask, prefix_keys, prefix_values,
    w_query, b_query, w_key, b_key, w_value, b_value, w_attn_out, b_attn_out, gain_attn, shift_attn,
    w_ffn_in, b_ffn_in, w_ffn_out, b_ffn_out, gain_ffn, shift_ffn,
):
    z = lax.axis_index("prefix")
    side = z % 2
    rows = jnp.stack([2 * side, jnp.ones_like(side)]).astype(jnp.int32)
    pre = jnp.concatenate([prefix_keys, prefix_values], axis=0)
    vec = jnp.concatenate([b_query, b_key, b_value, b_ffn_in, jnp.zeros((256,), f32)]).reshape(8, 256)
    small = lax.axis_size("dp") == 8 and lax.axis_size("prefix") == 4
    whole = gather if small else gather_plain
    pre, vec, w_qkv, w_out, w_up, w_down = whole(
        pre, vec, w_query, w_key, w_value, w_attn_out, w_ffn_in, w_ffn_out
    )
    by_group = lambda p: jnp.pad(p.reshape(PRE, 4, 256).transpose(1, 0, 2), ((0, 0), (0, 128 - PRE), (0, 0)))
    pk, pv = by_group(pre[:, :24]), by_group(pre[:, 24:])
    b_qkv = vec[:, :3].reshape(4, 1, 768)
    b_up = vec[:, 3:7].reshape(1, 4 * D)
    line = lambda v: v.reshape(1, -1)

    seg = jnp.stack([jnp.where(side == 0, segment_ids[0], segment_ids[2]), segment_ids[1]])
    mask = jnp.stack([jnp.where(side == 0, key_mask[0], key_mask[2]), key_mask[1]])
    win = windows(seg)
    segk = jnp.broadcast_to(jnp.where(mask == 1, seg, -1)[:, :, None], (2, L, 128))
    segq = seg[:, None, :]

    qkv, ctx, lse = attn_fwd(rows, win, hidden_in, w_qkv, b_qkv, pk, pv, segk, segq)
    out, out_own, gfirst, gctx, delta = tokens(
        rows, ctx, hidden_in, cotangent, w_out, w_up, w_down, line(b_attn_out), line(gain_attn), line(shift_attn),
        b_up, line(b_ffn_out), line(gain_ffn), line(shift_ffn),
    )
    pairs = [(i, i + 1 - 2 * (i % 2)) for i in range(lax.axis_size("prefix"))]
    swap = lambda v: lax.ppermute(v, "prefix", pairs)
    put = lambda v, r: lax.dynamic_update_slice_in_dim(v, r[None], 2 - rows[0], 0)
    out_other = swap(out_own[0])
    args = (rows, win, qkv, gctx, lse, delta, pk, pv, segk, segq, gfirst, w_qkv)
    gin, gin_own, uniq = attn_bwd(0, *args)
    gin_other = swap(gin_own)
    n = PRE // lax.axis_size("prefix")
    other = swap(lax.dynamic_slice_in_dim(uniq, (z + 1 - 2 * side) * n, n, 1))
    gin, _, shared = attn_bwd(1, *args, into=gin)
    if small:
        keys, values = total_grads(uniq, shared, other)
    else:
        mine = lax.dynamic_slice_in_dim(uniq + shared, z * n, n, 1) + other
        keys, values = lax.psum(mine, "dp")
    return put(out, out_other), put(gin, gin_other), keys, values


def solution(mesh):
    return jax.shard_map(
        body,
        mesh=mesh,
        in_specs=(
            P("dp", None, None), P("dp", None, None), P("dp", None), P("dp", None),
            P("prefix", None), P("prefix", None),
            P("dp", "prefix"), P("prefix"), P("dp", "prefix"), P("prefix"), P("dp", "prefix"), P("prefix"),
            P("prefix", "dp"), P(), P(), P(),
            P("dp", "prefix"), P("prefix"), P("prefix", "dp"), P(), P(), P(),
        ),
        out_specs=(P("dp", None, None), P("dp", None, None), P("prefix", None), P("prefix", None)),
        check_vma=False,
    )
```

```python
import functools
import jax
import jax.numpy as jnp
from jax import lax
from jax.experimental import pallas as pl
from jax.experimental.pallas import tpu as pltpu
from jax.sharding import PartitionSpec as P

L = 1024
D = 1024
PRE = 96
BLK = 128
NEG = -1e30
CLASSES = (2, 3, 4, 5, 6, 8)
bf16 = jnp.bfloat16
f32 = jnp.float32


def nt(a, b):
    return lax.dot_general(a, b, (((1,), (1,)), ((), ())), preferred_element_type=f32)


def nn(a, b):
    return jnp.dot(a, b, preferred_element_type=f32)


def stack_heads(tile):
    lane = lax.broadcasted_iota(jnp.int32, tile.shape, 1)
    zero = jnp.zeros_like(tile)
    return jnp.concatenate([jnp.where(lane < 64, tile, zero), jnp.where(lane >= 64, tile, zero)], axis=0)


def windows(seg):
    tiles = seg.shape[-1] // BLK
    first = seg[..., ::BLK]
    last = seg[..., BLK - 1 :: BLK]
    start = jnp.sum((seg[..., None, :] < first[..., :, None]).astype(jnp.int32), axis=-1) // BLK
    stop = (jnp.sum((seg[..., None, :] <= last[..., :, None]).astype(jnp.int32), axis=-1) + BLK - 1) // BLK
    need = stop - start
    size = jnp.full_like(need, CLASSES[-1])
    for n in reversed(CLASSES[:-1]):
        size = jnp.where(need <= n, n, size)
    start = jnp.minimum(start, tiles - size)
    return jnp.stack([start, size], axis=-1)


NP = 8


def attn_fwd_kernel(rows, win, x, w, b, pk, pv, segk, segq, qkv, ctx, lse, vt):
    row = pl.program_id(0)
    for g in range(4):
        y = nn(x[0], w[g]) + b[g]
        q = (y[:, :256].astype(bf16) * 0.125).astype(bf16)
        qkv[0, g, :, :256] = q
        kv = y[:, 256:].astype(bf16)
        qkv[0, g, :, 256:] = kv
        vt[256 * g : 256 * g + 256, :L] = kv[:, 256:].T
        vt[256 * g : 256 * g + 256, L:] = pv[g].T

    def tile(t, carry):
        start = win[row, t, 0]
        size = win[row, t, 1]
        q0 = pl.multiple_of(t * BLK, BLK)
        k0 = pl.multiple_of(start * BLK, BLK)

        def run(n):
            W = n * BLK
            mask = segk[0, pl.ds(k0, W), :] == segq[0, :, pl.ds(q0, BLK)]

            def batch(i, carry):
                jobs = []
                for j in range(NP):
                    p = i * NP + j
                    g, half = p // 2, j % 2
                    lanes = slice(128 * half, 128 * half + 128)
                    klanes = slice(256 + 128 * half, 384 + 128 * half)
                    q2 = stack_heads(qkv[0, g, pl.ds(q0, BLK), lanes])
                    jobs.append((p, g, half, nt(qkv[0, g, pl.ds(k0, W), klanes], q2), nt(pk[g, :, lanes], q2)))
                stage = []
                for p, g, half, s, sp in jobs:
                    s = jnp.concatenate([jnp.where(mask, s[:, :128], NEG), jnp.where(mask, s[:, 128:], NEG)], axis=1)
                    top = jnp.maximum(jnp.max(s, axis=0, keepdims=True), jnp.max(sp, axis=0, keepdims=True))
                    stage.append((s, sp, top))
                probs = []
                for s, sp, top in stage:
                    e = jnp.exp(s - top)
                    ep = jnp.exp(sp - top)
                    total = jnp.sum(e, axis=0, keepdims=True) + jnp.sum(ep, axis=0, keepdims=True)
                    probs.append((e.astype(bf16), ep.astype(bf16), total, top))
                outs = []
                for (p, g, half, _, _), (e, ep, total, top) in zip(jobs, probs):
                    r0 = pl.multiple_of(p * 128, 128)
                    outs.append(nn(vt[pl.ds(r0, 128), pl.ds(k0, W)], e) + nn(vt[pl.ds(r0, 128), L : L + PRE], ep))
                for (p, g, half, _, _), (e, ep, total, top), o in zip(jobs, probs, outs):
                    o = o * (1.0 / total)
                    o = jnp.concatenate([o[:64, :128], o[64:, 128:]], axis=0)
                    r0 = pl.multiple_of(p * 128, 128)
                    ctx[0, pl.ds(q0, BLK), pl.ds(r0, 128)] = o.T.astype(bf16)
                    lt = top + jnp.log(total)
                    lse[0, g, 2 * half : 2 * half + 1, pl.ds(q0, BLK)] = lt[:, :128]
                    lse[0, g, 2 * half + 1 : 2 * half + 2, pl.ds(q0, BLK)] = lt[:, 128:]
                return carry

            lax.fori_loop(0, 8 // NP, batch, 0)

        for n in CLASSES:
            pl.when(size == n)(functools.partial(run, n))
        return carry

    lax.fori_loop(0, L // BLK, tile, 0)


def attn_fwd(rows, win, x, w, b, pk, pv, segk, segq):
    R = rows.shape[0]
    row = lambda r, *_: (r, 0, 0)
    all_ = lambda r, *_: (0, 0, 0)
    return pl.pallas_call(
        attn_fwd_kernel,
        grid_spec=pltpu.PrefetchScalarGridSpec(
            num_scalar_prefetch=2,
            grid=(R,),
            in_specs=[
                pl.BlockSpec((1, L, D), lambda r, rows, win: (rows[r], 0, 0)),
                pl.BlockSpec((4, D, 768), all_),
                pl.BlockSpec((4, 1, 768), all_),
                pl.BlockSpec((4, PRE, 256), all_),
                pl.BlockSpec((4, PRE, 256), all_),
                pl.BlockSpec((1, L, 128), row),
                pl.BlockSpec((1, 1, L), row),
            ],
            out_specs=[
                pl.BlockSpec((1, 4, L, 768), lambda r, *_: (r, 0, 0, 0)),
                pl.BlockSpec((1, L, D), row),
                pl.BlockSpec((1, 4, 4, L), lambda r, *_: (r, 0, 0, 0)),
            ],
            scratch_shapes=[pltpu.VMEM((D, L + PRE), bf16)],
        ),
        out_shape=[
            jax.ShapeDtypeStruct((R, 4, L, 768), bf16),
            jax.ShapeDtypeStruct((R, L, D), bf16),
            jax.ShapeDtypeStruct((R, 4, 4, L), f32),
        ],
        compiler_params=pltpu.CompilerParams(vmem_limit_bytes=60 << 20),
        name="attn_fwd",
    )(rows, win, x, w, b, pk, pv, segk, segq)


NB = 4


def attn_bwd_kernel(row, rows, win, qkv, gctx, lse, delta, pk, pv, segk, segq, gfirst_h, w_h, *rest):
    gin, own, pgrad, dqt, dall, gfirst, w, sem = rest[-8:]
    late = [
        pltpu.make_async_copy(gfirst_h.at[row], gfirst, sem.at[0]),
        pltpu.make_async_copy(w_h, w, sem.at[1]),
    ]
    for c in late:
        c.start()

    def blocks(jobs, mask, q0, W, first):
        n = jobs[0][3].shape[0]
        stage = []
        for p, g, half, kt, vt in jobs:
            lanes = slice(128 * half, 128 * half + 128)
            k2 = stack_heads(kt)
            qw = qkv[0, g, pl.ds(q0, W), lanes]
            dow = gctx[0, pl.ds(q0, W), pl.ds(pl.multiple_of(p * 128, 128), 128)]
            stage.append((k2, qw, dow, nt(k2, qw), nt(stack_heads(vt), dow)))
        probs = []
        for (p, g, half, _, _), (k2, qw, dow, s, dp) in zip(jobs, stage):
            ps, ds = [], []
            for h in range(2):
                r = 2 * half + h
                sh = s[h * n : h * n + n] - lse[0, g, r : r + 1, pl.ds(q0, W)]
                if mask is not None:
                    sh = jnp.where(mask, sh, NEG)
                ph = jnp.exp(sh)
                ps.append(ph.astype(bf16))
                ds.append((ph * (dp[h * n : h * n + n] - delta[0, g, r : r + 1, pl.ds(q0, W)])).astype(bf16))
            probs.append((jnp.concatenate(ps, axis=0), jnp.concatenate(ds, axis=0)))
        lane = lax.broadcasted_iota(jnp.int32, (n, 128), 1)
        res = []
        for (p, g, half, _, _), (k2, qw, dow, _, _), (pb, db) in zip(jobs, stage, probs):
            dv = nn(pb, dow)
            dk = nn(db, qw)
            res.append((jnp.where(lane < 64, dk[:n], dk[n:]), jnp.where(lane < 64, dv[:n], dv[n:])))
        for (p, g, half, _, _), (k2, _, _, _, _), (pb, db) in zip(jobs, stage, probs):
            part = nn(k2.T, db)
            r0 = pl.multiple_of(p * 128, 128)
            if first:
                dqt[pl.ds(r0, 128), pl.ds(q0, W)] = part
            else:
                dqt[pl.ds(r0, 128), pl.ds(q0, W)] += part
        return res

    def prefix(i, carry):
        jobs = []
        for j in range(NB):
            p = i * NB + j
            g, half = p // 2, j % 2
            lanes = slice(128 * half, 128 * half + 128)
            jobs.append((p, g, half, pk[g, :, lanes], pv[g, :, lanes]))
        total = None
        for c in range(2):
            part = blocks(jobs, None, c * 512, 512, True)
            total = part if total is None else [(a + c_, b + d) for (a, b), (c_, d) in zip(total, part)]
        for (p, g, half, _, _), (dk, dv) in zip(jobs, total):
            cols = pl.ds(pl.multiple_of(p * 128, 128), 128)
            pgrad[0, :, cols] = dk
            pgrad[1, :, cols] = dv
        return carry

    lax.fori_loop(0, 8 // NB, prefix, 0)

    def tile(t, carry):
        start = win[row, t, 0]
        size = win[row, t, 1]
        k0 = pl.multiple_of(t * BLK, BLK)
        q0 = pl.multiple_of(start * BLK, BLK)

        def run(n):
            W = n * BLK
            sk = segk[0, pl.ds(k0, BLK), :]
            sq = segq[0, :, pl.ds(q0, W)]
            mask = jnp.concatenate([sk] * n, axis=1) == sq

            def batch(i, carry):
                jobs = []
                for j in range(NB):
                    p = i * NB + j
                    g, half = p // 2, j % 2
                    kt = qkv[0, g, pl.ds(k0, BLK), 256 + 128 * half : 384 + 128 * half]
                    vt = qkv[0, g, pl.ds(k0, BLK), 512 + 128 * half : 640 + 128 * half]
                    jobs.append((p, g, half, kt, vt))
                for (p, g, half, _, _), (dk, dv) in zip(jobs, blocks(jobs, mask, q0, W, False)):
                    dall[g, pl.ds(k0, BLK), 256 + 128 * half : 384 + 128 * half] = dk.astype(bf16)
                    dall[g, pl.ds(k0, BLK), 512 + 128 * half : 640 + 128 * half] = dv.astype(bf16)
                return carry

            lax.fori_loop(0, 8 // NB, batch, 0)

        for n in CLASSES:
            pl.when(size == n)(functools.partial(run, n))
        return carry

    lax.fori_loop(0, L // BLK, tile, 0)
    for c in late:
        c.wait()
    for g in range(4):
        dall[g, :, :256] = (dqt[256 * g : 256 * g + 256, :].T * 0.125).astype(bf16)
    for c in range(2):
        cols = slice(512 * c, 512 * c + 512)
        acc = gfirst[:, cols].astype(f32)
        for i in range(4):
            acc = acc + nt(dall[i], w[i, cols, :])
        low = acc.astype(bf16)
        gin[0, :, cols] = low
        own[:, cols] = low


def attn_bwd(r, rows, win, qkv, gctx, lse, delta, pk, pv, segk, segq, gfirst, w, into=None):
    row = lambda i, *_: (r, 0, 0)
    row4 = lambda i, *_: (r, 0, 0, 0)
    all_ = lambda i, *_: (0, 0, 0)
    extra = [] if into is None else [into]
    return pl.pallas_call(
        functools.partial(attn_bwd_kernel, r),
        grid_spec=pltpu.PrefetchScalarGridSpec(
            num_scalar_prefetch=2,
            grid=(1,),
            in_specs=[
                pl.BlockSpec((1, 4, L, 768), row4),
                pl.BlockSpec((1, L, D), row),
                pl.BlockSpec((1, 4, 4, L), row4),
                pl.BlockSpec((1, 4, 4, L), row4),
                pl.BlockSpec((4, PRE, 256), all_),
                pl.BlockSpec((4, PRE, 256), all_),
                pl.BlockSpec((1, L, 128), row),
                pl.BlockSpec((1, 1, L), row),
                pl.BlockSpec(memory_space=pl.ANY),
                pl.BlockSpec(memory_space=pl.ANY),
            ]
            + [pl.BlockSpec(memory_space=pl.ANY) for _ in extra],
            out_specs=[
                pl.BlockSpec((1, L, D), lambda i, rows, win: (rows[r], 0, 0)),
                pl.BlockSpec((L, D), lambda i, *_: (0, 0)),
                pl.BlockSpec((2, PRE, D), all_),
            ],
            scratch_shapes=[
                pltpu.VMEM((D, L), f32),
                pltpu.VMEM((4, L, 768), bf16),
                pltpu.VMEM((L, D), bf16),
                pltpu.VMEM((4, D, 768), bf16),
                pltpu.SemaphoreType.DMA((2,)),
            ],
        ),
        out_shape=[
            jax.ShapeDtypeStruct((3, L, D), bf16),
            jax.ShapeDtypeStruct((L, D), bf16),
            jax.ShapeDtypeStruct((2, PRE, D), f32),
        ],
        input_output_aliases={12: 0} if extra else {},
        compiler_params=pltpu.CompilerParams(vmem_limit_bytes=60 << 20),
        cost_estimate=pl.CostEstimate(flops=40 * 10**9, bytes_accessed=32 << 20, transcendentals=0),
        name="attn_bwd",
    )(rows, win, qkv, gctx, lse, delta, pk, pv, segk, segq, gfirst, w, *extra)


HC = 512
TM = 512
EPS = 1e-5


ERF = (0.7978849414895208, 0.03633308441063725, -3.2594747109729314e-05, -5.5306315505082965e-05,
       3.964772884359942e-06, -1.3226625462816106e-07, 1.7562766828961903e-09)


def gelu_parts(v):
    u = v * v
    w = jnp.minimum(u, 31.36)
    p = ERF[6] * w + ERF[5]
    for c in ERF[4::-1]:
        p = p * w + c
    phi = 0.5 * jnp.tanh(v * p) + 0.5
    return v * phi, phi


def norm_stats(z):
    mean = jnp.mean(z, axis=1, keepdims=True)
    c = z - mean
    var = jnp.mean(c * c, axis=1, keepdims=True)
    r = lax.rsqrt(var + EPS)
    return c * r, r


RC = 512


def tokens_kernel(rows, ctx, x, cot, wo, win, wout, bo, g1, s1, bi, b2, g2, s2, out, own, gf, gc, delta, xhat, zbuf, low, act, gp, rs, vb):
    M = TM

    def dot_cols(i, carry):
        c0 = pl.multiple_of(i * 256, 256)
        zbuf[:, pl.ds(c0, 256)] = nn(ctx[...], wo[:, pl.ds(c0, 256)]) + x[:, pl.ds(c0, 256)].astype(f32)
        return carry

    lax.fori_loop(0, 4, dot_cols, 0, unroll=4)

    def ln1(i, carry):
        r0 = i * RC
        n, r = norm_stats(zbuf[pl.ds(r0, RC), :] + bo[...])
        xhat[pl.ds(r0, RC), :] = n
        rs[pl.ds(r0, RC), :] = jnp.broadcast_to(r, (RC, 128))
        y = n * g1[...] + s1[...]
        zbuf[pl.ds(r0, RC), :] = y
        low[pl.ds(r0, RC), :] = y.astype(bf16)
        return carry

    ln1(0, 0)

    def up(i, carry):
        z, c = i // 2, i % 2
        c0 = pl.multiple_of(c * HC, HC)
        h0 = pl.multiple_of(i * HC, HC)
        h = nn(low[...], win[z, :, pl.ds(c0, HC)]) + bi[z, :, pl.ds(pl.multiple_of(768 + c * HC, 256), HC)]
        a, d = gelu_parts(h)
        act[:, pl.ds(h0, HC)] = a.astype(bf16)
        gp[:, pl.ds(h0, HC)] = d.astype(bf16)
        vb[:, pl.ds(h0, HC)] = h.astype(bf16)
        return carry

    lax.fori_loop(0, 8, up, 0, unroll=8)

    def down(i, carry):
        c0 = pl.multiple_of(i * 256, 256)
        zbuf[:, pl.ds(c0, 256)] += nn(act[...], wout[:, pl.ds(c0, 256)])
        return carry

    lax.fori_loop(0, 4, down, 0, unroll=4)

    def ln2(i, carry):
        r0 = i * RC
        n, r = norm_stats(zbuf[pl.ds(r0, RC), :] + b2[...])
        result = (n * g2[...] + s2[...]).astype(bf16)
        out[pl.ds(r0, RC), :] = result
        own[pl.ds(r0, RC), :] = result
        g = cot[pl.ds(r0, RC), :].astype(f32) * g2[...]
        m1 = jnp.mean(g, axis=1, keepdims=True)
        m2 = jnp.mean(g * n, axis=1, keepdims=True)
        d = (g - m1 - n * m2) * r
        zbuf[pl.ds(r0, RC), :] = d
        low[pl.ds(r0, RC), :] = d.astype(bf16)
        return carry

    ln2(0, 0)

    def back(i, carry):
        h0 = pl.multiple_of(i * HC, HC)
        d = nt(low[...], wout[pl.ds(h0, HC), :])
        v = vb[:, pl.ds(h0, HC)].astype(f32)
        slope = gp[:, pl.ds(h0, HC)].astype(f32) + v * (jnp.exp(-0.5 * v * v) * 0.3989422804014327)
        act[:, pl.ds(h0, HC)] = (d * slope).astype(bf16)
        return carry

    lax.fori_loop(0, 8, back, 0, unroll=8)

    def back2(i, carry):
        c0 = pl.multiple_of(i * 256, 256)
        acc = zbuf[:, pl.ds(c0, 256)]
        for z in range(4):
            acc = acc + nt(act[:, 1024 * z : 1024 * z + 1024], win[z, pl.ds(c0, 256), :])
        zbuf[:, pl.ds(c0, 256)] = acc
        return carry

    lax.fori_loop(0, 4, back2, 0, unroll=4)

    def ln1b(i, carry):
        r0 = i * RC
        n = xhat[pl.ds(r0, RC), :]
        g = zbuf[pl.ds(r0, RC), :] * g1[...]
        m1 = jnp.mean(g, axis=1, keepdims=True)
        m2 = jnp.mean(g * n, axis=1, keepdims=True)
        d = (g - m1 - n * m2) * rs[pl.ds(r0, RC), 0:1]
        gf[pl.ds(r0, RC), :] = d.astype(bf16)
        return carry

    ln1b(0, 0)

    def gcols(i, carry):
        c0 = pl.multiple_of(i * 256, 256)
        part = nt(gf[...], wo[pl.ds(c0, 256), :]).astype(bf16)
        gc[:, pl.ds(c0, 256)] = part
        prod = part.astype(f32) * ctx[:, pl.ds(c0, 256)].astype(f32)
        high = prod.astype(bf16)
        rest = (prod - high.astype(f32)).astype(bf16)
        row = lax.broadcasted_iota(jnp.int32, (256, 128), 0)
        lane = lax.broadcasted_iota(jnp.int32, (256, 128), 1)
        pick = jnp.where(row // 64 + 8 * i == lane, 1.0, 0.0).astype(bf16)
        carry = carry + nn(high, pick) + nn(rest, pick)
        return carry

    heads = lax.fori_loop(0, 4, gcols, jnp.zeros((M, 128), f32), unroll=4).T
    for g in range(4):
        delta[g] = heads[8 * g : 8 * g + 4]


def tokens(rows, ctx, x, cot, wo, win, wout, bo, g1, s1, bi, b2, g2, s2):
    R = ctx.shape[0]
    per = L // TM
    own = pl.BlockSpec((None, TM, D), lambda i, rows: (1 - i // per, i % per, 0))
    pick = pl.BlockSpec((None, TM, D), lambda i, rows: (rows[1 - i // per], i % per, 0))
    whole = lambda a: pl.BlockSpec(a.shape, lambda i, rows: (0,) * a.ndim, pipeline_mode=pl.Buffered(1))
    consts = (wo, win, wout, bo, g1, s1, bi, b2, g2, s2)
    return pl.pallas_call(
        tokens_kernel,
        grid_spec=pltpu.PrefetchScalarGridSpec(
            num_scalar_prefetch=1,
            grid=(R * per,),
            in_specs=[own, pick, pick] + [whole(a) for a in consts],
            out_specs=[pick, pl.BlockSpec((TM, D), lambda i, rows: (jnp.maximum(i - per, 0), 0)), own, own, pl.BlockSpec((None, 4, 4, TM), lambda i, rows: (1 - i // per, 0, 0, i % per))],
            scratch_shapes=[
                pltpu.VMEM((TM, D), f32),
                pltpu.VMEM((TM, D), f32),
                pltpu.VMEM((TM, D), bf16),
                pltpu.VMEM((TM, 4 * D), bf16),
                pltpu.VMEM((TM, 4 * D), bf16),
                pltpu.VMEM((TM, 128), f32),
                pltpu.VMEM((TM, 4 * D), bf16),
            ],
        ),
        out_shape=[
            jax.ShapeDtypeStruct((3, L, D), bf16),
            jax.ShapeDtypeStruct((L, D), bf16),
            jax.ShapeDtypeStruct((R, L, D), bf16),
            jax.ShapeDtypeStruct((R, L, D), bf16),
            jax.ShapeDtypeStruct((R, 4, 4, L), f32),
        ],
        compiler_params=pltpu.CompilerParams(vmem_limit_bytes=60 << 20),
        cost_estimate=pl.CostEstimate(flops=80 * 10**9, bytes_accessed=40 << 20, transcendentals=0),
        name="tokens",
    )(rows, ctx, x, cot, *consts)


SPAN = 512
KINDS = 10


def front_kernel(
    hid, seg, msk, pk_s, pv_s, bq, bk, bv, bi, wq, wk, wv, wo_s, wi_s, wu_s,
    wqkv, wo, wi, wu, qkv, ctx, lse, pk, pv, vec, segk, segq,
    own0, x, wbuf, qb, vt, cb, pre, xsem, lsem, osem, ssem, rsem,
):
    d = lax.axis_index("dp")
    z = lax.axis_index("prefix")
    core, xx, yy = d % 2, (d // 2) % 2, d // 4
    dc = d + 1 - 2 * core
    dx = d + 2 - 4 * xx
    dy = d + 4 - 8 * yy
    dxy = dx + dy - d
    unique = 2 * (z % 2)
    MESH = pl.DeviceIdType.MESH

    def region(pay, zz, dd, half=None):
        if pay >= 4:
            return (pre, vec)[pay - 4].at[zz]
        if pay == 0:
            n, ref = 128, lambda o, s: wqkv.at[zz, pl.ds(128 * dd + o, s), :]
        elif pay == 1:
            n, ref = 256, lambda o, s: wo.at[pl.ds(256 * zz + o, s), pl.ds(128 * dd, 128)]
        elif pay == 2:
            n, ref = 128, lambda o, s: wi.at[zz, pl.ds(128 * dd + o, s), :]
        else:
            n, ref = 1024, lambda o, s: wu.at[pl.ds(1024 * zz + o, s), pl.ds(128 * dd, 128)]
        return ref(0, n) if half is None else ref(half * (n // 2), n // 2)

    own0[:, 0:256] = wq[...]
    own0[:, 256:512] = wk[...]
    own0[:, 512:768] = wv[...]
    shards = (own0, wo_s, wi_s, wu_s)
    xin = [pltpu.make_async_copy(hid.at[unique], x.at[0], xsem.at[0]), pltpu.make_async_copy(hid.at[1], x.at[1], xsem.at[1])]
    for c in xin:
        c.start()

    bar = pltpu.get_barrier_semaphore()

    def hello(dev):
        pl.semaphore_signal(bar, inc=1, device_id=dev, device_id_type=MESH)

    for dd in (dc, dx, dy):
        hello((dd, z))
    pl.when(z > 0)(lambda: hello((d, z - 1)))
    pl.when(z < 3)(lambda: hello((d, z + 1)))

    pre[z, 0:24, :] = pk_s[...]
    pre[z, 32:56, :] = pv_s[...]
    vec[z, :, 0:256] = bq[...]
    vec[z, :, 256:512] = bk[...]
    vec[z, :, 512:768] = bv[...]
    vec[z, :, 768:] = bi[...]
    for r in range(2):
        own = seg[pl.ds(unique, 1), :] if r == 0 else seg[1:2, :]
        real = msk[pl.ds(unique, 1), :] if r == 0 else msk[1:2, :]
        segq[r] = own.astype(f32)
        keys = jnp.where(real == 1, own, -1).astype(f32)
        segk[r] = jnp.broadcast_to(keys, (128, L)).T

    local = [pltpu.make_async_copy(shards[i], region(i, z, d), lsem.at[i]) for i in range(4)]
    for c in local:
        c.start()
    peers = jnp.where(z > 0, 1, 0) + jnp.where(z < 3, 1, 0)
    pl.semaphore_wait(bar, 3 + peers)

    def copy(kind, pay, zz, dd, half, dev, skind, src=None):
        r = region(pay, zz, dd, half)
        return pltpu.make_async_remote_copy(
            src_ref=r if src is None else src, dst_ref=r, send_sem=ssem.at[pay * 4 + zz, skind], recv_sem=rsem.at[pay * 4 + zz, kind],
            device_id=dev, device_id_type=MESH,
        )

    def block(k):
        second = jnp.where(z == 0, 1, z - 1)
        third = jnp.where(z == 0, 2, jnp.where(z == 3, 1, z + 1))
        last = jnp.where(z <= 1, 3, 0)
        return jnp.where(k == 0, z, jnp.where(k == 1, second, jnp.where(k == 2, third, last)))

    def up(pay, zz, src=None):
        return copy(0, pay, zz, d, None, (d, z + 1), 10, src)

    def down(pay, zz, src=None):
        return copy(0, pay, zz, d, None, (d, z - 1), 0, src)

    def along(pay, h):
        @pl.when(z >= h)
        def _():
            up(pay, z - h).wait_recv()
            pl.when(z < 3)(lambda: up(pay, z - h).start())

        @pl.when(z + h <= 3)
        def _():
            down(pay, z + h).wait_recv()
            pl.when(z > 0)(lambda: down(pay, z + h).start())

    def stage1(pay, k, src=None):
        zz = block(k)
        copy(1, pay, zz, d, None, (dx, z), 1, src).start()
        copy(2, pay, zz, d, None, (dy, z), 2, src).start()
        copy(5, pay, zz, d, None, (dc, z), 5, src).start()

    def stage2(pay, k):
        zz = block(k)
        copy(1, pay, zz, dx, None, (dx, z), 1).wait_recv()
        copy(3, pay, zz, dx, 0, (dy, z), 3).start()
        copy(6, pay, zz, dx, None, (dc, z), 6).start()
        copy(2, pay, zz, dy, None, (dy, z), 2).wait_recv()
        copy(4, pay, zz, dy, 1, (dx, z), 4).start()
        copy(7, pay, zz, dy, None, (dc, z), 7).start()

    def stage3(pay, k):
        zz = block(k)
        copy(3, pay, zz, dxy, 0, (dy, z), 3).wait_recv()
        copy(8, pay, zz, dxy, 0, (dc, z), 8).start()
        copy(4, pay, zz, dxy, 1, (dx, z), 4).wait_recv()
        copy(9, pay, zz, dxy, 1, (dc, z), 9).start()

    def stage4(pay, k):
        zz = block(k)
        o = dc - d
        copy(5, pay, zz, d + o, None, (dc, z), 5).wait_recv()
        copy(6, pay, zz, dx + o, None, (dc, z), 6).wait_recv()
        copy(7, pay, zz, dy + o, None, (dc, z), 7).wait_recv()
        copy(8, pay, zz, dxy + o, 0, (dc, z), 8).wait_recv()
        copy(9, pay, zz, dxy + o, 1, (dc, z), 9).wait_recv()

    def drain(pay, zz):
        pl.when((zz <= z) & (z < 3))(lambda: up(pay, zz).wait_send())
        pl.when((zz >= z) & (z > 0))(lambda: down(pay, zz).wait_send())
        if pay >= 4:
            return
        copy(1, pay, zz, d, None, (dx, z), 1).wait_send()
        copy(2, pay, zz, d, None, (dy, z), 2).wait_send()
        copy(3, pay, zz, dx, 0, (dy, z), 3).wait_send()
        copy(4, pay, zz, dy, 1, (dx, z), 4).wait_send()
        copy(5, pay, zz, d, None, (dc, z), 5).wait_send()
        copy(6, pay, zz, dx, None, (dc, z), 6).wait_send()
        copy(7, pay, zz, dy, None, (dc, z), 7).wait_send()
        copy(8, pay, zz, dxy, 0, (dc, z), 8).wait_send()
        copy(9, pay, zz, dxy, 1, (dc, z), 9).wait_send()

    ffn = (2, 3, 1)
    stage1(0, 0, own0)
    for pay in (0, 4, 5) + ffn:
        src = shards[pay] if pay < 4 else None
        pl.when(z < 3)(functools.partial(lambda p, src: up(p, z, src).start(), pay, src))
        pl.when(z > 0)(functools.partial(lambda p, src: down(p, z, src).start(), pay, src))
    stage1(2, 0, wi_s)
    stage2(0, 0)
    along(0, 1)
    stage1(0, 1)
    for pay in (4, 5):
        along(pay, 1)
    stage3(0, 0)
    stage1(3, 0, wu_s)
    stage1(1, 0, wo_s)
    for pay in (4, 5):
        along(pay, 2)
    along(0, 2)
    for pay in (4, 5):
        along(pay, 3)
    for g in range(4):
        lanes = slice(256 * g, 256 * g + 256)
        for ref, o in ((pk, 0), (pv, 32)):
            parts = [pre[i, o : o + 32, lanes].astype(f32)[:24] for i in range(4)]
            ref[g] = jnp.concatenate(parts, axis=0).astype(bf16)
    for c in xin + local:
        c.wait()

    def outs(zz):
        q = [pltpu.make_async_copy(qb.at[r], qkv.at[r, zz], osem.at[r]) for r in range(2)]
        c = [
            pltpu.make_async_copy(cb.at[r], ctx.at[r, :, pl.ds(pl.multiple_of(256 * zz, 256), 256)], osem.at[2 + r])
            for r in range(2)
        ]
        return q, c

    def project(r, zz):
        y = nn(x[r], wbuf[...]) + vec[zz, :, 0:768]
        qb[r, :, 0:256] = (y[:, :256].astype(bf16) * 0.125).astype(bf16)
        kv = y[:, 256:].astype(bf16)
        qb[r, :, 256:] = kv
        vt[r, :, :L] = kv[:, 256:].T
        vt[r, :, L:] = pv[zz].T

    def attend(t, zz):
        jobs = []
        for tt in (t, L // BLK - 1 - t):
            first = max(0, tt - SPAN // BLK)
            stop = min(L // BLK, tt + SPAN // BLK + 1)
            k = slice(first * BLK, stop * BLK)
            q = slice(tt * BLK, tt * BLK + BLK)
            for r in range(2):
                seen = segk[r, k, :] == segq[r, :, q]
                for p in range(2):
                    lanes = slice(128 * p, 128 * p + 128)
                    q2 = stack_heads(qb[r, q, lanes])
                    s = nt(qb[r, k, 256 + 128 * p : 384 + 128 * p], q2)
                    jobs.append((r, p, q, k, lanes, seen, s, nt(pk[zz, :, lanes], q2)))
        stage = []
        for r, p, q, k, lanes, seen, s, sp in jobs:
            s = jnp.concatenate([jnp.where(seen, s[:, :128], NEG), jnp.where(seen, s[:, 128:], NEG)], axis=1)
            top = jnp.maximum(jnp.max(s, axis=0, keepdims=True), jnp.max(sp, axis=0, keepdims=True))
            stage.append((s, sp, top))
        probs = []
        for s, sp, top in stage:
            e = jnp.exp(s - top)
            ep = jnp.exp(sp - top)
            total = jnp.sum(e, axis=0, keepdims=True) + jnp.sum(ep, axis=0, keepdims=True)
            probs.append((e.astype(bf16), ep.astype(bf16), total, top))
        res = []
        for (r, p, q, k, lanes, _, _, _), (e, ep, total, top) in zip(jobs, probs):
            res.append(nn(vt[r, lanes, k], e) + nn(vt[r, lanes, L : L + PRE], ep))
        for (r, p, q, k, lanes, _, _, _), (e, ep, total, top), o in zip(jobs, probs, res):
            o = o * (1.0 / total)
            o = jnp.concatenate([o[:64, :128], o[64:, 128:]], axis=0)
            cb[r, q, lanes] = o.T.astype(bf16)
            lt = top + jnp.log(total)
            lse[r, zz, 2 * p : 2 * p + 1, q] = lt[:, :128]
            lse[r, zz, 2 * p + 1 : 2 * p + 2, q] = lt[:, 128:]

    def group(s, carry):
        zz = block(s)

        def soon(far, fn, pays):
            @pl.when(s + far <= 3)
            def _():
                for pay in pays:
                    fn(pay, s + far)

        soon(2, stage1, (0,))
        stage4(0, s)
        win = pltpu.make_async_copy(wqkv.at[zz], wbuf, xsem.at[2])
        win.start()
        soon(1, stage2, (0,))

        @pl.when(s > 0)
        def _():
            q, c = outs(block(s - 1))
            for o in q + c:
                o.wait()

        win.wait()
        project(0, zz)
        stage2(2, s)
        soon(1, stage3, (0,))
        project(1, zz)
        q, c = outs(zz)
        for o in q:
            o.start()
        soon(1, along, ffn)
        soon(1, stage1, ffn)
        attend(0, zz)
        stage2(3, s)
        soon(3, along, (0,))
        attend(1, zz)
        stage2(1, s)
        stage3(2, s)
        attend(2, zz)
        stage3(3, s)
        stage3(1, s)
        attend(3, zz)
        for o in c:
            o.start()
        return carry

    lax.fori_loop(0, 4, group, 0)
    q, c = outs(block(3))
    for o in q + c:
        o.wait()

    def finish(k, carry):
        for pay in (1, 2, 3):
            stage4(pay, k)
        for pay in range(6):
            drain(pay, k)
        return carry

    lax.fori_loop(0, 4, finish, 0)


def front(hid, seg, msk, pk, pv, bq, bk, bv, bi, wq, wk, wv, wo, wi, wu):
    any_ = pl.BlockSpec(memory_space=pl.ANY)
    vmem = pl.BlockSpec(memory_space=pltpu.VMEM)
    shape = jax.ShapeDtypeStruct
    return pl.pallas_call(
        front_kernel,
        in_specs=[any_] + [vmem] * 14,
        out_specs=[any_] * 6 + [vmem] * 6,
        out_shape=[
            shape((4, D, 768), bf16),
            shape((D, D), bf16),
            shape((4, D, D), bf16),
            shape((4 * D, D), bf16),
            shape((2, 4, L, 768), bf16),
            shape((2, L, D), bf16),
            shape((2, 4, 4, L), f32),
            shape((4, PRE, 256), bf16),
            shape((4, PRE, 256), bf16),
            shape((4, 1, 1792), f32),
            shape((2, L, 128), f32),
            shape((2, 1, L), f32),
        ],
        scratch_shapes=[
            pltpu.VMEM((128, 768), bf16),
            pltpu.VMEM((2, L, D), bf16),
            pltpu.VMEM((D, 768), bf16),
            pltpu.VMEM((2, L, 768), bf16),
            pltpu.VMEM((2, 256, L + PRE), bf16),
            pltpu.VMEM((2, L, 256), bf16),
            pltpu.VMEM((4, 64, D), bf16),
            pltpu.SemaphoreType.DMA((3,)),
            pltpu.SemaphoreType.DMA((4,)),
            pltpu.SemaphoreType.DMA((4,)),
            pltpu.SemaphoreType.DMA((24, KINDS + 1)),
            pltpu.SemaphoreType.DMA((24, KINDS)),
        ],
        compiler_params=pltpu.CompilerParams(
            collective_id=0, has_side_effects=True, vmem_limit_bytes=60 << 20
        ),
        name="front",
    )(hid, seg, msk, pk, pv, bq, bk, bv, bi, wq, wk, wv, wo, wi, wu)


def front_plain(rows, hid, seg, msk, pk, pv, bq, bk, bv, bi, wq, wk, wv, wo, wi, wu):
    over = lambda v, axis, at: lax.all_gather(v, axis, axis=at, tiled=True)
    each = lambda v: lax.all_gather(v, "prefix")
    wqkv = each(jnp.concatenate([over(w, "dp", 0) for w in (wq, wk, wv)], axis=1))
    vec = each(jnp.concatenate([bq, bk, bv, bi], axis=1))
    by_group = lambda p: over(p, "prefix", 0).reshape(PRE, 4, 256).transpose(1, 0, 2)
    pk, pv = by_group(pk), by_group(pv)
    segk = jnp.broadcast_to(jnp.where(msk == 1, seg, -1)[rows][:, :, None], (2, L, 128)).astype(f32)
    segq = seg[rows][:, None, :].astype(f32)
    qkv, ctx, lse = attn_fwd(rows, windows(seg[rows]), hid, wqkv, vec[:, :, :768], pk, pv, segk, segq)
    return (
        wqkv, over(over(wo, "dp", 1), "prefix", 0), each(over(wi, "dp", 0)), over(over(wu, "dp", 1), "prefix", 0),
        qkv, ctx, lse, pk, pv, vec, segk, segq,
    )


def total_kernel(uniq, shared, key, value, away, other, mine, half, slots, ssem, rsem):
    d = lax.axis_index("dp")
    z = lax.axis_index("prefix")
    core, chip = d % 2, d // 2
    xx, yy = chip % 2, chip // 2
    dc = d + 1 - 2 * core
    peers = [((d + 2 - 4 * xx), chip + 1 - 2 * xx), ((d + 4 - 8 * yy), chip + 2 - 4 * yy)]
    peers.append((peers[0][0] + peers[1][0] - d, 3 - chip))
    zp = z + 1 - 2 * (z % 2)
    bar = pltpu.get_barrier_semaphore()
    pl.semaphore_signal(bar, inc=1, device_id=(d, zp), device_id_type=pl.DeviceIdType.MESH)
    for dd in (dc, *(p for p, _ in peers)):
        pl.semaphore_signal(bar, inc=1, device_id=(dd, z), device_id_type=pl.DeviceIdType.MESH)
    n = key.shape[0]
    r0 = pl.multiple_of(z * n, 8)
    away[...] = uniq[:, pl.ds(pl.multiple_of(zp * n, 8), n), :]
    pl.semaphore_wait(bar, 5)

    def send(src, dst, i, dd, zz=None):
        return pltpu.make_async_remote_copy(
            src_ref=src, dst_ref=dst, send_sem=ssem.at[i], recv_sem=rsem.at[i],
            device_id=(dd, z if zz is None else zz), device_id_type=pl.DeviceIdType.MESH,
        )

    swap = send(away, other, 6, d, zp)
    swap.start()
    mine[...] = uniq[:, pl.ds(r0, n), :] + shared[:, pl.ds(r0, n), :]
    swap.wait()
    mine[...] += other[...]

    first = send(mine.at[1 - core], half, 0, dc)
    first.start()
    first.wait()
    slots[chip] = mine[core] + half[...]
    copies = [send(slots.at[chip], slots.at[chip], 1 + i, dd) for i, (dd, _) in enumerate(peers)]
    for c in copies:
        c.start()
    for c in copies:
        c.wait()
    total = (slots[0] + slots[1]) + (slots[2] + slots[3])

    @pl.when(core == 0)
    def _():
        key[...] = total
        last = send(key, key, 4, dc)
        last.start()
        last.wait_send()
        send(value, value, 5, dc).wait_recv()

    @pl.when(core == 1)
    def _():
        value[...] = total
        last = send(value, value, 5, dc)
        last.start()
        last.wait_send()
        send(key, key, 4, dc).wait_recv()


def total_grads(uniq, shared):
    n = PRE // 4
    vmem = pl.BlockSpec(memory_space=pltpu.VMEM)
    return pl.pallas_call(
        total_kernel,
        in_specs=[vmem] * 2,
        out_specs=[vmem] * 2,
        out_shape=[jax.ShapeDtypeStruct((n, D), f32)] * 2,
        scratch_shapes=[
            pltpu.VMEM((2, n, D), f32),
            pltpu.VMEM((2, n, D), f32),
            pltpu.VMEM((2, n, D), f32),
            pltpu.VMEM((n, D), f32),
            pltpu.VMEM((4, n, D), f32),
            pltpu.SemaphoreType.DMA((7,)),
            pltpu.SemaphoreType.DMA((7,)),
        ],
        compiler_params=pltpu.CompilerParams(collective_id=1, has_side_effects=True),
        name="total_grads",
    )(uniq, shared)


def body(
    hidden_in, cotangent, segment_ids, key_mask, prefix_keys, prefix_values,
    w_query, b_query, w_key, b_key, w_value, b_value, w_attn_out, b_attn_out, gain_attn, shift_attn,
    w_ffn_in, b_ffn_in, w_ffn_out, b_ffn_out, gain_ffn, shift_ffn,
):
    z = lax.axis_index("prefix")
    side = z % 2
    rows = jnp.stack([2 * side, jnp.ones_like(side)]).astype(jnp.int32)
    line = lambda v: v.reshape(1, -1)
    small = lax.axis_size("dp") == 8 and lax.axis_size("prefix") == 4
    start = front if small else functools.partial(front_plain, rows)
    w_qkv, w_out, w_up, w_down, qkv, ctx, lse, pk, pv, vec, segk, segq = start(
        hidden_in, segment_ids, key_mask, prefix_keys, prefix_values,
        line(b_query), line(b_key), line(b_value), line(b_ffn_in),
        w_query, w_key, w_value, w_attn_out, w_ffn_in, w_ffn_out,
    )
    win = windows(jnp.stack([jnp.where(side == 0, segment_ids[0], segment_ids[2]), segment_ids[1]]))
    out, out_own, gfirst, gctx, delta = tokens(
        rows, ctx, hidden_in, cotangent, w_out, w_up, w_down, line(b_attn_out), line(gain_attn), line(shift_attn),
        vec, line(b_ffn_out), line(gain_ffn), line(shift_ffn),
    )
    pairs = [(i, i + 1 - 2 * (i % 2)) for i in range(lax.axis_size("prefix"))]
    swap = lambda v: lax.ppermute(v, "prefix", pairs)
    put = lambda v, r: lax.dynamic_update_slice_in_dim(v, r[None], 2 - rows[0], 0)
    out_other = swap(out_own)
    args = (rows, win, qkv, gctx, lse, delta, pk, pv, segk, segq, gfirst, w_qkv)
    gin, gin_own, uniq = attn_bwd(0, *args)
    gin_other = swap(gin_own)
    gin, out_other = lax.optimization_barrier((gin, out_other))
    gin, _, shared = attn_bwd(1, *args, into=gin)
    if small:
        keys, values = total_grads(uniq, shared)
    else:
        n = PRE // lax.axis_size("prefix")
        other = swap(lax.dynamic_slice_in_dim(uniq, (z + 1 - 2 * side) * n, n, 1))
        keys, values = lax.psum(lax.dynamic_slice_in_dim(uniq + shared, z * n, n, 1) + other, "dp")
    return put(out, out_other), put(gin, gin_other), keys, values


def solution(mesh):
    return jax.shard_map(
        body,
        mesh=mesh,
        in_specs=(
            P("dp", None, None), P("dp", None, None), P("dp", None), P("dp", None),
            P("prefix", None), P("prefix", None),
            P("dp", "prefix"), P("prefix"), P("dp", "prefix"), P("prefix"), P("dp", "prefix"), P("prefix"),
            P("prefix", "dp"), P(), P(), P(),
            P("dp", "prefix"), P("prefix"), P("prefix", "dp"), P(), P(), P(),
        ),
        out_specs=(P("dp", None, None), P("dp", None, None), P("prefix", None), P("prefix", None)),
        check_vma=False,
    )
```

```python
import functools
import jax
import jax.numpy as jnp
from jax import lax
from jax.experimental import pallas as pl
from jax.experimental.pallas import tpu as pltpu
from jax.sharding import PartitionSpec as P

L = 1024
D = 1024
PRE = 96
BLK = 128
NEG = -1e30
CLASSES = (2, 3, 4, 5, 6, 8)
bf16 = jnp.bfloat16
f32 = jnp.float32


def nt(a, b):
    return lax.dot_general(a, b, (((1,), (1,)), ((), ())), preferred_element_type=f32)


def nn(a, b):
    return jnp.dot(a, b, preferred_element_type=f32)


def stack_heads(tile):
    lane = lax.broadcasted_iota(jnp.int32, tile.shape, 1)
    zero = jnp.zeros_like(tile)
    return jnp.concatenate([jnp.where(lane < 64, tile, zero), jnp.where(lane >= 64, tile, zero)], axis=0)


def windows(seg):
    tiles = seg.shape[-1] // BLK
    first = seg[..., ::BLK]
    last = seg[..., BLK - 1 :: BLK]
    start = jnp.sum((seg[..., None, :] < first[..., :, None]).astype(jnp.int32), axis=-1) // BLK
    stop = (jnp.sum((seg[..., None, :] <= last[..., :, None]).astype(jnp.int32), axis=-1) + BLK - 1) // BLK
    need = stop - start
    size = jnp.full_like(need, CLASSES[-1])
    for n in reversed(CLASSES[:-1]):
        size = jnp.where(need <= n, n, size)
    start = jnp.minimum(start, tiles - size)
    return jnp.stack([start, size], axis=-1)


NP = 8


def attn_fwd_kernel(rows, win, x, w, b, pk, pv, segk, segq, qkv, ctx, lse, vt):
    row = pl.program_id(0)
    for g in range(4):
        y = nn(x[0], w[g]) + b[g]
        q = (y[:, :256].astype(bf16) * 0.125).astype(bf16)
        qkv[0, g, :, :256] = q
        kv = y[:, 256:].astype(bf16)
        qkv[0, g, :, 256:] = kv
        vt[256 * g : 256 * g + 256, :L] = kv[:, 256:].T
        vt[256 * g : 256 * g + 256, L:] = pv[g].T

    def tile(t, carry):
        start = win[row, t, 0]
        size = win[row, t, 1]
        q0 = pl.multiple_of(t * BLK, BLK)
        k0 = pl.multiple_of(start * BLK, BLK)

        def run(n):
            W = n * BLK
            mask = segk[0, pl.ds(k0, W), :] == segq[0, :, pl.ds(q0, BLK)]

            def batch(i, carry):
                jobs = []
                for j in range(NP):
                    p = i * NP + j
                    g, half = p // 2, j % 2
                    lanes = slice(128 * half, 128 * half + 128)
                    klanes = slice(256 + 128 * half, 384 + 128 * half)
                    q2 = stack_heads(qkv[0, g, pl.ds(q0, BLK), lanes])
                    jobs.append((p, g, half, nt(qkv[0, g, pl.ds(k0, W), klanes], q2), nt(pk[g, :, lanes], q2)))
                stage = []
                for p, g, half, s, sp in jobs:
                    s = jnp.concatenate([jnp.where(mask, s[:, :128], NEG), jnp.where(mask, s[:, 128:], NEG)], axis=1)
                    top = jnp.maximum(jnp.max(s, axis=0, keepdims=True), jnp.max(sp, axis=0, keepdims=True))
                    stage.append((s, sp, top))
                probs = []
                for s, sp, top in stage:
                    e = jnp.exp(s - top)
                    ep = jnp.exp(sp - top)
                    total = jnp.sum(e, axis=0, keepdims=True) + jnp.sum(ep, axis=0, keepdims=True)
                    probs.append((e.astype(bf16), ep.astype(bf16), total, top))
                outs = []
                for (p, g, half, _, _), (e, ep, total, top) in zip(jobs, probs):
                    r0 = pl.multiple_of(p * 128, 128)
                    outs.append(nn(vt[pl.ds(r0, 128), pl.ds(k0, W)], e) + nn(vt[pl.ds(r0, 128), L : L + PRE], ep))
                for (p, g, half, _, _), (e, ep, total, top), o in zip(jobs, probs, outs):
                    o = o * (1.0 / total)
                    o = jnp.concatenate([o[:64, :128], o[64:, 128:]], axis=0)
                    r0 = pl.multiple_of(p * 128, 128)
                    ctx[0, pl.ds(q0, BLK), pl.ds(r0, 128)] = o.T.astype(bf16)
                    lt = top + jnp.log(total)
                    lse[0, g, 2 * half : 2 * half + 1, pl.ds(q0, BLK)] = lt[:, :128]
                    lse[0, g, 2 * half + 1 : 2 * half + 2, pl.ds(q0, BLK)] = lt[:, 128:]
                return carry

            lax.fori_loop(0, 8 // NP, batch, 0)

        for n in CLASSES:
            pl.when(size == n)(functools.partial(run, n))
        return carry

    lax.fori_loop(0, L // BLK, tile, 0)


def attn_fwd(rows, win, x, w, b, pk, pv, segk, segq):
    R = rows.shape[0]
    row = lambda r, *_: (r, 0, 0)
    all_ = lambda r, *_: (0, 0, 0)
    return pl.pallas_call(
        attn_fwd_kernel,
        grid_spec=pltpu.PrefetchScalarGridSpec(
            num_scalar_prefetch=2,
            grid=(R,),
            in_specs=[
                pl.BlockSpec((1, L, D), lambda r, rows, win: (rows[r], 0, 0)),
                pl.BlockSpec((4, D, 768), all_),
                pl.BlockSpec((4, 1, 768), all_),
                pl.BlockSpec((4, PRE, 256), all_),
                pl.BlockSpec((4, PRE, 256), all_),
                pl.BlockSpec((1, L, 128), row),
                pl.BlockSpec((1, 1, L), row),
            ],
            out_specs=[
                pl.BlockSpec((1, 4, L, 768), lambda r, *_: (r, 0, 0, 0)),
                pl.BlockSpec((1, L, D), row),
                pl.BlockSpec((1, 4, 4, L), lambda r, *_: (r, 0, 0, 0)),
            ],
            scratch_shapes=[pltpu.VMEM((D, L + PRE), bf16)],
        ),
        out_shape=[
            jax.ShapeDtypeStruct((R, 4, L, 768), bf16),
            jax.ShapeDtypeStruct((R, L, D), bf16),
            jax.ShapeDtypeStruct((R, 4, 4, L), f32),
        ],
        compiler_params=pltpu.CompilerParams(vmem_limit_bytes=60 << 20),
        name="attn_fwd",
    )(rows, win, x, w, b, pk, pv, segk, segq)


NB = 4


def attn_bwd_kernel(
    row, rows, win, place, qkv_h, ctx_h, lse, gf_a, gf_b, pk, pv, segk, segq, wo_h, w_h, *rest
):
    gin, own, pgrad, dqt, dall, gfirst, gctx, ctx, qkv, delta, wo, w, sem = rest[-13:]
    half = L // 2
    moves = [
        (gf_a, gfirst.at[pl.ds(pl.multiple_of(place[0] * half, half), half)]),
        (gf_b, gfirst.at[pl.ds(pl.multiple_of(place[1] * half, half), half)]),
        (wo_h, wo),
        (ctx_h.at[row], ctx),
        (qkv_h.at[row], qkv),
        (w_h, w),
    ]
    moves = [pltpu.make_async_copy(src, dst, sem.at[i]) for i, (src, dst) in enumerate(moves)]
    for c in moves:
        c.start()
    for c in moves[:4]:
        c.wait()
    heads = jnp.zeros((L, 128), f32)
    for i in range(4):
        cols = slice(256 * i, 256 * i + 256)
        part = nt(gfirst[...], wo[cols, :]).astype(bf16)
        gctx[:, cols] = part
        prod = part.astype(f32) * ctx[:, cols].astype(f32)
        high = prod.astype(bf16)
        low = (prod - high.astype(f32)).astype(bf16)
        r = lax.broadcasted_iota(jnp.int32, (256, 128), 0)
        c = lax.broadcasted_iota(jnp.int32, (256, 128), 1)
        pick = jnp.where(r // 64 + 8 * i == c, 1.0, 0.0).astype(bf16)
        heads = heads + nn(high, pick) + nn(low, pick)
    heads = heads.T
    for i in range(4):
        delta[i] = heads[8 * i : 8 * i + 8]
    moves[4].wait()

    def blocks(jobs, mask, q0, W, first):
        n = jobs[0][3].shape[0]
        stage = []
        for p, g, half, kt, vt in jobs:
            lanes = slice(128 * half, 128 * half + 128)
            k2 = stack_heads(kt)
            qw = qkv[g, pl.ds(q0, W), lanes]
            dow = gctx[pl.ds(q0, W), pl.ds(pl.multiple_of(p * 128, 128), 128)]
            stage.append((k2, qw, dow, nt(k2, qw), nt(stack_heads(vt), dow)))
        probs = []
        for (p, g, half, _, _), (k2, qw, dow, s, dp) in zip(jobs, stage):
            ps, ds = [], []
            for h in range(2):
                r = 2 * half + h
                sh = s[h * n : h * n + n] - lse[0, g, r : r + 1, pl.ds(q0, W)]
                if mask is not None:
                    sh = jnp.where(mask, sh, NEG)
                ph = jnp.exp(sh)
                ps.append(ph.astype(bf16))
                ds.append((ph * (dp[h * n : h * n + n] - delta[g, r : r + 1, pl.ds(q0, W)])).astype(bf16))
            probs.append((jnp.concatenate(ps, axis=0), jnp.concatenate(ds, axis=0)))
        lane = lax.broadcasted_iota(jnp.int32, (n, 128), 1)
        res = []
        for (p, g, half, _, _), (k2, qw, dow, _, _), (pb, db) in zip(jobs, stage, probs):
            dv = nn(pb, dow)
            dk = nn(db, qw)
            res.append((jnp.where(lane < 64, dk[:n], dk[n:]), jnp.where(lane < 64, dv[:n], dv[n:])))
        for (p, g, half, _, _), (k2, _, _, _, _), (pb, db) in zip(jobs, stage, probs):
            part = nn(k2.T, db)
            r0 = pl.multiple_of(p * 128, 128)
            if first:
                dqt[pl.ds(r0, 128), pl.ds(q0, W)] = part
            else:
                dqt[pl.ds(r0, 128), pl.ds(q0, W)] += part
        return res

    def prefix(i, carry):
        jobs = []
        for j in range(NB):
            p = i * NB + j
            g, half = p // 2, j % 2
            lanes = slice(128 * half, 128 * half + 128)
            jobs.append((p, g, half, pk[g, :, lanes], pv[g, :, lanes]))
        total = None
        for c in range(2):
            part = blocks(jobs, None, c * 512, 512, True)
            total = part if total is None else [(a + c_, b + d) for (a, b), (c_, d) in zip(total, part)]
        for (p, g, half, _, _), (dk, dv) in zip(jobs, total):
            cols = pl.ds(pl.multiple_of(p * 128, 128), 128)
            pgrad[0, :, cols] = dk
            pgrad[1, :, cols] = dv
        return carry

    lax.fori_loop(0, 8 // NB, prefix, 0)

    def tile(t, carry):
        start = win[row, t, 0]
        size = win[row, t, 1]
        k0 = pl.multiple_of(t * BLK, BLK)
        q0 = pl.multiple_of(start * BLK, BLK)

        def run(n):
            W = n * BLK
            sk = segk[0, pl.ds(k0, BLK), :]
            sq = segq[0, :, pl.ds(q0, W)]
            mask = jnp.concatenate([sk] * n, axis=1) == sq

            def batch(i, carry):
                jobs = []
                for j in range(NB):
                    p = i * NB + j
                    g, half = p // 2, j % 2
                    kt = qkv[g, pl.ds(k0, BLK), 256 + 128 * half : 384 + 128 * half]
                    vt = qkv[g, pl.ds(k0, BLK), 512 + 128 * half : 640 + 128 * half]
                    jobs.append((p, g, half, kt, vt))
                for (p, g, half, _, _), (dk, dv) in zip(jobs, blocks(jobs, mask, q0, W, False)):
                    dall[g, pl.ds(k0, BLK), 256 + 128 * half : 384 + 128 * half] = dk.astype(bf16)
                    dall[g, pl.ds(k0, BLK), 512 + 128 * half : 640 + 128 * half] = dv.astype(bf16)
                return carry

            lax.fori_loop(0, 8 // NB, batch, 0)

        for n in CLASSES:
            pl.when(size == n)(functools.partial(run, n))
        return carry

    lax.fori_loop(0, L // BLK, tile, 0)
    moves[5].wait()
    for g in range(4):
        dall[g, :, :256] = (dqt[256 * g : 256 * g + 256, :].T * 0.125).astype(bf16)
    for c in range(2):
        cols = slice(512 * c, 512 * c + 512)
        acc = gfirst[:, cols].astype(f32)
        for i in range(4):
            acc = acc + nt(dall[i], w[i, cols, :])
        low = acc.astype(bf16)
        gin[0, :, cols] = low
        own[:, cols] = low


def attn_bwd(r, rows, win, place, qkv, ctx, lse, gf_a, gf_b, pk, pv, segk, segq, wo, w, into=None):
    row = lambda i, *_: (r, 0, 0)
    row4 = lambda i, *_: (r, 0, 0, 0)
    all_ = lambda i, *_: (0, 0, 0)
    any_ = pl.BlockSpec(memory_space=pl.ANY)
    extra = [] if into is None else [into]
    return pl.pallas_call(
        functools.partial(attn_bwd_kernel, r),
        grid_spec=pltpu.PrefetchScalarGridSpec(
            num_scalar_prefetch=3,
            grid=(1,),
            in_specs=[
                any_,
                any_,
                pl.BlockSpec((1, 4, 4, L), row4),
                any_,
                any_,
                pl.BlockSpec((4, PRE, 256), all_),
                pl.BlockSpec((4, PRE, 256), all_),
                pl.BlockSpec((1, L, 128), row),
                pl.BlockSpec((1, 1, L), row),
                any_,
                any_,
            ]
            + [any_ for _ in extra],
            out_specs=[
                pl.BlockSpec((1, L, D), lambda i, rows, win, place: (rows[r], 0, 0)),
                pl.BlockSpec((L, D), lambda i, *_: (0, 0)),
                pl.BlockSpec((2, PRE, D), all_),
            ],
            scratch_shapes=[
                pltpu.VMEM((D, L), f32),
                pltpu.VMEM((4, L, 768), bf16),
                pltpu.VMEM((L, D), bf16),
                pltpu.VMEM((L, D), bf16),
                pltpu.VMEM((L, D), bf16),
                pltpu.VMEM((4, L, 768), bf16),
                pltpu.VMEM((4, 8, L), f32),
                pltpu.VMEM((D, D), bf16),
                pltpu.VMEM((4, D, 768), bf16),
                pltpu.SemaphoreType.DMA((6,)),
            ],
        ),
        out_shape=[
            jax.ShapeDtypeStruct((3, L, D), bf16),
            jax.ShapeDtypeStruct((L, D), bf16),
            jax.ShapeDtypeStruct((2, PRE, D), f32),
        ],
        input_output_aliases={14: 0} if extra else {},
        compiler_params=pltpu.CompilerParams(vmem_limit_bytes=60 << 20),
        cost_estimate=pl.CostEstimate(flops=40 * 10**9, bytes_accessed=32 << 20, transcendentals=0),
        name="attn_bwd",
    )(rows, win, place, qkv, ctx, lse, gf_a, gf_b, pk, pv, segk, segq, wo, w, *extra)


HC = 512
TM = 512
EPS = 1e-5


ERF = (0.7978849414895208, 0.03633308441063725, -3.2594747109729314e-05, -5.5306315505082965e-05,
       3.964772884359942e-06, -1.3226625462816106e-07, 1.7562766828961903e-09)


def gelu_parts(v):
    u = v * v
    w = jnp.minimum(u, 31.36)
    p = ERF[6] * w + ERF[5]
    for c in ERF[4::-1]:
        p = p * w + c
    phi = 0.5 * jnp.tanh(v * p) + 0.5
    return v * phi, phi


def norm_stats(z):
    mean = jnp.mean(z, axis=1, keepdims=True)
    c = z - mean
    var = jnp.mean(c * c, axis=1, keepdims=True)
    r = lax.rsqrt(var + EPS)
    return c * r, r


def tokens_kernel(
    pos, ctx, x, cot, wo_h, win_h, wout_h, bo, g1, s1, bi, b2, g2, s2, *rest
):
    out, own, gf, wo, win, wout, xhat, zbuf, low, act, gp, rs, vb, sem = rest[-14:]
    M = TM
    fetch_o = pltpu.make_async_copy(wo_h, wo, sem.at[0])
    fetch_i = [pltpu.make_async_copy(win_h.at[i], win.at[i], sem.at[1 + i]) for i in range(4)]
    fetch_u = [
        pltpu.make_async_copy(wout_h.at[pl.ds(1024 * i, 1024)], wout.at[pl.ds(1024 * i, 1024)], sem.at[5 + i])
        for i in range(4)
    ]
    for c in [fetch_o] + fetch_i + fetch_u:
        c.start()
    fetch_o.wait()

    for c0 in range(0, D, 256):
        cols = slice(c0, c0 + 256)
        zbuf[:, cols] = nn(ctx[...], wo[:, cols]) + x[:, cols].astype(f32)

    n, r = norm_stats(zbuf[...] + bo[...])
    xhat[...] = n
    rs[...] = jnp.broadcast_to(r, (M, 128))
    y = n * g1[...] + s1[...]
    zbuf[...] = y
    low[...] = y.astype(bf16)

    for i in range(8):
        z, c = i // 2, i % 2
        if c == 0:
            fetch_i[z].wait()
        cols = slice(i * HC, i * HC + HC)
        h = nn(low[...], win[z, :, c * HC : c * HC + HC]) + bi[z, :, 768 + c * HC : 768 + c * HC + HC]
        a, phi = gelu_parts(h)
        act[:, cols] = a.astype(bf16)
        gp[:, cols] = phi.astype(bf16)
        vb[:, cols] = h.astype(bf16)

    for c in fetch_u:
        c.wait()
    for c0 in range(0, D, 256):
        cols = slice(c0, c0 + 256)
        zbuf[:, cols] += nn(act[...], wout[:, cols])

    n, r = norm_stats(zbuf[...] + b2[...])
    result = (n * g2[...] + s2[...]).astype(bf16)
    out[...] = result
    own[...] = result
    g = cot[...].astype(f32) * g2[...]
    m1 = jnp.mean(g, axis=1, keepdims=True)
    m2 = jnp.mean(g * n, axis=1, keepdims=True)
    d = (g - m1 - n * m2) * r
    zbuf[...] = d
    low[...] = d.astype(bf16)

    for i in range(8):
        cols = slice(i * HC, i * HC + HC)
        d = nt(low[...], wout[cols, :])
        v = vb[:, cols].astype(f32)
        slope = gp[:, cols].astype(f32) + v * (jnp.exp(-0.5 * v * v) * 0.3989422804014327)
        act[:, cols] = (d * slope).astype(bf16)

    for c0 in range(0, D, 256):
        cols = slice(c0, c0 + 256)
        acc = zbuf[:, cols]
        for z in range(4):
            acc = acc + nt(act[:, 1024 * z : 1024 * z + 1024], win[z, cols, :])
        zbuf[:, cols] = acc

    n = xhat[...]
    g = zbuf[...] * g1[...]
    m1 = jnp.mean(g, axis=1, keepdims=True)
    m2 = jnp.mean(g * n, axis=1, keepdims=True)
    gf[...] = ((g - m1 - n * m2) * rs[:, 0:1]).astype(bf16)


def tokens(pos, ctx, x, cot, wo, win, wout, bo, g1, s1, bi, b2, g2, s2, into=None):
    mine = pl.BlockSpec((None, TM, D), lambda i, pos: (pos[0], pos[2], 0))
    pick = pl.BlockSpec((None, TM, D), lambda i, pos: (pos[1], pos[2], 0))
    tile = pl.BlockSpec((TM, D), lambda i, pos: (0, 0))
    any_ = pl.BlockSpec(memory_space=pl.ANY)
    whole = lambda a: pl.BlockSpec(a.shape, lambda i, pos: (0,) * a.ndim)
    vectors = (bo, g1, s1, bi, b2, g2, s2)
    extra = [] if into is None else [into]
    return pl.pallas_call(
        tokens_kernel,
        grid_spec=pltpu.PrefetchScalarGridSpec(
            num_scalar_prefetch=1,
            grid=(1,),
            in_specs=[mine, pick, pick, any_, any_, any_] + [whole(a) for a in vectors] + [any_ for _ in extra],
            out_specs=[pick, tile, tile],
            scratch_shapes=[
                pltpu.VMEM((D, D), bf16),
                pltpu.VMEM((4, D, D), bf16),
                pltpu.VMEM((4 * D, D), bf16),
                pltpu.VMEM((TM, D), f32),
                pltpu.VMEM((TM, D), f32),
                pltpu.VMEM((TM, D), bf16),
                pltpu.VMEM((TM, 4 * D), bf16),
                pltpu.VMEM((TM, 4 * D), bf16),
                pltpu.VMEM((TM, 128), f32),
                pltpu.VMEM((TM, 4 * D), bf16),
                pltpu.SemaphoreType.DMA((9,)),
            ],
        ),
        out_shape=[
            jax.ShapeDtypeStruct((3, L, D), bf16),
            jax.ShapeDtypeStruct((TM, D), bf16),
            jax.ShapeDtypeStruct((TM, D), bf16),
        ],
        input_output_aliases={14: 0} if extra else {},
        compiler_params=pltpu.CompilerParams(vmem_limit_bytes=60 << 20),
        cost_estimate=pl.CostEstimate(flops=25 * 10**9, bytes_accessed=24 << 20, transcendentals=0),
        name="tokens",
    )(pos, ctx, x, cot, wo, win, wout, *vectors, *extra)


SPAN = 512
KINDS = 10


def front_kernel(
    hid, seg, msk, pk_s, pv_s, bq, bk, bv, bi, wq, wk, wv, wo_s, wi_s, wu_s,
    wqkv, wo, wi, wu, qkv, ctx, lse, pk, pv, vec, segk, segq,
    own0, x, wbuf, qb, vt, cb, pre, xsem, lsem, osem, ssem, rsem,
):
    d = lax.axis_index("dp")
    z = lax.axis_index("prefix")
    core, xx, yy = d % 2, (d // 2) % 2, d // 4
    dc = d + 1 - 2 * core
    dx = d + 2 - 4 * xx
    dy = d + 4 - 8 * yy
    dxy = dx + dy - d
    unique = 2 * (z % 2)
    MESH = pl.DeviceIdType.MESH

    def region(pay, zz, dd, half=None):
        if pay >= 4:
            return (pre, vec)[pay - 4].at[zz]
        if pay == 0:
            n, ref = 128, lambda o, s: wqkv.at[zz, pl.ds(128 * dd + o, s), :]
        elif pay == 1:
            n, ref = 256, lambda o, s: wo.at[pl.ds(256 * zz + o, s), pl.ds(128 * dd, 128)]
        elif pay == 2:
            n, ref = 128, lambda o, s: wi.at[zz, pl.ds(128 * dd + o, s), :]
        else:
            n, ref = 1024, lambda o, s: wu.at[pl.ds(1024 * zz + o, s), pl.ds(128 * dd, 128)]
        return ref(0, n) if half is None else ref(half * (n // 2), n // 2)

    own0[:, 0:256] = wq[...]
    own0[:, 256:512] = wk[...]
    own0[:, 512:768] = wv[...]
    shards = (own0, wo_s, wi_s, wu_s)
    xin = [pltpu.make_async_copy(hid.at[unique], x.at[0], xsem.at[0]), pltpu.make_async_copy(hid.at[1], x.at[1], xsem.at[1])]
    for c in xin:
        c.start()

    bar = pltpu.get_barrier_semaphore()

    def hello(dev):
        pl.semaphore_signal(bar, inc=1, device_id=dev, device_id_type=MESH)

    for dd in (dc, dx, dy):
        hello((dd, z))
    pl.when(z > 0)(lambda: hello((d, z - 1)))
    pl.when(z < 3)(lambda: hello((d, z + 1)))

    pre[z, 0:24, :] = pk_s[...]
    pre[z, 32:56, :] = pv_s[...]
    vec[z, :, 0:256] = bq[...]
    vec[z, :, 256:512] = bk[...]
    vec[z, :, 512:768] = bv[...]
    vec[z, :, 768:] = bi[...]
    for r in range(2):
        own = seg[pl.ds(unique, 1), :] if r == 0 else seg[1:2, :]
        real = msk[pl.ds(unique, 1), :] if r == 0 else msk[1:2, :]
        segq[r] = own.astype(f32)
        keys = jnp.where(real == 1, own, -1).astype(f32)
        segk[r] = jnp.broadcast_to(keys, (128, L)).T

    local = [pltpu.make_async_copy(shards[i], region(i, z, d), lsem.at[i]) for i in range(4)]
    for c in local:
        c.start()
    peers = jnp.where(z > 0, 1, 0) + jnp.where(z < 3, 1, 0)
    pl.semaphore_wait(bar, 3 + peers)

    def copy(kind, pay, zz, dd, half, dev, skind, src=None):
        r = region(pay, zz, dd, half)
        return pltpu.make_async_remote_copy(
            src_ref=r if src is None else src, dst_ref=r, send_sem=ssem.at[pay * 4 + zz, skind], recv_sem=rsem.at[pay * 4 + zz, kind],
            device_id=dev, device_id_type=MESH,
        )

    def block(k):
        second = jnp.where(z == 0, 1, z - 1)
        third = jnp.where(z == 0, 2, jnp.where(z == 3, 1, z + 1))
        last = jnp.where(z <= 1, 3, 0)
        return jnp.where(k == 0, z, jnp.where(k == 1, second, jnp.where(k == 2, third, last)))

    def up(pay, zz, src=None):
        return copy(0, pay, zz, d, None, (d, z + 1), 10, src)

    def down(pay, zz, src=None):
        return copy(0, pay, zz, d, None, (d, z - 1), 0, src)

    def along(pay, h):
        @pl.when(z >= h)
        def _():
            up(pay, z - h).wait_recv()
            pl.when(z < 3)(lambda: up(pay, z - h).start())

        @pl.when(z + h <= 3)
        def _():
            down(pay, z + h).wait_recv()
            pl.when(z > 0)(lambda: down(pay, z + h).start())

    def stage1(pay, k, src=None):
        zz = block(k)
        copy(1, pay, zz, d, None, (dx, z), 1, src).start()
        copy(2, pay, zz, d, None, (dy, z), 2, src).start()
        copy(5, pay, zz, d, None, (dc, z), 5, src).start()

    def stage2(pay, k):
        zz = block(k)
        copy(1, pay, zz, dx, None, (dx, z), 1).wait_recv()
        copy(3, pay, zz, dx, 0, (dy, z), 3).start()
        copy(6, pay, zz, dx, None, (dc, z), 6).start()
        copy(2, pay, zz, dy, None, (dy, z), 2).wait_recv()
        copy(4, pay, zz, dy, 1, (dx, z), 4).start()
        copy(7, pay, zz, dy, None, (dc, z), 7).start()

    def stage3(pay, k):
        zz = block(k)
        copy(3, pay, zz, dxy, 0, (dy, z), 3).wait_recv()
        copy(8, pay, zz, dxy, 0, (dc, z), 8).start()
        copy(4, pay, zz, dxy, 1, (dx, z), 4).wait_recv()
        copy(9, pay, zz, dxy, 1, (dc, z), 9).start()

    def stage4(pay, k):
        zz = block(k)
        o = dc - d
        copy(5, pay, zz, d + o, None, (dc, z), 5).wait_recv()
        copy(6, pay, zz, dx + o, None, (dc, z), 6).wait_recv()
        copy(7, pay, zz, dy + o, None, (dc, z), 7).wait_recv()
        copy(8, pay, zz, dxy + o, 0, (dc, z), 8).wait_recv()
        copy(9, pay, zz, dxy + o, 1, (dc, z), 9).wait_recv()

    def drain(pay, zz):
        pl.when((zz <= z) & (z < 3))(lambda: up(pay, zz).wait_send())
        pl.when((zz >= z) & (z > 0))(lambda: down(pay, zz).wait_send())
        if pay >= 4:
            return
        copy(1, pay, zz, d, None, (dx, z), 1).wait_send()
        copy(2, pay, zz, d, None, (dy, z), 2).wait_send()
        copy(3, pay, zz, dx, 0, (dy, z), 3).wait_send()
        copy(4, pay, zz, dy, 1, (dx, z), 4).wait_send()
        copy(5, pay, zz, d, None, (dc, z), 5).wait_send()
        copy(6, pay, zz, dx, None, (dc, z), 6).wait_send()
        copy(7, pay, zz, dy, None, (dc, z), 7).wait_send()
        copy(8, pay, zz, dxy, 0, (dc, z), 8).wait_send()
        copy(9, pay, zz, dxy, 1, (dc, z), 9).wait_send()

    ffn = (2, 3, 1)
    stage1(0, 0, own0)
    for pay in (0, 4, 5) + ffn:
        src = shards[pay] if pay < 4 else None
        pl.when(z < 3)(functools.partial(lambda p, src: up(p, z, src).start(), pay, src))
        pl.when(z > 0)(functools.partial(lambda p, src: down(p, z, src).start(), pay, src))
    stage1(2, 0, wi_s)
    stage2(0, 0)
    along(0, 1)
    stage1(0, 1)
    for pay in (4, 5):
        along(pay, 1)
    stage3(0, 0)
    stage1(3, 0, wu_s)
    stage1(1, 0, wo_s)
    for pay in (4, 5):
        along(pay, 2)
    along(0, 2)
    for pay in (4, 5):
        along(pay, 3)
    for g in range(4):
        lanes = slice(256 * g, 256 * g + 256)
        for ref, o in ((pk, 0), (pv, 32)):
            parts = [pre[i, o : o + 32, lanes].astype(f32)[:24] for i in range(4)]
            ref[g] = jnp.concatenate(parts, axis=0).astype(bf16)
    for c in xin + local:
        c.wait()

    def outs(zz):
        q = [pltpu.make_async_copy(qb.at[r], qkv.at[r, zz], osem.at[r]) for r in range(2)]
        c = [
            pltpu.make_async_copy(cb.at[r], ctx.at[r, :, pl.ds(pl.multiple_of(256 * zz, 256), 256)], osem.at[2 + r])
            for r in range(2)
        ]
        return q, c

    def project(r, zz):
        y = nn(x[r], wbuf[...]) + vec[zz, :, 0:768]
        qb[r, :, 0:256] = (y[:, :256].astype(bf16) * 0.125).astype(bf16)
        kv = y[:, 256:].astype(bf16)
        qb[r, :, 256:] = kv
        vt[r, :, :L] = kv[:, 256:].T
        vt[r, :, L:] = pv[zz].T

    def attend(t, zz):
        jobs = []
        for tt in (t, L // BLK - 1 - t):
            first = max(0, tt - SPAN // BLK)
            stop = min(L // BLK, tt + SPAN // BLK + 1)
            k = slice(first * BLK, stop * BLK)
            q = slice(tt * BLK, tt * BLK + BLK)
            for r in range(2):
                seen = segk[r, k, :] == segq[r, :, q]
                for p in range(2):
                    lanes = slice(128 * p, 128 * p + 128)
                    q2 = stack_heads(qb[r, q, lanes])
                    s = nt(qb[r, k, 256 + 128 * p : 384 + 128 * p], q2)
                    jobs.append((r, p, q, k, lanes, seen, s, nt(pk[zz, :, lanes], q2)))
        stage = []
        for r, p, q, k, lanes, seen, s, sp in jobs:
            s = jnp.concatenate([jnp.where(seen, s[:, :128], NEG), jnp.where(seen, s[:, 128:], NEG)], axis=1)
            top = jnp.maximum(jnp.max(s, axis=0, keepdims=True), jnp.max(sp, axis=0, keepdims=True))
            stage.append((s, sp, top))
        probs = []
        for s, sp, top in stage:
            e = jnp.exp(s - top)
            ep = jnp.exp(sp - top)
            total = jnp.sum(e, axis=0, keepdims=True) + jnp.sum(ep, axis=0, keepdims=True)
            probs.append((e.astype(bf16), ep.astype(bf16), total, top))
        res = []
        for (r, p, q, k, lanes, _, _, _), (e, ep, total, top) in zip(jobs, probs):
            res.append(nn(vt[r, lanes, k], e) + nn(vt[r, lanes, L : L + PRE], ep))
        for (r, p, q, k, lanes, _, _, _), (e, ep, total, top), o in zip(jobs, probs, res):
            o = o * (1.0 / total)
            o = jnp.concatenate([o[:64, :128], o[64:, 128:]], axis=0)
            cb[r, q, lanes] = o.T.astype(bf16)
            lt = top + jnp.log(total)
            lse[r, zz, 2 * p : 2 * p + 1, q] = lt[:, :128]
            lse[r, zz, 2 * p + 1 : 2 * p + 2, q] = lt[:, 128:]

    def group(s, carry):
        zz = block(s)

        def soon(far, fn, pays):
            @pl.when(s + far <= 3)
            def _():
                for pay in pays:
                    fn(pay, s + far)

        soon(2, stage1, (0,))
        stage4(0, s)
        win = pltpu.make_async_copy(wqkv.at[zz], wbuf, xsem.at[2])
        win.start()
        soon(1, stage2, (0,))

        @pl.when(s > 0)
        def _():
            q, c = outs(block(s - 1))
            for o in q + c:
                o.wait()

        win.wait()
        project(0, zz)
        stage2(2, s)
        soon(1, along, ffn)
        soon(1, stage1, ffn)
        project(1, zz)
        q, c = outs(zz)
        for o in q:
            o.start()
        attend(0, zz)
        stage2(3, s)
        soon(3, along, (0,))
        attend(1, zz)
        stage2(1, s)
        attend(2, zz)
        soon(1, stage3, (0,))

        @pl.when(s > 0)
        def _():
            for pay in ffn:
                stage3(pay, s - 1)

        attend(3, zz)
        for o in c:
            o.start()
        return carry

    lax.fori_loop(0, 4, group, 0)
    for pay in ffn:
        stage3(pay, 3)
    q, c = outs(block(3))
    for o in q + c:
        o.wait()

    def finish(k, carry):
        for pay in (1, 2, 3):
            stage4(pay, k)
        for pay in range(6):
            drain(pay, k)
        return carry

    lax.fori_loop(0, 4, finish, 0)


def front(hid, seg, msk, pk, pv, bq, bk, bv, bi, wq, wk, wv, wo, wi, wu):
    any_ = pl.BlockSpec(memory_space=pl.ANY)
    vmem = pl.BlockSpec(memory_space=pltpu.VMEM)
    shape = jax.ShapeDtypeStruct
    return pl.pallas_call(
        front_kernel,
        in_specs=[any_] + [vmem] * 14,
        out_specs=[any_] * 6 + [vmem] * 6,
        out_shape=[
            shape((4, D, 768), bf16),
            shape((D, D), bf16),
            shape((4, D, D), bf16),
            shape((4 * D, D), bf16),
            shape((2, 4, L, 768), bf16),
            shape((2, L, D), bf16),
            shape((2, 4, 4, L), f32),
            shape((4, PRE, 256), bf16),
            shape((4, PRE, 256), bf16),
            shape((4, 1, 1792), f32),
            shape((2, L, 128), f32),
            shape((2, 1, L), f32),
        ],
        scratch_shapes=[
            pltpu.VMEM((128, 768), bf16),
            pltpu.VMEM((2, L, D), bf16),
            pltpu.VMEM((D, 768), bf16),
            pltpu.VMEM((2, L, 768), bf16),
            pltpu.VMEM((2, 256, L + PRE), bf16),
            pltpu.VMEM((2, L, 256), bf16),
            pltpu.VMEM((4, 64, D), bf16),
            pltpu.SemaphoreType.DMA((3,)),
            pltpu.SemaphoreType.DMA((4,)),
            pltpu.SemaphoreType.DMA((4,)),
            pltpu.SemaphoreType.DMA((24, KINDS + 1)),
            pltpu.SemaphoreType.DMA((24, KINDS)),
        ],
        compiler_params=pltpu.CompilerParams(
            collective_id=0, has_side_effects=True, vmem_limit_bytes=60 << 20
        ),
        name="front",
    )(hid, seg, msk, pk, pv, bq, bk, bv, bi, wq, wk, wv, wo, wi, wu)


def front_plain(rows, hid, seg, msk, pk, pv, bq, bk, bv, bi, wq, wk, wv, wo, wi, wu):
    over = lambda v, axis, at: lax.all_gather(v, axis, axis=at, tiled=True)
    each = lambda v: lax.all_gather(v, "prefix")
    wqkv = each(jnp.concatenate([over(w, "dp", 0) for w in (wq, wk, wv)], axis=1))
    vec = each(jnp.concatenate([bq, bk, bv, bi], axis=1))
    by_group = lambda p: over(p, "prefix", 0).reshape(PRE, 4, 256).transpose(1, 0, 2)
    pk, pv = by_group(pk), by_group(pv)
    segk = jnp.broadcast_to(jnp.where(msk == 1, seg, -1)[rows][:, :, None], (2, L, 128)).astype(f32)
    segq = seg[rows][:, None, :].astype(f32)
    qkv, ctx, lse = attn_fwd(rows, windows(seg[rows]), hid, wqkv, vec[:, :, :768], pk, pv, segk, segq)
    return (
        wqkv, over(over(wo, "dp", 1), "prefix", 0), each(over(wi, "dp", 0)), over(over(wu, "dp", 1), "prefix", 0),
        qkv, ctx, lse, pk, pv, vec, segk, segq,
    )


def total_kernel(uniq, shared, key, value, away, other, mine, half, slots, ssem, rsem):
    d = lax.axis_index("dp")
    z = lax.axis_index("prefix")
    core, chip = d % 2, d // 2
    xx, yy = chip % 2, chip // 2
    dc = d + 1 - 2 * core
    peers = [((d + 2 - 4 * xx), chip + 1 - 2 * xx), ((d + 4 - 8 * yy), chip + 2 - 4 * yy)]
    peers.append((peers[0][0] + peers[1][0] - d, 3 - chip))
    zp = z + 1 - 2 * (z % 2)
    bar = pltpu.get_barrier_semaphore()
    pl.semaphore_signal(bar, inc=1, device_id=(d, zp), device_id_type=pl.DeviceIdType.MESH)
    for dd in (dc, *(p for p, _ in peers)):
        pl.semaphore_signal(bar, inc=1, device_id=(dd, z), device_id_type=pl.DeviceIdType.MESH)
    n = key.shape[0]
    r0 = pl.multiple_of(z * n, 8)
    away[...] = uniq[:, pl.ds(pl.multiple_of(zp * n, 8), n), :]
    pl.semaphore_wait(bar, 5)

    def send(src, dst, i, dd, zz=None):
        return pltpu.make_async_remote_copy(
            src_ref=src, dst_ref=dst, send_sem=ssem.at[i], recv_sem=rsem.at[i],
            device_id=(dd, z if zz is None else zz), device_id_type=pl.DeviceIdType.MESH,
        )

    swap = send(away, other, 6, d, zp)
    swap.start()
    mine[...] = uniq[:, pl.ds(r0, n), :] + shared[:, pl.ds(r0, n), :]
    swap.wait()
    mine[...] += other[...]

    first = send(mine.at[1 - core], half, 0, dc)
    first.start()
    first.wait()
    slots[chip] = mine[core] + half[...]
    copies = [send(slots.at[chip], slots.at[chip], 1 + i, dd) for i, (dd, _) in enumerate(peers)]
    for c in copies:
        c.start()
    for c in copies:
        c.wait()
    total = (slots[0] + slots[1]) + (slots[2] + slots[3])

    @pl.when(core == 0)
    def _():
        key[...] = total
        last = send(key, key, 4, dc)
        last.start()
        last.wait_send()
        send(value, value, 5, dc).wait_recv()

    @pl.when(core == 1)
    def _():
        value[...] = total
        last = send(value, value, 5, dc)
        last.start()
        last.wait_send()
        send(key, key, 4, dc).wait_recv()


def total_grads(uniq, shared):
    n = PRE // 4
    vmem = pl.BlockSpec(memory_space=pltpu.VMEM)
    return pl.pallas_call(
        total_kernel,
        in_specs=[vmem] * 2,
        out_specs=[vmem] * 2,
        out_shape=[jax.ShapeDtypeStruct((n, D), f32)] * 2,
        scratch_shapes=[
            pltpu.VMEM((2, n, D), f32),
            pltpu.VMEM((2, n, D), f32),
            pltpu.VMEM((2, n, D), f32),
            pltpu.VMEM((n, D), f32),
            pltpu.VMEM((4, n, D), f32),
            pltpu.SemaphoreType.DMA((7,)),
            pltpu.SemaphoreType.DMA((7,)),
        ],
        compiler_params=pltpu.CompilerParams(collective_id=1, has_side_effects=True),
        name="total_grads",
    )(uniq, shared)


def body(
    hidden_in, cotangent, segment_ids, key_mask, prefix_keys, prefix_values,
    w_query, b_query, w_key, b_key, w_value, b_value, w_attn_out, b_attn_out, gain_attn, shift_attn,
    w_ffn_in, b_ffn_in, w_ffn_out, b_ffn_out, gain_ffn, shift_ffn,
):
    z = lax.axis_index("prefix")
    side = z % 2
    rows = jnp.stack([2 * side, jnp.ones_like(side)]).astype(jnp.int32)
    line = lambda v: v.reshape(1, -1)
    small = lax.axis_size("dp") == 8 and lax.axis_size("prefix") == 4
    start = front if small else functools.partial(front_plain, rows)
    w_qkv, w_out, w_up, w_down, qkv, ctx, lse, pk, pv, vec, segk, segq = start(
        hidden_in, segment_ids, key_mask, prefix_keys, prefix_values,
        line(b_query), line(b_key), line(b_value), line(b_ffn_in),
        w_query, w_key, w_value, w_attn_out, w_ffn_in, w_ffn_out,
    )
    win = windows(jnp.stack([jnp.where(side == 0, segment_ids[0], segment_ids[2]), segment_ids[1]]))
    weights = (
        w_out, w_up, w_down, line(b_attn_out), line(gain_attn), line(shift_attn),
        vec, line(b_ffn_out), line(gain_ffn), line(shift_ffn),
    )
    pairs = [(i, i + 1 - 2 * (i % 2)) for i in range(lax.axis_size("prefix"))]
    swap = lambda v: lax.ppermute(v, "prefix", pairs)
    tie = lax.optimization_barrier
    tile = lambda *pos, into=None: tokens(
        jnp.stack([jnp.int32(p) for p in pos]), ctx, hidden_in, cotangent, *weights, into=into
    )
    out, out_s, gf_s = tile(1, 1, side)
    gf_s_other = swap(gf_s)
    out, out_a, gf_a = tile(0, rows[0], 0, into=out)
    out, gf_s_other = tie((out, gf_s_other))
    out_s_other = swap(out_s)
    out, out_b, gf_b = tile(0, rows[0], 1, into=out)
    gf_b, out_s_other = tie((gf_b, out_s_other))
    out_a_other, out_b_other = swap(out_a), swap(out_b)
    common = (pk, pv, segk, segq, w_out, w_qkv)
    gin, gin_own, uniq = attn_bwd(0, rows, win, jnp.array([0, 1], jnp.int32), qkv, ctx, lse, gf_a, gf_b, *common)
    gin, out_a_other, out_b_other = tie((gin, out_a_other, out_b_other))
    gin_other = swap(gin_own)
    gin, _, shared = attn_bwd(
        1, rows, win, jnp.stack([side, 1 - side]).astype(jnp.int32), qkv, ctx, lse, gf_s, gf_s_other, *common, into=gin
    )
    put = lambda v, r, row, at: lax.dynamic_update_slice(v, r[None], (row, at, 0))
    other = 2 - rows[0]
    out = put(out, out_s_other, 1, (1 - side) * TM)
    out = put(put(out, out_a_other, other, 0), out_b_other, other, TM)
    if small:
        keys, values = total_grads(uniq, shared)
    else:
        n = PRE // lax.axis_size("prefix")
        theirs = swap(lax.dynamic_slice_in_dim(uniq, (z + 1 - 2 * side) * n, n, 1))
        keys, values = lax.psum(lax.dynamic_slice_in_dim(uniq + shared, z * n, n, 1) + theirs, "dp")
    return out, put(gin, gin_other, other, 0), keys, values


def solution(mesh):
    return jax.shard_map(
        body,
        mesh=mesh,
        in_specs=(
            P("dp", None, None), P("dp", None, None), P("dp", None), P("dp", None),
            P("prefix", None), P("prefix", None),
            P("dp", "prefix"), P("prefix"), P("dp", "prefix"), P("prefix"), P("dp", "prefix"), P("prefix"),
            P("prefix", "dp"), P(), P(), P(),
            P("dp", "prefix"), P("prefix"), P("prefix", "dp"), P(), P(), P(),
        ),
        out_specs=(P("dp", None, None), P("dp", None, None), P("prefix", None), P("prefix", None)),
        check_vma=False,
    )
```

```python
import functools
import jax
import jax.numpy as jnp
from jax import lax
from jax.experimental import pallas as pl
from jax.experimental.pallas import tpu as pltpu
from jax.sharding import PartitionSpec as P

L = 1024
D = 1024
PRE = 96
BLK = 128
NEG = -1e30
CLASSES = (2, 3, 4, 5, 6, 8)
bf16 = jnp.bfloat16
f32 = jnp.float32


def nt(a, b):
    return lax.dot_general(a, b, (((1,), (1,)), ((), ())), preferred_element_type=f32)


def nn(a, b):
    return jnp.dot(a, b, preferred_element_type=f32)


def stack_heads(tile):
    lane = lax.broadcasted_iota(jnp.int32, tile.shape, 1)
    zero = jnp.zeros_like(tile)
    return jnp.concatenate([jnp.where(lane < 64, tile, zero), jnp.where(lane >= 64, tile, zero)], axis=0)


def windows(seg):
    tiles = seg.shape[-1] // BLK
    first = seg[..., ::BLK]
    last = seg[..., BLK - 1 :: BLK]
    start = jnp.sum((seg[..., None, :] < first[..., :, None]).astype(jnp.int32), axis=-1) // BLK
    stop = (jnp.sum((seg[..., None, :] <= last[..., :, None]).astype(jnp.int32), axis=-1) + BLK - 1) // BLK
    need = stop - start
    size = jnp.full_like(need, CLASSES[-1])
    for n in reversed(CLASSES[:-1]):
        size = jnp.where(need <= n, n, size)
    start = jnp.minimum(start, tiles - size)
    return jnp.stack([start, size], axis=-1)


NP = 8


def attn_fwd_kernel(rows, win, x, w, b, pk, pv, segk, segq, qkv, ctx, lse, vt):
    row = pl.program_id(0)
    for g in range(4):
        y = nn(x[0], w[g]) + b[g]
        q = (y[:, :256].astype(bf16) * 0.125).astype(bf16)
        qkv[0, g, :, :256] = q
        kv = y[:, 256:].astype(bf16)
        qkv[0, g, :, 256:] = kv
        vt[256 * g : 256 * g + 256, :L] = kv[:, 256:].T
        vt[256 * g : 256 * g + 256, L:] = pv[g].T

    def tile(t, carry):
        start = win[row, t, 0]
        size = win[row, t, 1]
        q0 = pl.multiple_of(t * BLK, BLK)
        k0 = pl.multiple_of(start * BLK, BLK)

        def run(n):
            W = n * BLK
            mask = segk[0, pl.ds(k0, W), :] == segq[0, :, pl.ds(q0, BLK)]

            def batch(i, carry):
                jobs = []
                for j in range(NP):
                    p = i * NP + j
                    g, half = p // 2, j % 2
                    lanes = slice(128 * half, 128 * half + 128)
                    klanes = slice(256 + 128 * half, 384 + 128 * half)
                    q2 = stack_heads(qkv[0, g, pl.ds(q0, BLK), lanes])
                    jobs.append((p, g, half, nt(qkv[0, g, pl.ds(k0, W), klanes], q2), nt(pk[g, :, lanes], q2)))
                stage = []
                for p, g, half, s, sp in jobs:
                    s = jnp.concatenate([jnp.where(mask, s[:, :128], NEG), jnp.where(mask, s[:, 128:], NEG)], axis=1)
                    top = jnp.maximum(jnp.max(s, axis=0, keepdims=True), jnp.max(sp, axis=0, keepdims=True))
                    stage.append((s, sp, top))
                probs = []
                for s, sp, top in stage:
                    e = jnp.exp(s - top)
                    ep = jnp.exp(sp - top)
                    total = jnp.sum(e, axis=0, keepdims=True) + jnp.sum(ep, axis=0, keepdims=True)
                    probs.append((e.astype(bf16), ep.astype(bf16), total, top))
                outs = []
                for (p, g, half, _, _), (e, ep, total, top) in zip(jobs, probs):
                    r0 = pl.multiple_of(p * 128, 128)
                    outs.append(nn(vt[pl.ds(r0, 128), pl.ds(k0, W)], e) + nn(vt[pl.ds(r0, 128), L : L + PRE], ep))
                for (p, g, half, _, _), (e, ep, total, top), o in zip(jobs, probs, outs):
                    o = o * (1.0 / total)
                    o = jnp.concatenate([o[:64, :128], o[64:, 128:]], axis=0)
                    r0 = pl.multiple_of(p * 128, 128)
                    ctx[0, pl.ds(q0, BLK), pl.ds(r0, 128)] = o.T.astype(bf16)
                    lt = top + jnp.log(total)
                    lse[0, g, 2 * half : 2 * half + 1, pl.ds(q0, BLK)] = lt[:, :128]
                    lse[0, g, 2 * half + 1 : 2 * half + 2, pl.ds(q0, BLK)] = lt[:, 128:]
                return carry

            lax.fori_loop(0, 8 // NP, batch, 0)

        for n in CLASSES:
            pl.when(size == n)(functools.partial(run, n))
        return carry

    lax.fori_loop(0, L // BLK, tile, 0)


def attn_fwd(rows, win, x, w, b, pk, pv, segk, segq):
    R = rows.shape[0]
    row = lambda r, *_: (r, 0, 0)
    all_ = lambda r, *_: (0, 0, 0)
    return pl.pallas_call(
        attn_fwd_kernel,
        grid_spec=pltpu.PrefetchScalarGridSpec(
            num_scalar_prefetch=2,
            grid=(R,),
            in_specs=[
                pl.BlockSpec((1, L, D), lambda r, rows, win: (rows[r], 0, 0)),
                pl.BlockSpec((4, D, 768), all_),
                pl.BlockSpec((4, 1, 768), all_),
                pl.BlockSpec((4, PRE, 256), all_),
                pl.BlockSpec((4, PRE, 256), all_),
                pl.BlockSpec((1, L, 128), row),
                pl.BlockSpec((1, 1, L), row),
            ],
            out_specs=[
                pl.BlockSpec((1, 4, L, 768), lambda r, *_: (r, 0, 0, 0)),
                pl.BlockSpec((1, L, D), row),
                pl.BlockSpec((1, 4, 4, L), lambda r, *_: (r, 0, 0, 0)),
            ],
            scratch_shapes=[pltpu.VMEM((D, L + PRE), bf16)],
        ),
        out_shape=[
            jax.ShapeDtypeStruct((R, 4, L, 768), bf16),
            jax.ShapeDtypeStruct((R, L, D), bf16),
            jax.ShapeDtypeStruct((R, 4, 4, L), f32),
        ],
        compiler_params=pltpu.CompilerParams(vmem_limit_bytes=60 << 20),
        name="attn_fwd",
    )(rows, win, x, w, b, pk, pv, segk, segq)


NB = 4


def attn_bwd_kernel(
    row, parts, info, win, qkv_h, ctx_h, lse, gf_a, pk, pv, segk, segq, wo_h, w_h, *rest
):
    dqt, dall, gfirst, gctx, ctx, qkv, delta, wo, w, sem = rest[-10:]
    if row == 0:
        gin, own, pgrad = rest[-13:-10]
        moves = [(gf_a, gfirst)]
    else:
        gf_s, out_u, out_s = rest[:3]
        gin, out, pgrad, stage, osem = rest[-15:-10]
        half = L // 2
        moves = [
            (gf_a, gfirst.at[pl.ds(pl.multiple_of(info[2] * half, half), half)]),
            (gf_s, gfirst.at[pl.ds(pl.multiple_of(info[3] * half, half), half)]),
        ]
    moves += [(wo_h, wo), (ctx_h.at[row], ctx), (qkv_h.at[row], qkv), (w_h, w)]
    moves = [pltpu.make_async_copy(src, dst, sem.at[i]) for i, (src, dst) in enumerate(moves)]
    for c in moves:
        c.start()
    if row == 1:
        arrived = [
            pltpu.make_async_copy(out_u, stage.at[0:L], osem.at[0]),
            pltpu.make_async_copy(out_s, stage.at[L : L + TM], osem.at[1]),
        ]
        placed = [
            pltpu.make_async_copy(stage.at[0:L], out.at[2 - info[0]], osem.at[2]),
            pltpu.make_async_copy(
                stage.at[L : L + TM], out.at[1, pl.ds(pl.multiple_of(info[3] * TM, TM), TM)], osem.at[3]
            ),
        ]
        for c in arrived:
            c.start()
    for c in moves[:-2]:
        c.wait()
    heads = jnp.zeros((L, 128), f32)
    for i in range(4):
        cols = slice(256 * i, 256 * i + 256)
        part = nt(gfirst[...], wo[cols, :]).astype(bf16)
        gctx[:, cols] = part
        prod = part.astype(f32) * ctx[:, cols].astype(f32)
        high = prod.astype(bf16)
        low = (prod - high.astype(f32)).astype(bf16)
        r = lax.broadcasted_iota(jnp.int32, (256, 128), 0)
        c = lax.broadcasted_iota(jnp.int32, (256, 128), 1)
        pick = jnp.where(r // 64 + 8 * i == c, 1.0, 0.0).astype(bf16)
        heads = heads + nn(high, pick) + nn(low, pick)
    heads = heads.T
    for i in range(4):
        delta[i] = heads[8 * i : 8 * i + 8]
    moves[-2].wait()

    def blocks(jobs, mask, q0, W, first):
        n = jobs[0][3].shape[0]
        stage = []
        for p, g, half, kt, vt in jobs:
            lanes = slice(128 * half, 128 * half + 128)
            k2 = stack_heads(kt)
            qw = qkv[g, pl.ds(q0, W), lanes]
            dow = gctx[pl.ds(q0, W), pl.ds(pl.multiple_of(p * 128, 128), 128)]
            stage.append((k2, qw, dow, nt(k2, qw), nt(stack_heads(vt), dow)))
        probs = []
        for (p, g, half, _, _), (k2, qw, dow, s, dp) in zip(jobs, stage):
            ps, ds = [], []
            for h in range(2):
                r = 2 * half + h
                sh = s[h * n : h * n + n] - lse[0, g, r : r + 1, pl.ds(q0, W)]
                if mask is not None:
                    sh = jnp.where(mask, sh, NEG)
                ph = jnp.exp(sh)
                ps.append(ph.astype(bf16))
                ds.append((ph * (dp[h * n : h * n + n] - delta[g, r : r + 1, pl.ds(q0, W)])).astype(bf16))
            probs.append((jnp.concatenate(ps, axis=0), jnp.concatenate(ds, axis=0)))
        lane = lax.broadcasted_iota(jnp.int32, (n, 128), 1)
        res = []
        for (p, g, half, _, _), (k2, qw, dow, _, _), (pb, db) in zip(jobs, stage, probs):
            dv = nn(pb, dow)
            dk = nn(db, qw)
            res.append((jnp.where(lane < 64, dk[:n], dk[n:]), jnp.where(lane < 64, dv[:n], dv[n:])))
        for (p, g, half, _, _), (k2, _, _, _, _), (pb, db) in zip(jobs, stage, probs):
            part = nn(k2.T, db)
            r0 = pl.multiple_of(p * 128, 128)
            if first:
                dqt[pl.ds(r0, 128), pl.ds(q0, W)] = part
            else:
                dqt[pl.ds(r0, 128), pl.ds(q0, W)] += part
        return res

    def prefix(i, carry):
        jobs = []
        for j in range(NB):
            p = i * NB + j
            g, half = p // 2, j % 2
            lanes = slice(128 * half, 128 * half + 128)
            jobs.append((p, g, half, pk[g, :, lanes], pv[g, :, lanes]))
        total = None
        for c in range(2):
            part = blocks(jobs, None, c * 512, 512, True)
            total = part if total is None else [(a + c_, b + d) for (a, b), (c_, d) in zip(total, part)]
        for (p, g, half, _, _), (dk, dv) in zip(jobs, total):
            cols = pl.ds(pl.multiple_of(p * 128, 128), 128)
            pgrad[0, :, cols] = dk
            pgrad[1, :, cols] = dv
        return carry

    lax.fori_loop(0, 8 // NB, prefix, 0)
    if row == 0:
        r0 = pl.multiple_of(info[4] * parts, 8)
        own[L:] = jnp.concatenate([pgrad[0, pl.ds(r0, parts), :], pgrad[1, pl.ds(r0, parts), :]], axis=0).astype(bf16)
    else:
        for c, d in zip(arrived, placed):
            c.wait()
            d.start()

    def tile(t, carry):
        start = win[row, t, 0]
        size = win[row, 8 + t, 0]
        k0 = pl.multiple_of(t * BLK, BLK)
        q0 = pl.multiple_of(start * BLK, BLK)

        def run(n):
            W = n * BLK
            sk = segk[0, pl.ds(k0, BLK), :]
            sq = segq[0, :, pl.ds(q0, W)]
            mask = jnp.concatenate([sk] * n, axis=1) == sq

            def batch(i, carry):
                jobs = []
                for j in range(NB):
                    p = i * NB + j
                    g, half = p // 2, j % 2
                    kt = qkv[g, pl.ds(k0, BLK), 256 + 128 * half : 384 + 128 * half]
                    vt = qkv[g, pl.ds(k0, BLK), 512 + 128 * half : 640 + 128 * half]
                    jobs.append((p, g, half, kt, vt))
                for (p, g, half, _, _), (dk, dv) in zip(jobs, blocks(jobs, mask, q0, W, False)):
                    dall[g, pl.ds(k0, BLK), 256 + 128 * half : 384 + 128 * half] = dk.astype(bf16)
                    dall[g, pl.ds(k0, BLK), 512 + 128 * half : 640 + 128 * half] = dv.astype(bf16)
                return carry

            lax.fori_loop(0, 8 // NB, batch, 0)

        for n in CLASSES:
            pl.when(size == n)(functools.partial(run, n))
        return carry

    lax.fori_loop(0, L // BLK, tile, 0)
    moves[-1].wait()
    for g in range(4):
        dall[g, :, :256] = (dqt[256 * g : 256 * g + 256, :].T * 0.125).astype(bf16)
    for c in range(2):
        cols = slice(512 * c, 512 * c + 512)
        acc = gfirst[:, cols].astype(f32)
        for i in range(4):
            acc = acc + nt(dall[i], w[i, cols, :])
        low = acc.astype(bf16)
        gin[0, :, cols] = low
        if row == 0:
            own[:L, cols] = low
    if row == 1:
        for c in placed:
            c.wait()


def attn_bwd(r, parts, info, win, qkv, ctx, lse, gf, pk, pv, segk, segq, wo, w, more=()):
    row = lambda i, *_: (r, 0, 0)
    row4 = lambda i, *_: (r, 0, 0, 0)
    all_ = lambda i, *_: (0, 0, 0)
    any_ = pl.BlockSpec(memory_space=pl.ANY)
    shape = jax.ShapeDtypeStruct
    rows = pl.BlockSpec((1, L, D), lambda i, info, win: (info[r], 0, 0))
    grads = pl.BlockSpec((2, PRE, D), all_)
    if r == 0:
        out_specs = [rows, pl.BlockSpec((L + 2 * parts, D), lambda i, *_: (0, 0)), grads]
        out_shape = [shape((3, L, D), bf16), shape((L + 2 * parts, D), bf16), shape((2, PRE, D), f32)]
        scratch = []
    else:
        out_specs = [rows, any_, grads]
        out_shape = [shape((3, L, D), bf16), shape((3, L, D), bf16), shape((2, PRE, D), f32)]
        scratch = [pltpu.VMEM((L + TM, D), bf16), pltpu.SemaphoreType.DMA((4,))]
    return pl.pallas_call(
        functools.partial(attn_bwd_kernel, r, parts),
        grid_spec=pltpu.PrefetchScalarGridSpec(
            num_scalar_prefetch=2,
            grid=(1,),
            in_specs=[
                any_,
                any_,
                pl.BlockSpec((1, 4, 4, L), row4),
                any_,
                pl.BlockSpec((4, PRE, 256), all_),
                pl.BlockSpec((4, PRE, 256), all_),
                pl.BlockSpec((1, L, 128), row),
                pl.BlockSpec((1, 1, L), row),
                any_,
                any_,
            ]
            + [any_ for _ in more],
            out_specs=out_specs,
            scratch_shapes=scratch
            + [
                pltpu.VMEM((D, L), f32),
                pltpu.VMEM((4, L, 768), bf16),
                pltpu.VMEM((L, D), bf16),
                pltpu.VMEM((L, D), bf16),
                pltpu.VMEM((L, D), bf16),
                pltpu.VMEM((4, L, 768), bf16),
                pltpu.VMEM((4, 8, L), f32),
                pltpu.VMEM((D, D), bf16),
                pltpu.VMEM((4, D, 768), bf16),
                pltpu.SemaphoreType.DMA((6,)),
            ],
        ),
        out_shape=out_shape,
        input_output_aliases={15: 0, 16: 1} if more else {},
        compiler_params=pltpu.CompilerParams(vmem_limit_bytes=60 << 20),
        cost_estimate=pl.CostEstimate(flops=40 * 10**9, bytes_accessed=32 << 20, transcendentals=0),
        name="attn_bwd",
    )(info, win, qkv, ctx, lse, gf, pk, pv, segk, segq, wo, w, *more)


HC = 512
TM = 512
EPS = 1e-5


ERF = (0.797881942323396, 0.036345746572412886, -4.589167395636408e-05, -5.002340812775584e-05,
       3.05428266992555e-06, -6.449413176560626e-08)


def gelu_parts(v):
    u = v * v
    w = jnp.minimum(u, 31.36)
    p = ERF[5] * w + ERF[4]
    for c in ERF[3::-1]:
        p = p * w + c
    phi = 0.5 * jnp.tanh(v * p) + 0.5
    return v * phi, phi


def norm_stats(z):
    mean = jnp.mean(z, axis=1, keepdims=True)
    c = z - mean
    var = jnp.mean(c * c, axis=1, keepdims=True)
    r = lax.rsqrt(var + EPS)
    return c * r, r


def tokens_kernel(shared, info, ctx_h, x_h, cot_h, wo_h, win_h, wout_h, bo, g1, s1, bi, b2, g2, s2, *rest):
    out, own, gf, ctx, x, cot, wo, win, wout, xhat, zbuf, low, act, gp, rs, vb, wsem, tsem = rest[-18:]
    tiles = own.shape[0] // TM
    r, row = (1, info[1]) if shared else (0, info[0])
    at = pl.multiple_of(info[2] * TM, TM) if shared else 0
    M = TM
    fetch_o = pltpu.make_async_copy(wo_h, wo, wsem.at[0])
    fetch_i = [pltpu.make_async_copy(win_h.at[i], win.at[i], wsem.at[1 + i]) for i in range(4)]
    fetch_u = [
        pltpu.make_async_copy(wout_h.at[pl.ds(1024 * i, 1024)], wout.at[pl.ds(1024 * i, 1024)], wsem.at[5 + i])
        for i in range(4)
    ]
    part = lambda j: slice(j * TM, j * TM + TM)
    fetch = lambda src, k, dst, j, i: pltpu.make_async_copy(
        src.at[k, pl.ds(at + j * TM, TM)], dst.at[part(j)], tsem.at[4 * j + i]
    )
    fetch_c = [fetch(ctx_h, r, ctx, j, 0) for j in range(tiles)]
    fetch_x = [fetch(x_h, row, x, j, 1) for j in range(tiles)]
    fetch_t = [fetch(cot_h, row, cot, j, 2) for j in range(tiles)]
    result = [
        pltpu.make_async_copy(own.at[part(j)], out.at[row, pl.ds(at + j * TM, TM)], tsem.at[4 * j + 3])
        for j in range(tiles)
    ]
    for c in [fetch_c[0], fetch_o, fetch_x[0]] + fetch_i + [fetch_t[0]] + fetch_u + fetch_c[1:] + fetch_x[1:] + fetch_t[1:]:
        c.start()

    for j in range(tiles):
        at_j = part(j)
        fetch_c[j].wait()
        if j == 0:
            fetch_o.wait()
        fetch_x[j].wait()
        for c0 in range(0, D, 256):
            cols = slice(c0, c0 + 256)
            zbuf[:, cols] = nn(ctx[at_j], wo[:, cols]) + x[at_j, cols].astype(f32)

        n, r_ = norm_stats(zbuf[...] + bo[...])
        xhat[...] = n
        rs[...] = jnp.broadcast_to(r_, (M, 128))
        y = n * g1[...] + s1[...]
        zbuf[...] = y
        low[...] = y.astype(bf16)

        for i in range(8):
            z, c = i // 2, i % 2
            if c == 0 and j == 0:
                fetch_i[z].wait()
            cols = slice(i * HC, i * HC + HC)
            h = nn(low[...], win[z, :, c * HC : c * HC + HC]) + bi[z, :, 768 + c * HC : 768 + c * HC + HC]
            a, phi = gelu_parts(h)
            act[:, cols] = a.astype(bf16)
            gp[:, cols] = phi.astype(bf16)
            vb[:, cols] = h.astype(bf16)

        if j == 0:
            for c in fetch_u:
                c.wait()
        for c0 in range(0, D, 256):
            cols = slice(c0, c0 + 256)
            zbuf[:, cols] += nn(act[...], wout[:, cols])

        fetch_t[j].wait()
        n, r_ = norm_stats(zbuf[...] + b2[...])
        own[at_j] = (n * g2[...] + s2[...]).astype(bf16)
        result[j].start()
        g = cot[at_j].astype(f32) * g2[...]
        m1 = jnp.mean(g, axis=1, keepdims=True)
        m2 = jnp.mean(g * n, axis=1, keepdims=True)
        d = (g - m1 - n * m2) * r_
        zbuf[...] = d
        low[...] = d.astype(bf16)

        for i in range(8):
            cols = slice(i * HC, i * HC + HC)
            d = nt(low[...], wout[cols, :])
            v = vb[:, cols].astype(f32)
            slope = gp[:, cols].astype(f32) + v * (jnp.exp(-0.5 * v * v) * 0.3989422804014327)
            act[:, cols] = (d * slope).astype(bf16)

        for c0 in range(0, D, 256):
            cols = slice(c0, c0 + 256)
            acc = zbuf[:, cols]
            for z in range(4):
                acc = acc + nt(act[:, 1024 * z : 1024 * z + 1024], win[z, cols, :])
            zbuf[:, cols] = acc

        n = xhat[...]
        g = zbuf[...] * g1[...]
        m1 = jnp.mean(g, axis=1, keepdims=True)
        m2 = jnp.mean(g * n, axis=1, keepdims=True)
        gf[at_j] = ((g - m1 - n * m2) * rs[:, 0:1]).astype(bf16)
    for c in result:
        c.wait()


def tokens(shared, info, ctx, x, cot, wo, win, wout, bo, g1, s1, bi, b2, g2, s2, into=None):
    n = TM if shared else L
    any_ = pl.BlockSpec(memory_space=pl.ANY)
    whole = lambda a: pl.BlockSpec(a.shape, lambda i, info: (0,) * a.ndim)
    block = pl.BlockSpec((n, D), lambda i, info: (0, 0))
    vectors = (bo, g1, s1, bi, b2, g2, s2)
    extra = [] if into is None else [into]
    return pl.pallas_call(
        functools.partial(tokens_kernel, shared),
        grid_spec=pltpu.PrefetchScalarGridSpec(
            num_scalar_prefetch=1,
            grid=(1,),
            in_specs=[any_] * 6 + [whole(a) for a in vectors] + [any_ for _ in extra],
            out_specs=[any_, block, block],
            scratch_shapes=[
                pltpu.VMEM((n, D), bf16),
                pltpu.VMEM((n, D), bf16),
                pltpu.VMEM((n, D), bf16),
                pltpu.VMEM((D, D), bf16),
                pltpu.VMEM((4, D, D), bf16),
                pltpu.VMEM((4 * D, D), bf16),
                pltpu.VMEM((TM, D), f32),
                pltpu.VMEM((TM, D), f32),
                pltpu.VMEM((TM, D), bf16),
                pltpu.VMEM((TM, 4 * D), bf16),
                pltpu.VMEM((TM, 4 * D), bf16),
                pltpu.VMEM((TM, 128), f32),
                pltpu.VMEM((TM, 4 * D), bf16),
                pltpu.SemaphoreType.DMA((9,)),
                pltpu.SemaphoreType.DMA((8,)),
            ],
        ),
        out_shape=[
            jax.ShapeDtypeStruct((3, L, D), bf16),
            jax.ShapeDtypeStruct((n, D), bf16),
            jax.ShapeDtypeStruct((n, D), bf16),
        ],
        input_output_aliases={14: 0} if extra else {},
        compiler_params=pltpu.CompilerParams(vmem_limit_bytes=60 << 20),
        cost_estimate=pl.CostEstimate(flops=(n // TM) * 25 * 10**9, bytes_accessed=24 << 20, transcendentals=0),
        name="tokens",
    )(info, ctx, x, cot, wo, win, wout, *vectors, *extra)


SPAN = 512
KINDS = 10


def front_kernel(
    hid, seg, msk, pk_s, pv_s, bq, bk, bv, bi, wq, wk, wv, wo_s, wi_s, wu_s,
    wqkv, wo, wi, wu, qkv, ctx, lse, pk, pv, vec, segk, segq, wins,
    own0, x, wbuf, qb, vt, cb, pre, xsem, lsem, osem, ssem, rsem,
):
    d = lax.axis_index("dp")
    z = lax.axis_index("prefix")
    core, xx, yy = d % 2, (d // 2) % 2, d // 4
    dc = d + 1 - 2 * core
    dx = d + 2 - 4 * xx
    dy = d + 4 - 8 * yy
    dxy = dx + dy - d
    unique = 2 * (z % 2)
    MESH = pl.DeviceIdType.MESH

    def region(pay, zz, dd, half=None):
        if pay in (4, 5):
            return (pre, vec)[pay - 4].at[zz]
        if pay == 0:
            n, ref = 128, lambda o, s: wqkv.at[zz, pl.ds(128 * dd + o, s), :]
        elif pay == 1:
            n, ref = 256, lambda o, s: wo.at[pl.ds(256 * zz + o, s), pl.ds(128 * dd, 128)]
        elif pay == 2:
            n, ref = 128, lambda o, s: wi.at[zz, pl.ds(128 * dd + o, s), :]
        else:
            o0 = 0 if pay == 3 else 512
            n, ref = 512, lambda o, s: wu.at[pl.ds(1024 * zz + o0 + o, s), pl.ds(128 * dd, 128)]
        return ref(0, n) if half is None else ref(half * (n // 2), n // 2)

    def rows_of(zz, c):
        return wu.at[pl.ds(1024 * zz + 512 + 256 * c, 256), :]

    own0[:, 0:256] = wq[...]
    own0[:, 256:512] = wk[...]
    own0[:, 512:768] = wv[...]
    shards = {0: own0, 1: wo_s, 2: wi_s, 3: wu_s.at[0:512], 6: wu_s.at[512:1024]}
    xin = [pltpu.make_async_copy(hid.at[unique], x.at[0], xsem.at[0]), pltpu.make_async_copy(hid.at[1], x.at[1], xsem.at[1])]
    for c in xin:
        c.start()

    bar = pltpu.get_barrier_semaphore()

    def hello(dev):
        pl.semaphore_signal(bar, inc=1, device_id=dev, device_id_type=MESH)

    for dd in (dc, dx, dy):
        hello((dd, z))
    pl.when(z > 0)(lambda: hello((d, z - 1)))
    pl.when(z < 3)(lambda: hello((d, z + 1)))

    pre[z, 0:24, :] = pk_s[...]
    pre[z, 32:56, :] = pv_s[...]
    vec[z, :, 0:256] = bq[...]
    vec[z, :, 256:512] = bk[...]
    vec[z, :, 512:768] = bv[...]
    vec[z, :, 768:] = bi[...]
    for r in range(2):
        own = seg[pl.ds(unique, 1), :] if r == 0 else seg[1:2, :]
        real = msk[pl.ds(unique, 1), :] if r == 0 else msk[1:2, :]
        segq[r] = own.astype(f32)
        keys = jnp.where(real == 1, own, -1).astype(f32)
        segk[r] = jnp.broadcast_to(keys, (128, L)).T
        line = own.astype(f32)
        for t in range(L // BLK):
            first, last = line[:, t * BLK : t * BLK + 1], line[:, t * BLK + BLK - 1 : t * BLK + BLK]
            begin = jnp.floor(jnp.sum(jnp.where(line < first, 1.0, 0.0), axis=1, keepdims=True) / BLK)
            stop = jnp.floor((jnp.sum(jnp.where(line <= last, 1.0, 0.0), axis=1, keepdims=True) + (BLK - 1)) / BLK)
            size = jnp.full_like(begin, float(CLASSES[-1]))
            for n in reversed(CLASSES[:-1]):
                size = jnp.where(stop - begin <= n, float(n), size)
            begin = jnp.minimum(begin, L // BLK - size)
            wins[r, t : t + 1, :] = jnp.broadcast_to(begin, (1, 128)).astype(jnp.int32)
            wins[r, 8 + t : 9 + t, :] = jnp.broadcast_to(size, (1, 128)).astype(jnp.int32)

    local = [pltpu.make_async_copy(src, region(p, z, d), lsem.at[i]) for i, (p, src) in enumerate(shards.items())]
    for c in local:
        c.start()
    peers = jnp.where(z > 0, 1, 0) + jnp.where(z < 3, 1, 0)
    pl.semaphore_wait(bar, 3 + peers)

    def copy(kind, pay, zz, dd, half, dev, skind, src=None):
        r = region(pay, zz, dd, half)
        return pltpu.make_async_remote_copy(
            src_ref=r if src is None else src, dst_ref=r, send_sem=ssem.at[pay * 4 + zz, skind], recv_sem=rsem.at[pay * 4 + zz, kind],
            device_id=dev, device_id_type=MESH,
        )

    def block(k):
        second = jnp.where(z == 0, 1, z - 1)
        third = jnp.where(z == 0, 2, jnp.where(z == 3, 1, z + 1))
        last = jnp.where(z <= 1, 3, 0)
        return jnp.where(k == 0, z, jnp.where(k == 1, second, jnp.where(k == 2, third, last)))

    def up(pay, zz, src=None):
        return copy(0, pay, zz, d, None, (d, z + 1), 10, src)

    def down(pay, zz, src=None):
        return copy(0, pay, zz, d, None, (d, z - 1), 0, src)

    def along(pay, h):
        @pl.when(z >= h)
        def _():
            up(pay, z - h).wait_recv()
            pl.when(z < 3)(lambda: up(pay, z - h).start())

        @pl.when(z + h <= 3)
        def _():
            down(pay, z + h).wait_recv()
            pl.when(z > 0)(lambda: down(pay, z + h).start())

    def stage1(pay, k, src=None):
        zz = block(k)
        copy(1, pay, zz, d, None, (dx, z), 1, src).start()
        copy(2, pay, zz, d, None, (dy, z), 2, src).start()
        copy(5, pay, zz, d, None, (dc, z), 5, src).start()

    def stage2(pay, k):
        zz = block(k)
        copy(1, pay, zz, dx, None, (dx, z), 1).wait_recv()
        copy(3, pay, zz, dx, 0, (dy, z), 3).start()
        copy(6, pay, zz, dx, None, (dc, z), 6).start()
        copy(2, pay, zz, dy, None, (dy, z), 2).wait_recv()
        copy(4, pay, zz, dy, 1, (dx, z), 4).start()
        copy(7, pay, zz, dy, None, (dc, z), 7).start()

    def stage3(pay, k):
        zz = block(k)
        copy(3, pay, zz, dxy, 0, (dy, z), 3).wait_recv()
        copy(8, pay, zz, dxy, 0, (dc, z), 8).start()
        copy(4, pay, zz, dxy, 1, (dx, z), 4).wait_recv()
        copy(9, pay, zz, dxy, 1, (dc, z), 9).start()

    def stage4(pay, k):
        zz = block(k)
        o = dc - d
        copy(5, pay, zz, d + o, None, (dc, z), 5).wait_recv()
        copy(6, pay, zz, dx + o, None, (dc, z), 6).wait_recv()
        copy(7, pay, zz, dy + o, None, (dc, z), 7).wait_recv()
        copy(8, pay, zz, dxy + o, 0, (dc, z), 8).wait_recv()
        copy(9, pay, zz, dxy + o, 1, (dc, z), 9).wait_recv()

    def haul(zz, dz, kind):
        r = rows_of(zz, core)
        return pltpu.make_async_remote_copy(
            src_ref=r, dst_ref=r, send_sem=ssem.at[24 + zz, kind], recv_sem=rsem.at[24 + zz, 0],
            device_id=(d, z + dz), device_id_type=MESH,
        )

    def share(zz, c):
        r = rows_of(zz, c)
        return pltpu.make_async_remote_copy(
            src_ref=r, dst_ref=r, send_sem=ssem.at[24 + zz, 5], recv_sem=rsem.at[24 + zz, 5],
            device_id=(dc, z), device_id_type=MESH,
        )

    def haul_on(h):
        @pl.when(z >= h)
        def _():
            haul(z - h, 1, 10).wait_recv()
            pl.when(z < 3)(lambda: haul(z - h, 1, 10).start())
            share(z - h, core).start()

        @pl.when(z + h <= 3)
        def _():
            haul(z + h, -1, 0).wait_recv()
            pl.when(z > 0)(lambda: haul(z + h, -1, 0).start())
            share(z + h, core).start()

    def drain(pay, zz):
        if pay != 6:
            pl.when((zz <= z) & (z < 3))(lambda: up(pay, zz).wait_send())
            pl.when((zz >= z) & (z > 0))(lambda: down(pay, zz).wait_send())
        if pay in (4, 5):
            return
        copy(1, pay, zz, d, None, (dx, z), 1).wait_send()
        copy(2, pay, zz, d, None, (dy, z), 2).wait_send()
        copy(3, pay, zz, dx, 0, (dy, z), 3).wait_send()
        copy(4, pay, zz, dy, 1, (dx, z), 4).wait_send()
        copy(5, pay, zz, d, None, (dc, z), 5).wait_send()
        copy(6, pay, zz, dx, None, (dc, z), 6).wait_send()
        copy(7, pay, zz, dy, None, (dc, z), 7).wait_send()
        copy(8, pay, zz, dxy, 0, (dc, z), 8).wait_send()
        copy(9, pay, zz, dxy, 1, (dc, z), 9).wait_send()

    ffn = (2, 3, 1)
    ffn = (2, 3, 1)

    def set_out(pay):
        src = shards.get(pay)
        pl.when(z < 3)(lambda: up(pay, z, src).start())
        pl.when(z > 0)(lambda: down(pay, z, src).start())

    stage1(0, 0, own0)
    for pay in (0, 4, 5):
        set_out(pay)
    stage2(0, 0)
    for pay in (4, 5, 0):
        along(pay, 1)
    stage1(0, 1)
    stage3(0, 0)
    for pay in (4, 5):
        along(pay, 2)
    for pay in ffn:
        set_out(pay)
    for pay in (4, 5):
        along(pay, 3)
    stage1(2, 0, wi_s)
    for g in range(4):
        lanes = slice(256 * g, 256 * g + 256)
        for ref, o in ((pk, 0), (pv, 32)):
            parts = [pre[i, o : o + 32, lanes].astype(f32)[:24] for i in range(4)]
            ref[g] = jnp.concatenate(parts, axis=0).astype(bf16)
    for c in xin + local:
        c.wait()

    def outs(zz):
        q = [pltpu.make_async_copy(qb.at[r], qkv.at[r, zz], osem.at[r]) for r in range(2)]
        c = [
            pltpu.make_async_copy(cb.at[r], ctx.at[r, :, pl.ds(pl.multiple_of(256 * zz, 256), 256)], osem.at[2 + r])
            for r in range(2)
        ]
        return q, c

    def project(r, zz):
        y = nn(x[r], wbuf[...]) + vec[zz, :, 0:768]
        qb[r, :, 0:256] = (y[:, :256].astype(bf16) * 0.125).astype(bf16)
        kv = y[:, 256:].astype(bf16)
        qb[r, :, 256:] = kv
        vt[r, :, :L] = kv[:, 256:].T
        vt[r, :, L:] = pv[zz].T

    def attend(t, zz):
        jobs = []
        for tt in (t, L // BLK - 1 - t):
            first = max(0, tt - SPAN // BLK)
            stop = min(L // BLK, tt + SPAN // BLK + 1)
            k = slice(first * BLK, stop * BLK)
            q = slice(tt * BLK, tt * BLK + BLK)
            for r in range(2):
                seen = segk[r, k, :] == segq[r, :, q]
                for p in range(2):
                    lanes = slice(128 * p, 128 * p + 128)
                    q2 = stack_heads(qb[r, q, lanes])
                    s = nt(qb[r, k, 256 + 128 * p : 384 + 128 * p], q2)
                    jobs.append((r, p, q, k, lanes, seen, s, nt(pk[zz, :, lanes], q2)))
        stage = []
        for r, p, q, k, lanes, seen, s, sp in jobs:
            s = jnp.concatenate([jnp.where(seen, s[:, :128], NEG), jnp.where(seen, s[:, 128:], NEG)], axis=1)
            top = jnp.maximum(jnp.max(s, axis=0, keepdims=True), jnp.max(sp, axis=0, keepdims=True))
            stage.append((s, sp, top))
        probs = []
        for s, sp, top in stage:
            e = jnp.exp(s - top)
            ep = jnp.exp(sp - top)
            total = jnp.sum(e, axis=0, keepdims=True) + jnp.sum(ep, axis=0, keepdims=True)
            probs.append((e.astype(bf16), ep.astype(bf16), total, top))
        res = []
        for (r, p, q, k, lanes, _, _, _), (e, ep, total, top) in zip(jobs, probs):
            res.append(nn(vt[r, lanes, k], e) + nn(vt[r, lanes, L : L + PRE], ep))
        for (r, p, q, k, lanes, _, _, _), (e, ep, total, top), o in zip(jobs, probs, res):
            o = o * (1.0 / total)
            o = jnp.concatenate([o[:64, :128], o[64:, 128:]], axis=0)
            cb[r, q, lanes] = o.T.astype(bf16)
            lt = top + jnp.log(total)
            lse[r, zz, 2 * p : 2 * p + 1, q] = lt[:, :128]
            lse[r, zz, 2 * p + 1 : 2 * p + 2, q] = lt[:, 128:]

    plan = {
        (0, 0): [("z", 0, 2), (1, 0, 2)],
        (0, 1): [(2, 0, 1)],
        (0, 2): [("z", 0, 3), (1, 0, 3)],
        (0, 3): [(3, 0, 1), (2, 0, 2), (1, 3, 0)],
        (0, 4): [(1, 6, 0), (1, 1, 0)],
        (0, 5): [(2, 0, 3)],
        (1, 0): [(3, 0, 2), ("z", 2, 1), ("z", 3, 1), ("z", 1, 1), (1, 2, 1)],
        (1, 1): [(2, 2, 0), (1, 3, 1)],
        (1, 2): [(3, 0, 3), (1, 1, 1)],
        (1, 3): [(2, 3, 0), (2, 6, 0)],
        (1, 4): [(2, 1, 0)],
        (1, 5): [("z", 2, 2), ("z", 3, 2), ("z", 1, 2), (1, 2, 2), (1, 3, 2)],
        (2, 0): [(3, 2, 0), (3, 3, 0), (3, 6, 0)],
        (2, 1): [(2, 2, 1), (1, 1, 2), ("h", 6, 0)],
        (2, 2): [(2, 3, 1), (3, 1, 0)],
        (2, 3): [(2, 1, 1)],
        (2, 4): [("z", 2, 3), ("z", 3, 3), ("z", 1, 3), (1, 2, 3), (1, 3, 3), (1, 1, 3)],
        (2, 5): [(3, 2, 1), (3, 3, 1)],
        (3, 0): [("h", 6, 1), (2, 2, 2), (3, 1, 1)],
        (3, 1): [(2, 3, 2)],
        (3, 2): [(2, 1, 2)],
        (3, 3): [("h", 6, 2), (3, 2, 2)],
        (3, 4): [(2, 2, 3)],
        (3, 5): [(3, 3, 2), (3, 1, 2)],
        (4, 0): [(2, 3, 3), (2, 1, 3), ("h", 6, 3), (3, 2, 3), (3, 3, 3), (3, 1, 3)],
    }

    def act(what, pay, k):
        if what == "z":
            along(pay, k)
        elif what == "h" and k == 0:
            stage4(6, 0)
            pl.when(z < 3)(lambda: haul(z, 1, 10).start())
            pl.when(z > 0)(lambda: haul(z, -1, 0).start())
        elif what == "h":
            haul_on(k)
        elif what == 1:
            stage1(pay, k, shards[pay] if k == 0 else None)
        else:
            (stage2, stage3)[what - 2](pay, k)

    def group(s, carry):
        zz = block(s)

        def pump(slot):
            for i in range(4):

                @pl.when(s == i)
                def _():
                    for step in plan[i, slot]:
                        act(*step)

        stage4(0, s)
        win = pltpu.make_async_copy(wqkv.at[zz], wbuf, xsem.at[2])
        win.start()

        @pl.when(s > 0)
        def _():
            q, c = outs(block(s - 1))
            for o in q + c:
                o.wait()

        win.wait()
        project(0, zz)
        pump(0)
        project(1, zz)
        q, c = outs(zz)
        for o in q:
            o.start()
        pump(1)
        for t in range(4):
            attend(t, zz)
            pump(2 + t)
        for o in c:
            o.start()
        return carry

    lax.fori_loop(0, 4, group, 0)
    for step in plan[4, 0]:
        act(*step)
    q, c = outs(block(3))
    for o in q + c:
        o.wait()

    def finish(k, done):
        for pay in (1, 2, 3):
            stage4(pay, k)
        for pay in range(6):
            drain(pay, k)

        @pl.when(k == z)
        def _():
            drain(6, k)

        @pl.when(k != z)
        def _():
            share(k, 1 - core).wait_recv()
            share(k, core).wait_send()

        pl.when((k <= z) & (z < 3))(lambda: haul(k, 1, 10).wait_send())
        pl.when((k >= z) & (z > 0))(lambda: haul(k, -1, 0).wait_send())
        return done

    lax.fori_loop(0, 4, finish, 0)


def front(hid, seg, msk, pk, pv, bq, bk, bv, bi, wq, wk, wv, wo, wi, wu):
    any_ = pl.BlockSpec(memory_space=pl.ANY)
    vmem = pl.BlockSpec(memory_space=pltpu.VMEM)
    shape = jax.ShapeDtypeStruct
    return pl.pallas_call(
        front_kernel,
        in_specs=[any_] + [vmem] * 14,
        out_specs=[any_] * 6 + [vmem] * 7,
        out_shape=[
            shape((4, D, 768), bf16),
            shape((D, D), bf16),
            shape((4, D, D), bf16),
            shape((4 * D, D), bf16),
            shape((2, 4, L, 768), bf16),
            shape((2, L, D), bf16),
            shape((2, 4, 4, L), f32),
            shape((4, PRE, 256), bf16),
            shape((4, PRE, 256), bf16),
            shape((4, 1, 1792), f32),
            shape((2, L, 128), f32),
            shape((2, 1, L), f32),
            shape((2, 16, 128), jnp.int32),
        ],
        scratch_shapes=[
            pltpu.VMEM((128, 768), bf16),
            pltpu.VMEM((2, L, D), bf16),
            pltpu.VMEM((D, 768), bf16),
            pltpu.VMEM((2, L, 768), bf16),
            pltpu.VMEM((2, 256, L + PRE), bf16),
            pltpu.VMEM((2, L, 256), bf16),
            pltpu.VMEM((4, 64, D), bf16),
            pltpu.SemaphoreType.DMA((3,)),
            pltpu.SemaphoreType.DMA((5,)),
            pltpu.SemaphoreType.DMA((4,)),
            pltpu.SemaphoreType.DMA((28, KINDS + 1)),
            pltpu.SemaphoreType.DMA((28, KINDS)),
        ],
        compiler_params=pltpu.CompilerParams(
            collective_id=0, has_side_effects=True, vmem_limit_bytes=60 << 20
        ),
        name="front",
    )(hid, seg, msk, pk, pv, bq, bk, bv, bi, wq, wk, wv, wo, wi, wu)


def front_plain(rows, hid, seg, msk, pk, pv, bq, bk, bv, bi, wq, wk, wv, wo, wi, wu):
    over = lambda v, axis, at: lax.all_gather(v, axis, axis=at, tiled=True)
    each = lambda v: lax.all_gather(v, "prefix")
    wqkv = each(jnp.concatenate([over(w, "dp", 0) for w in (wq, wk, wv)], axis=1))
    vec = each(jnp.concatenate([bq, bk, bv, bi], axis=1))
    by_group = lambda p: over(p, "prefix", 0).reshape(PRE, 4, 256).transpose(1, 0, 2)
    pk, pv = by_group(pk), by_group(pv)
    segk = jnp.broadcast_to(jnp.where(msk == 1, seg, -1)[rows][:, :, None], (2, L, 128)).astype(f32)
    segq = seg[rows][:, None, :].astype(f32)
    win = windows(seg[rows])
    qkv, ctx, lse = attn_fwd(rows, win, hid, wqkv, vec[:, :, :768], pk, pv, segk, segq)
    wins = jnp.broadcast_to(jnp.concatenate([win[..., 0], win[..., 1]], axis=1)[:, :, None], (2, 16, 128))
    return (
        wqkv, over(over(wo, "dp", 1), "prefix", 0), each(over(wi, "dp", 0)), over(over(wu, "dp", 1), "prefix", 0),
        qkv, ctx, lse, pk, pv, vec, segk, segq, wins,
    )


def total_kernel(uniq, shared, came, key, value, other, mine, half, slots, osem, ssem, rsem):
    d = lax.axis_index("dp")
    z = lax.axis_index("prefix")
    core, chip = d % 2, d // 2
    xx, yy = chip % 2, chip // 2
    dc = d + 1 - 2 * core
    peers = [((d + 2 - 4 * xx), chip + 1 - 2 * xx), ((d + 4 - 8 * yy), chip + 2 - 4 * yy)]
    peers.append((peers[0][0] + peers[1][0] - d, 3 - chip))
    bar = pltpu.get_barrier_semaphore()
    for dd in (dc, *(p for p, _ in peers)):
        pl.semaphore_signal(bar, inc=1, device_id=(dd, z), device_id_type=pl.DeviceIdType.MESH)
    n = key.shape[0]
    r0 = pl.multiple_of(z * n, 8)
    theirs = pltpu.make_async_copy(came.at[pl.ds(L, 2 * n)], other, osem)
    theirs.start()
    theirs.wait()
    add = other[...].astype(f32)
    for i in range(2):
        mine[i] = uniq[i, pl.ds(r0, n), :] + shared[i, pl.ds(r0, n), :] + add[i * n : i * n + n]
    pl.semaphore_wait(bar, 4)

    def send(src, dst, i, dd):
        return pltpu.make_async_remote_copy(
            src_ref=src, dst_ref=dst, send_sem=ssem.at[i], recv_sem=rsem.at[i],
            device_id=(dd, z), device_id_type=pl.DeviceIdType.MESH,
        )

    first = send(mine.at[1 - core], half, 0, dc)
    first.start()
    first.wait()
    slots[chip] = mine[core] + half[...]
    copies = [send(slots.at[chip], slots.at[chip], 1 + i, dd) for i, (dd, _) in enumerate(peers)]
    for c in copies:
        c.start()
    for c in copies:
        c.wait()
    total = (slots[0] + slots[1]) + (slots[2] + slots[3])

    @pl.when(core == 0)
    def _():
        key[...] = total
        last = send(key, key, 4, dc)
        last.start()
        last.wait_send()
        send(value, value, 5, dc).wait_recv()

    @pl.when(core == 1)
    def _():
        value[...] = total
        last = send(value, value, 5, dc)
        last.start()
        last.wait_send()
        send(key, key, 4, dc).wait_recv()


def total_grads(uniq, shared, came):
    n = PRE // 4
    vmem = pl.BlockSpec(memory_space=pltpu.VMEM)
    return pl.pallas_call(
        total_kernel,
        in_specs=[vmem, vmem, pl.BlockSpec(memory_space=pl.ANY)],
        out_specs=[vmem] * 2,
        out_shape=[jax.ShapeDtypeStruct((n, D), f32)] * 2,
        scratch_shapes=[
            pltpu.VMEM((2 * n, D), bf16),
            pltpu.VMEM((2, n, D), f32),
            pltpu.VMEM((n, D), f32),
            pltpu.VMEM((4, n, D), f32),
            pltpu.SemaphoreType.DMA,
            pltpu.SemaphoreType.DMA((6,)),
            pltpu.SemaphoreType.DMA((6,)),
        ],
        compiler_params=pltpu.CompilerParams(collective_id=1, has_side_effects=True),
        name="total_grads",
    )(uniq, shared, came)


def body(
    hidden_in, cotangent, segment_ids, key_mask, prefix_keys, prefix_values,
    w_query, b_query, w_key, b_key, w_value, b_value, w_attn_out, b_attn_out, gain_attn, shift_attn,
    w_ffn_in, b_ffn_in, w_ffn_out, b_ffn_out, gain_ffn, shift_ffn,
):
    z = lax.axis_index("prefix")
    side = z % 2
    info = jnp.stack([2 * side, jnp.ones_like(side), side, 1 - side, z + 1 - 2 * side]).astype(jnp.int32)
    line = lambda v: v.reshape(1, -1)
    small = lax.axis_size("dp") == 8 and lax.axis_size("prefix") == 4
    start = front if small else functools.partial(front_plain, info[:2])
    w_qkv, w_out, w_up, w_down, qkv, ctx, lse, pk, pv, vec, segk, segq, win = start(
        hidden_in, segment_ids, key_mask, prefix_keys, prefix_values,
        line(b_query), line(b_key), line(b_value), line(b_ffn_in),
        w_query, w_key, w_value, w_attn_out, w_ffn_in, w_ffn_out,
    )
    weights = (
        w_out, w_up, w_down, line(b_attn_out), line(gain_attn), line(shift_attn),
        vec, line(b_ffn_out), line(gain_ffn), line(shift_ffn),
    )
    pairs = [(i, i + 1 - 2 * (i % 2)) for i in range(lax.axis_size("prefix"))]
    swap = lambda v: lax.ppermute(v, "prefix", pairs)
    tie = lax.optimization_barrier
    args = (info, ctx, hidden_in, cotangent, *weights)
    out, out_s, gf_s = tokens(True, *args)
    out_s_other, gf_s_other = swap(out_s), swap(gf_s)
    out, out_u, gf_u = tokens(False, *args, into=out)
    out, out_s_other, gf_s_other, gf_u = tie((out, out_s_other, gf_s_other, gf_u))
    out_u_other = swap(out_u)
    parts = PRE // lax.axis_size("prefix")
    common = (pk, pv, segk, segq, w_out, w_qkv)
    gin, gin_own, uniq = attn_bwd(0, parts, info, win, qkv, ctx, lse, gf_u, *common)
    gin, out_u_other = tie((gin, out_u_other))
    came = swap(gin_own)
    gin, out, shared = attn_bwd(
        1, parts, info, win, qkv, ctx, lse, gf_s, *common, more=(gf_s_other, out_u_other, out_s_other, gin, out)
    )
    if small:
        keys, values = total_grads(uniq, shared, came)
    else:
        own = lax.dynamic_slice_in_dim(uniq + shared, z * parts, parts, 1)
        keys, values = lax.psum(own + came[L:].reshape(2, parts, D).astype(f32), "dp")
    gin = lax.dynamic_update_slice(gin, came[None, :L], (2 - info[0], 0, 0))
    return out, gin, keys, values


def solution(mesh):
    return jax.shard_map(
        body,
        mesh=mesh,
        in_specs=(
            P("dp", None, None), P("dp", None, None), P("dp", None), P("dp", None),
            P("prefix", None), P("prefix", None),
            P("dp", "prefix"), P("prefix"), P("dp", "prefix"), P("prefix"), P("dp", "prefix"), P("prefix"),
            P("prefix", "dp"), P(), P(), P(),
            P("dp", "prefix"), P("prefix"), P("prefix", "dp"), P(), P(), P(),
        ),
        out_specs=(P("dp", None, None), P("dp", None, None), P("prefix", None), P("prefix", None)),
        check_vma=False,
    )
```

```python
import functools
import jax
import jax.numpy as jnp
from jax import lax
from jax.experimental import pallas as pl
from jax.experimental.pallas import tpu as pltpu
from jax.sharding import PartitionSpec as P

L = 1024
D = 1024
PRE = 96
BLK = 128
NEG = -1e30
CLASSES = (2, 3, 4, 5, 6, 8)
bf16 = jnp.bfloat16
f32 = jnp.float32


def nt(a, b):
    return lax.dot_general(a, b, (((1,), (1,)), ((), ())), preferred_element_type=f32)


def nn(a, b):
    return jnp.dot(a, b, preferred_element_type=f32)


def stack_heads(tile):
    lane = lax.broadcasted_iota(jnp.int32, tile.shape, 1)
    zero = jnp.zeros_like(tile)
    return jnp.concatenate([jnp.where(lane < 64, tile, zero), jnp.where(lane >= 64, tile, zero)], axis=0)


def windows(seg):
    tiles = seg.shape[-1] // BLK
    first = seg[..., ::BLK]
    last = seg[..., BLK - 1 :: BLK]
    start = jnp.sum((seg[..., None, :] < first[..., :, None]).astype(jnp.int32), axis=-1) // BLK
    stop = (jnp.sum((seg[..., None, :] <= last[..., :, None]).astype(jnp.int32), axis=-1) + BLK - 1) // BLK
    need = stop - start
    size = jnp.full_like(need, CLASSES[-1])
    for n in reversed(CLASSES[:-1]):
        size = jnp.where(need <= n, n, size)
    start = jnp.minimum(start, tiles - size)
    return jnp.stack([start, size], axis=-1)


NP = 8


def attn_fwd_kernel(rows, win, x, w, b, pk, pv, segk, segq, qkv, ctx, lse, vt):
    row = pl.program_id(0)
    for g in range(4):
        y = nn(x[0], w[g]) + b[g]
        q = (y[:, :256].astype(bf16) * 0.125).astype(bf16)
        qkv[0, g, :, :256] = q
        kv = y[:, 256:].astype(bf16)
        qkv[0, g, :, 256:] = kv
        vt[256 * g : 256 * g + 256, :L] = kv[:, 256:].T
        vt[256 * g : 256 * g + 256, L:] = pv[g].T

    def tile(t, carry):
        start = win[row, t, 0]
        size = win[row, t, 1]
        q0 = pl.multiple_of(t * BLK, BLK)
        k0 = pl.multiple_of(start * BLK, BLK)

        def run(n):
            W = n * BLK
            mask = segk[0, pl.ds(k0, W), :] == segq[0, :, pl.ds(q0, BLK)]

            def batch(i, carry):
                jobs = []
                for j in range(NP):
                    p = i * NP + j
                    g, half = p // 2, j % 2
                    lanes = slice(128 * half, 128 * half + 128)
                    klanes = slice(256 + 128 * half, 384 + 128 * half)
                    q2 = stack_heads(qkv[0, g, pl.ds(q0, BLK), lanes])
                    jobs.append((p, g, half, nt(qkv[0, g, pl.ds(k0, W), klanes], q2), nt(pk[g, :, lanes], q2)))
                stage = []
                for p, g, half, s, sp in jobs:
                    s = jnp.concatenate([jnp.where(mask, s[:, :128], NEG), jnp.where(mask, s[:, 128:], NEG)], axis=1)
                    top = jnp.maximum(jnp.max(s, axis=0, keepdims=True), jnp.max(sp, axis=0, keepdims=True))
                    stage.append((s, sp, top))
                probs = []
                for s, sp, top in stage:
                    e = jnp.exp(s - top)
                    ep = jnp.exp(sp - top)
                    total = jnp.sum(e, axis=0, keepdims=True) + jnp.sum(ep, axis=0, keepdims=True)
                    probs.append((e.astype(bf16), ep.astype(bf16), total, top))
                outs = []
                for (p, g, half, _, _), (e, ep, total, top) in zip(jobs, probs):
                    r0 = pl.multiple_of(p * 128, 128)
                    outs.append(nn(vt[pl.ds(r0, 128), pl.ds(k0, W)], e) + nn(vt[pl.ds(r0, 128), L : L + PRE], ep))
                for (p, g, half, _, _), (e, ep, total, top), o in zip(jobs, probs, outs):
                    o = o * (1.0 / total)
                    o = jnp.concatenate([o[:64, :128], o[64:, 128:]], axis=0)
                    r0 = pl.multiple_of(p * 128, 128)
                    ctx[0, pl.ds(q0, BLK), pl.ds(r0, 128)] = o.T.astype(bf16)
                    lt = top + jnp.log(total)
                    lse[0, g, 2 * half : 2 * half + 1, pl.ds(q0, BLK)] = lt[:, :128]
                    lse[0, g, 2 * half + 1 : 2 * half + 2, pl.ds(q0, BLK)] = lt[:, 128:]
                return carry

            lax.fori_loop(0, 8 // NP, batch, 0)

        for n in CLASSES:
            pl.when(size == n)(functools.partial(run, n))
        return carry

    lax.fori_loop(0, L // BLK, tile, 0)


def attn_fwd(rows, win, x, w, b, pk, pv, segk, segq):
    R = rows.shape[0]
    row = lambda r, *_: (r, 0, 0)
    all_ = lambda r, *_: (0, 0, 0)
    return pl.pallas_call(
        attn_fwd_kernel,
        grid_spec=pltpu.PrefetchScalarGridSpec(
            num_scalar_prefetch=2,
            grid=(R,),
            in_specs=[
                pl.BlockSpec((1, L, D), lambda r, rows, win: (rows[r], 0, 0)),
                pl.BlockSpec((4, D, 768), all_),
                pl.BlockSpec((4, 1, 768), all_),
                pl.BlockSpec((4, PRE, 256), all_),
                pl.BlockSpec((4, PRE, 256), all_),
                pl.BlockSpec((1, L, 128), row),
                pl.BlockSpec((1, 1, L), row),
            ],
            out_specs=[
                pl.BlockSpec((1, 4, L, 768), lambda r, *_: (r, 0, 0, 0)),
                pl.BlockSpec((1, L, D), row),
                pl.BlockSpec((1, 4, 4, L), lambda r, *_: (r, 0, 0, 0)),
            ],
            scratch_shapes=[pltpu.VMEM((D, L + PRE), bf16)],
        ),
        out_shape=[
            jax.ShapeDtypeStruct((R, 4, L, 768), bf16),
            jax.ShapeDtypeStruct((R, L, D), bf16),
            jax.ShapeDtypeStruct((R, 4, 4, L), f32),
        ],
        compiler_params=pltpu.CompilerParams(vmem_limit_bytes=60 << 20),
        name="attn_fwd",
    )(rows, win, x, w, b, pk, pv, segk, segq)


NB = 4


def attn_bwd_kernel(
    row, parts, info, win, qkv_h, ctx_h, lse, gf_a, pk, pv, segk, segq, wo_h, w_h, *rest
):
    dqt, dall, gfirst, gctx, ctx, qkv, delta, wo, w, sem = rest[-10:]
    if row == 0:
        gin, own, pgrad = rest[-13:-10]
        moves = [(gf_a, gfirst)]
    else:
        gf_s, out_u, out_s = rest[:3]
        gin, out, pgrad, stage, osem = rest[-15:-10]
        half = L // 2
        moves = [
            (gf_a, gfirst.at[pl.ds(pl.multiple_of(info[2] * half, half), half)]),
            (gf_s, gfirst.at[pl.ds(pl.multiple_of(info[3] * half, half), half)]),
        ]
    moves += [(wo_h, wo), (ctx_h.at[row], ctx), (qkv_h.at[row], qkv), (w_h, w)]
    moves = [pltpu.make_async_copy(src, dst, sem.at[i]) for i, (src, dst) in enumerate(moves)]
    for c in moves:
        c.start()
    if row == 1:
        arrived = [
            pltpu.make_async_copy(out_u, stage.at[0:L], osem.at[0]),
            pltpu.make_async_copy(out_s, stage.at[L : L + TM], osem.at[1]),
        ]
        placed = [
            pltpu.make_async_copy(stage.at[0:L], out.at[2 - info[0]], osem.at[2]),
            pltpu.make_async_copy(
                stage.at[L : L + TM], out.at[1, pl.ds(pl.multiple_of(info[3] * TM, TM), TM)], osem.at[3]
            ),
        ]
        for c in arrived:
            c.start()
    for c in moves[:-2]:
        c.wait()
    heads = jnp.zeros((L, 128), f32)
    for i in range(4):
        cols = slice(256 * i, 256 * i + 256)
        part = nt(gfirst[...], wo[cols, :]).astype(bf16)
        gctx[:, cols] = part
        prod = part.astype(f32) * ctx[:, cols].astype(f32)
        high = prod.astype(bf16)
        low = (prod - high.astype(f32)).astype(bf16)
        r = lax.broadcasted_iota(jnp.int32, (256, 128), 0)
        c = lax.broadcasted_iota(jnp.int32, (256, 128), 1)
        pick = jnp.where(r // 64 + 8 * i == c, 1.0, 0.0).astype(bf16)
        heads = heads + nn(high, pick) + nn(low, pick)
    heads = heads.T
    for i in range(4):
        delta[i] = heads[8 * i : 8 * i + 8]
    moves[-2].wait()

    def blocks(jobs, mask, q0, W, first):
        n = jobs[0][3].shape[0]
        stage = []
        for p, g, half, kt, vt in jobs:
            lanes = slice(128 * half, 128 * half + 128)
            k2 = stack_heads(kt)
            qw = qkv[g, pl.ds(q0, W), lanes]
            dow = gctx[pl.ds(q0, W), pl.ds(pl.multiple_of(p * 128, 128), 128)]
            stage.append((k2, qw, dow, nt(k2, qw), nt(stack_heads(vt), dow)))
        probs = []
        for (p, g, half, _, _), (k2, qw, dow, s, dp) in zip(jobs, stage):
            ps, ds = [], []
            for h in range(2):
                r = 2 * half + h
                sh = s[h * n : h * n + n] - lse[0, g, r : r + 1, pl.ds(q0, W)]
                if mask is not None:
                    sh = jnp.where(mask, sh, NEG)
                ph = jnp.exp(sh)
                ps.append(ph.astype(bf16))
                ds.append((ph * (dp[h * n : h * n + n] - delta[g, r : r + 1, pl.ds(q0, W)])).astype(bf16))
            probs.append((jnp.concatenate(ps, axis=0), jnp.concatenate(ds, axis=0)))
        lane = lax.broadcasted_iota(jnp.int32, (n, 128), 1)
        res = []
        for (p, g, half, _, _), (k2, qw, dow, _, _), (pb, db) in zip(jobs, stage, probs):
            dv = nn(pb, dow)
            dk = nn(db, qw)
            res.append((jnp.where(lane < 64, dk[:n], dk[n:]), jnp.where(lane < 64, dv[:n], dv[n:])))
        for (p, g, half, _, _), (k2, _, _, _, _), (pb, db) in zip(jobs, stage, probs):
            part = nn(k2.T, db)
            r0 = pl.multiple_of(p * 128, 128)
            if first:
                dqt[pl.ds(r0, 128), pl.ds(q0, W)] = part
            else:
                dqt[pl.ds(r0, 128), pl.ds(q0, W)] += part
        return res

    def prefix(i, carry):
        jobs = []
        for j in range(NB):
            p = i * NB + j
            g, half = p // 2, j % 2
            lanes = slice(128 * half, 128 * half + 128)
            jobs.append((p, g, half, pk[g, :, lanes], pv[g, :, lanes]))
        total = None
        for c in range(2):
            part = blocks(jobs, None, c * 512, 512, True)
            total = part if total is None else [(a + c_, b + d) for (a, b), (c_, d) in zip(total, part)]
        for (p, g, half, _, _), (dk, dv) in zip(jobs, total):
            cols = pl.ds(pl.multiple_of(p * 128, 128), 128)
            pgrad[0, :, cols] = dk
            pgrad[1, :, cols] = dv
        return carry

    lax.fori_loop(0, 8 // NB, prefix, 0)
    if row == 0:
        r0 = pl.multiple_of(info[4] * parts, 8)
        own[L:] = jnp.concatenate([pgrad[0, pl.ds(r0, parts), :], pgrad[1, pl.ds(r0, parts), :]], axis=0).astype(bf16)
    else:
        for c, d in zip(arrived, placed):
            c.wait()
            d.start()

    def tile(t, carry):
        start = win[row, t, 0]
        size = win[row, 8 + t, 0]
        k0 = pl.multiple_of(t * BLK, BLK)
        q0 = pl.multiple_of(start * BLK, BLK)

        def run(n):
            W = n * BLK
            sk = segk[0, pl.ds(k0, BLK), :]
            sq = segq[0, :, pl.ds(q0, W)]
            mask = jnp.concatenate([sk] * n, axis=1) == sq

            def batch(i, carry):
                jobs = []
                for j in range(NB):
                    p = i * NB + j
                    g, half = p // 2, j % 2
                    kt = qkv[g, pl.ds(k0, BLK), 256 + 128 * half : 384 + 128 * half]
                    vt = qkv[g, pl.ds(k0, BLK), 512 + 128 * half : 640 + 128 * half]
                    jobs.append((p, g, half, kt, vt))
                for (p, g, half, _, _), (dk, dv) in zip(jobs, blocks(jobs, mask, q0, W, False)):
                    dall[g, pl.ds(k0, BLK), 256 + 128 * half : 384 + 128 * half] = dk.astype(bf16)
                    dall[g, pl.ds(k0, BLK), 512 + 128 * half : 640 + 128 * half] = dv.astype(bf16)
                return carry

            lax.fori_loop(0, 8 // NB, batch, 0)

        for n in CLASSES:
            pl.when(size == n)(functools.partial(run, n))
        return carry

    lax.fori_loop(0, L // BLK, tile, 0)
    moves[-1].wait()
    for g in range(4):
        dall[g, :, :256] = (dqt[256 * g : 256 * g + 256, :].T * 0.125).astype(bf16)
    for c in range(2):
        cols = slice(512 * c, 512 * c + 512)
        acc = gfirst[:, cols].astype(f32)
        for i in range(4):
            acc = acc + nt(dall[i], w[i, cols, :])
        low = acc.astype(bf16)
        gin[0, :, cols] = low
        if row == 0:
            own[:L, cols] = low
    if row == 1:
        for c in placed:
            c.wait()


def attn_bwd(r, parts, info, win, qkv, ctx, lse, gf, pk, pv, segk, segq, wo, w, more=()):
    row = lambda i, *_: (r, 0, 0)
    row4 = lambda i, *_: (r, 0, 0, 0)
    all_ = lambda i, *_: (0, 0, 0)
    any_ = pl.BlockSpec(memory_space=pl.ANY)
    shape = jax.ShapeDtypeStruct
    rows = pl.BlockSpec((1, L, D), lambda i, info, win: (info[r], 0, 0))
    grads = pl.BlockSpec((2, PRE, D), all_)
    if r == 0:
        out_specs = [rows, pl.BlockSpec((L + 2 * parts, D), lambda i, *_: (0, 0)), grads]
        out_shape = [shape((3, L, D), bf16), shape((L + 2 * parts, D), bf16), shape((2, PRE, D), f32)]
        scratch = []
    else:
        out_specs = [rows, any_, grads]
        out_shape = [shape((3, L, D), bf16), shape((3, L, D), bf16), shape((2, PRE, D), f32)]
        scratch = [pltpu.VMEM((L + TM, D), bf16), pltpu.SemaphoreType.DMA((4,))]
    return pl.pallas_call(
        functools.partial(attn_bwd_kernel, r, parts),
        grid_spec=pltpu.PrefetchScalarGridSpec(
            num_scalar_prefetch=2,
            grid=(1,),
            in_specs=[
                any_,
                any_,
                pl.BlockSpec((1, 4, 4, L), row4),
                any_,
                pl.BlockSpec((4, PRE, 256), all_),
                pl.BlockSpec((4, PRE, 256), all_),
                pl.BlockSpec((1, L, 128), row),
                pl.BlockSpec((1, 1, L), row),
                any_,
                any_,
            ]
            + [any_ for _ in more],
            out_specs=out_specs,
            scratch_shapes=scratch
            + [
                pltpu.VMEM((D, L), f32),
                pltpu.VMEM((4, L, 768), bf16),
                pltpu.VMEM((L, D), bf16),
                pltpu.VMEM((L, D), bf16),
                pltpu.VMEM((L, D), bf16),
                pltpu.VMEM((4, L, 768), bf16),
                pltpu.VMEM((4, 8, L), f32),
                pltpu.VMEM((D, D), bf16),
                pltpu.VMEM((4, D, 768), bf16),
                pltpu.SemaphoreType.DMA((6,)),
            ],
        ),
        out_shape=out_shape,
        input_output_aliases={15: 0, 16: 1} if more else {},
        compiler_params=pltpu.CompilerParams(vmem_limit_bytes=60 << 20),
        cost_estimate=pl.CostEstimate(flops=40 * 10**9, bytes_accessed=32 << 20, transcendentals=0),
        name="attn_bwd",
    )(info, win, qkv, ctx, lse, gf, pk, pv, segk, segq, wo, w, *more)


HC = 512
TM = 512
EPS = 1e-5


ERF = (0.797881942323396, 0.036345746572412886, -4.589167395636408e-05, -5.002340812775584e-05,
       3.05428266992555e-06, -6.449413176560626e-08)


def gelu_parts(v):
    u = v * v
    w = jnp.minimum(u, 31.36)
    p = ERF[5] * w + ERF[4]
    for c in ERF[3::-1]:
        p = p * w + c
    phi = 0.5 * jnp.tanh(v * p) + 0.5
    return v * phi, phi


def norm_stats(z):
    mean = jnp.mean(z, axis=1, keepdims=True)
    c = z - mean
    var = jnp.mean(c * c, axis=1, keepdims=True)
    r = lax.rsqrt(var + EPS)
    return c * r, r


def tokens_kernel(shared, info, ctx_h, x_h, cot_h, wo_h, win_h, wout_h, bo, g1, s1, bi, b2, g2, s2, *rest):
    out, own, gf, ctx, x, cot, wo, win, wout, xhat, zbuf, low, act, gp, rs, vb, wsem, tsem = rest[-18:]
    tiles = own.shape[0] // TM
    r, row = (1, info[1]) if shared else (0, info[0])
    at = pl.multiple_of(info[2] * TM, TM) if shared else 0
    M = TM
    fetch_o = pltpu.make_async_copy(wo_h, wo, wsem.at[0])
    fetch_i = [pltpu.make_async_copy(win_h.at[i], win.at[i], wsem.at[1 + i]) for i in range(4)]
    fetch_u = [
        pltpu.make_async_copy(wout_h.at[pl.ds(1024 * i, 1024)], wout.at[pl.ds(1024 * i, 1024)], wsem.at[5 + i])
        for i in range(4)
    ]
    part = lambda j: slice(j * TM, j * TM + TM)
    fetch = lambda src, k, dst, j, i: pltpu.make_async_copy(
        src.at[k, pl.ds(at + j * TM, TM)], dst.at[part(j)], tsem.at[4 * j + i]
    )
    fetch_c = [fetch(ctx_h, r, ctx, j, 0) for j in range(tiles)]
    fetch_x = [fetch(x_h, row, x, j, 1) for j in range(tiles)]
    fetch_t = [fetch(cot_h, row, cot, j, 2) for j in range(tiles)]
    result = [
        pltpu.make_async_copy(own.at[part(j)], out.at[row, pl.ds(at + j * TM, TM)], tsem.at[4 * j + 3])
        for j in range(tiles)
    ]
    for c in [fetch_c[0], fetch_o, fetch_x[0]] + fetch_i + [fetch_t[0]] + fetch_u + fetch_c[1:] + fetch_x[1:] + fetch_t[1:]:
        c.start()

    for j in range(tiles):
        at_j = part(j)
        if j == 0:
            fetch_o.wait()
        fetch_c[j].wait()
        fetch_x[j].wait()
        for c0 in range(0, D, 256):
            cols = slice(c0, c0 + 256)
            zbuf[:, cols] = nn(ctx[at_j], wo[:, cols]) + x[at_j, cols].astype(f32)

        n, r_ = norm_stats(zbuf[...] + bo[...])
        xhat[...] = n
        rs[...] = jnp.broadcast_to(r_, (M, 128))
        y = n * g1[...] + s1[...]
        zbuf[...] = y
        low[...] = y.astype(bf16)

        early = fetch_i if tiles > 1 else fetch_i + fetch_u + fetch_t
        if j == 0:
            for c in early:
                c.wait()
        for i in range(8):
            z, c = i // 2, i % 2
            cols = slice(i * HC, i * HC + HC)
            h = nn(low[...], win[z, :, c * HC : c * HC + HC]) + bi[z, :, 768 + c * HC : 768 + c * HC + HC]
            a, phi = gelu_parts(h)
            act[:, cols] = a.astype(bf16)
            gp[:, cols] = phi.astype(bf16)
            vb[:, cols] = h.astype(bf16)

        if j == 0 and tiles > 1:
            for c in fetch_u:
                c.wait()
        for c0 in range(0, D, 256):
            cols = slice(c0, c0 + 256)
            zbuf[:, cols] += nn(act[...], wout[:, cols])

        if tiles > 1:
            fetch_t[j].wait()
        n, r_ = norm_stats(zbuf[...] + b2[...])
        own[at_j] = (n * g2[...] + s2[...]).astype(bf16)
        result[j].start()
        g = cot[at_j].astype(f32) * g2[...]
        m1 = jnp.mean(g, axis=1, keepdims=True)
        m2 = jnp.mean(g * n, axis=1, keepdims=True)
        d = (g - m1 - n * m2) * r_
        zbuf[...] = d
        low[...] = d.astype(bf16)

        for i in range(8):
            cols = slice(i * HC, i * HC + HC)
            d = nt(low[...], wout[cols, :])
            v = vb[:, cols].astype(f32)
            slope = gp[:, cols].astype(f32) + v * (jnp.exp(-0.5 * v * v) * 0.3989422804014327)
            act[:, cols] = (d * slope).astype(bf16)

        for c0 in range(0, D, 256):
            cols = slice(c0, c0 + 256)
            acc = zbuf[:, cols]
            for z in range(4):
                acc = acc + nt(act[:, 1024 * z : 1024 * z + 1024], win[z, cols, :])
            zbuf[:, cols] = acc

        n = xhat[...]
        g = zbuf[...] * g1[...]
        m1 = jnp.mean(g, axis=1, keepdims=True)
        m2 = jnp.mean(g * n, axis=1, keepdims=True)
        gf[at_j] = ((g - m1 - n * m2) * rs[:, 0:1]).astype(bf16)
    for c in result:
        c.wait()


def tokens(shared, info, ctx, x, cot, wo, win, wout, bo, g1, s1, bi, b2, g2, s2, into=None):
    n = TM if shared else L
    any_ = pl.BlockSpec(memory_space=pl.ANY)
    whole = lambda a: pl.BlockSpec(a.shape, lambda i, info: (0,) * a.ndim)
    block = pl.BlockSpec((n, D), lambda i, info: (0, 0))
    vectors = (bo, g1, s1, bi, b2, g2, s2)
    extra = [] if into is None else [into]
    return pl.pallas_call(
        functools.partial(tokens_kernel, shared),
        grid_spec=pltpu.PrefetchScalarGridSpec(
            num_scalar_prefetch=1,
            grid=(1,),
            in_specs=[any_] * 6 + [whole(a) for a in vectors] + [any_ for _ in extra],
            out_specs=[any_, block, block],
            scratch_shapes=[
                pltpu.VMEM((n, D), bf16),
                pltpu.VMEM((n, D), bf16),
                pltpu.VMEM((n, D), bf16),
                pltpu.VMEM((D, D), bf16),
                pltpu.VMEM((4, D, D), bf16),
                pltpu.VMEM((4 * D, D), bf16),
                pltpu.VMEM((TM, D), f32),
                pltpu.VMEM((TM, D), f32),
                pltpu.VMEM((TM, D), bf16),
                pltpu.VMEM((TM, 4 * D), bf16),
                pltpu.VMEM((TM, 4 * D), bf16),
                pltpu.VMEM((TM, 128), f32),
                pltpu.VMEM((TM, 4 * D), bf16),
                pltpu.SemaphoreType.DMA((9,)),
                pltpu.SemaphoreType.DMA((8,)),
            ],
        ),
        out_shape=[
            jax.ShapeDtypeStruct((3, L, D), bf16),
            jax.ShapeDtypeStruct((n, D), bf16),
            jax.ShapeDtypeStruct((n, D), bf16),
        ],
        input_output_aliases={14: 0} if extra else {},
        compiler_params=pltpu.CompilerParams(vmem_limit_bytes=60 << 20),
        cost_estimate=pl.CostEstimate(flops=(n // TM) * 25 * 10**9, bytes_accessed=24 << 20, transcendentals=0),
        name="tokens",
    )(info, ctx, x, cot, wo, win, wout, *vectors, *extra)


SPAN = 512
KINDS = 10


def front_kernel(
    hid, seg, msk, pk_s, pv_s, bq, bk, bv, bi, wq, wk, wv, wo_s, wi_s, wu_s,
    wqkv, wo, wi, wu, qkv, ctx, lse, pk, pv, vec, segk, segq, wins,
    own0, x, wbuf, qb, vt, cb, pre, xsem, lsem, osem, ssem, rsem,
):
    d = lax.axis_index("dp")
    z = lax.axis_index("prefix")
    core, xx, yy = d % 2, (d // 2) % 2, d // 4
    dc = d + 1 - 2 * core
    dx = d + 2 - 4 * xx
    dy = d + 4 - 8 * yy
    dxy = dx + dy - d
    unique = 2 * (z % 2)
    MESH = pl.DeviceIdType.MESH

    def region(pay, zz, dd, half=None):
        if pay in (4, 5):
            return (pre, vec)[pay - 4].at[zz]
        if pay == 0:
            n, ref = 128, lambda o, s: wqkv.at[zz, pl.ds(128 * dd + o, s), :]
        elif pay == 1:
            n, ref = 256, lambda o, s: wo.at[pl.ds(256 * zz + o, s), pl.ds(128 * dd, 128)]
        elif pay == 2:
            n, ref = 128, lambda o, s: wi.at[zz, pl.ds(128 * dd + o, s), :]
        else:
            o0 = 0 if pay == 3 else 512
            n, ref = 512, lambda o, s: wu.at[pl.ds(1024 * zz + o0 + o, s), pl.ds(128 * dd, 128)]
        return ref(0, n) if half is None else ref(half * (n // 2), n // 2)

    def rows_of(zz, c):
        return wu.at[pl.ds(1024 * zz + 512 + 256 * c, 256), :]

    own0[:, 0:256] = wq[...]
    own0[:, 256:512] = wk[...]
    own0[:, 512:768] = wv[...]
    shards = {0: own0, 1: wo_s, 2: wi_s, 3: wu_s.at[0:512], 6: wu_s.at[512:1024]}
    xin = [pltpu.make_async_copy(hid.at[unique], x.at[0], xsem.at[0]), pltpu.make_async_copy(hid.at[1], x.at[1], xsem.at[1])]
    for c in xin:
        c.start()

    bar = pltpu.get_barrier_semaphore()

    def hello(dev):
        pl.semaphore_signal(bar, inc=1, device_id=dev, device_id_type=MESH)

    for dd in (dc, dx, dy):
        hello((dd, z))
    pl.when(z > 0)(lambda: hello((d, z - 1)))
    pl.when(z < 3)(lambda: hello((d, z + 1)))

    pre[z, 0:24, :] = pk_s[...]
    pre[z, 32:56, :] = pv_s[...]
    vec[z, :, 0:256] = bq[...]
    vec[z, :, 256:512] = bk[...]
    vec[z, :, 512:768] = bv[...]
    vec[z, :, 768:] = bi[...]
    for r in range(2):
        own = seg[pl.ds(unique, 1), :] if r == 0 else seg[1:2, :]
        real = msk[pl.ds(unique, 1), :] if r == 0 else msk[1:2, :]
        segq[r] = own.astype(f32)
        keys = jnp.where(real == 1, own, -1).astype(f32)
        segk[r] = jnp.broadcast_to(keys, (128, L)).T
        line = own.astype(f32)
        for t in range(L // BLK):
            first, last = line[:, t * BLK : t * BLK + 1], line[:, t * BLK + BLK - 1 : t * BLK + BLK]
            begin = jnp.floor(jnp.sum(jnp.where(line < first, 1.0, 0.0), axis=1, keepdims=True) / BLK)
            stop = jnp.floor((jnp.sum(jnp.where(line <= last, 1.0, 0.0), axis=1, keepdims=True) + (BLK - 1)) / BLK)
            size = jnp.full_like(begin, float(CLASSES[-1]))
            for n in reversed(CLASSES[:-1]):
                size = jnp.where(stop - begin <= n, float(n), size)
            begin = jnp.minimum(begin, L // BLK - size)
            wins[r, t : t + 1, :] = jnp.broadcast_to(begin, (1, 128)).astype(jnp.int32)
            wins[r, 8 + t : 9 + t, :] = jnp.broadcast_to(size, (1, 128)).astype(jnp.int32)

    local = [pltpu.make_async_copy(src, region(p, z, d), lsem.at[i]) for i, (p, src) in enumerate(shards.items())]
    for c in local:
        c.start()
    peers = jnp.where(z > 0, 1, 0) + jnp.where(z < 3, 1, 0)
    pl.semaphore_wait(bar, 3 + peers)

    def copy(kind, pay, zz, dd, half, dev, skind, src=None):
        r = region(pay, zz, dd, half)
        return pltpu.make_async_remote_copy(
            src_ref=r if src is None else src, dst_ref=r, send_sem=ssem.at[pay * 4 + zz, skind], recv_sem=rsem.at[pay * 4 + zz, kind],
            device_id=dev, device_id_type=MESH,
        )

    def block(k):
        second = jnp.where(z == 0, 1, z - 1)
        third = jnp.where(z == 0, 2, jnp.where(z == 3, 1, z + 1))
        last = jnp.where(z <= 1, 3, 0)
        return jnp.where(k == 0, z, jnp.where(k == 1, second, jnp.where(k == 2, third, last)))

    def up(pay, zz, src=None):
        return copy(0, pay, zz, d, None, (d, z + 1), 10, src)

    def down(pay, zz, src=None):
        return copy(0, pay, zz, d, None, (d, z - 1), 0, src)

    def along(pay, h):
        @pl.when(z >= h)
        def _():
            up(pay, z - h).wait_recv()
            pl.when(z < 3)(lambda: up(pay, z - h).start())

        @pl.when(z + h <= 3)
        def _():
            down(pay, z + h).wait_recv()
            pl.when(z > 0)(lambda: down(pay, z + h).start())

    def stage1(pay, k, src=None):
        zz = block(k)
        copy(1, pay, zz, d, None, (dx, z), 1, src).start()
        copy(2, pay, zz, d, None, (dy, z), 2, src).start()
        copy(5, pay, zz, d, None, (dc, z), 5, src).start()

    def stage2(pay, k):
        zz = block(k)
        copy(1, pay, zz, dx, None, (dx, z), 1).wait_recv()
        copy(3, pay, zz, dx, 0, (dy, z), 3).start()
        copy(6, pay, zz, dx, None, (dc, z), 6).start()
        copy(2, pay, zz, dy, None, (dy, z), 2).wait_recv()
        copy(4, pay, zz, dy, 1, (dx, z), 4).start()
        copy(7, pay, zz, dy, None, (dc, z), 7).start()

    def stage3(pay, k):
        zz = block(k)
        copy(3, pay, zz, dxy, 0, (dy, z), 3).wait_recv()
        copy(8, pay, zz, dxy, 0, (dc, z), 8).start()
        copy(4, pay, zz, dxy, 1, (dx, z), 4).wait_recv()
        copy(9, pay, zz, dxy, 1, (dc, z), 9).start()

    def stage4(pay, k):
        zz = block(k)
        o = dc - d
        copy(5, pay, zz, d + o, None, (dc, z), 5).wait_recv()
        copy(6, pay, zz, dx + o, None, (dc, z), 6).wait_recv()
        copy(7, pay, zz, dy + o, None, (dc, z), 7).wait_recv()
        copy(8, pay, zz, dxy + o, 0, (dc, z), 8).wait_recv()
        copy(9, pay, zz, dxy + o, 1, (dc, z), 9).wait_recv()

    def haul(zz, dz, kind):
        r = rows_of(zz, core)
        return pltpu.make_async_remote_copy(
            src_ref=r, dst_ref=r, send_sem=ssem.at[24 + zz, kind], recv_sem=rsem.at[24 + zz, 0],
            device_id=(d, z + dz), device_id_type=MESH,
        )

    def share(zz, c):
        r = rows_of(zz, c)
        return pltpu.make_async_remote_copy(
            src_ref=r, dst_ref=r, send_sem=ssem.at[24 + zz, 5], recv_sem=rsem.at[24 + zz, 5],
            device_id=(dc, z), device_id_type=MESH,
        )

    def haul_on(h):
        @pl.when(z >= h)
        def _():
            haul(z - h, 1, 10).wait_recv()
            pl.when(z < 3)(lambda: haul(z - h, 1, 10).start())
            share(z - h, core).start()

        @pl.when(z + h <= 3)
        def _():
            haul(z + h, -1, 0).wait_recv()
            pl.when(z > 0)(lambda: haul(z + h, -1, 0).start())
            share(z + h, core).start()

    def drain(pay, zz):
        if pay != 6:
            pl.when((zz <= z) & (z < 3))(lambda: up(pay, zz).wait_send())
            pl.when((zz >= z) & (z > 0))(lambda: down(pay, zz).wait_send())
        if pay in (4, 5):
            return
        copy(1, pay, zz, d, None, (dx, z), 1).wait_send()
        copy(2, pay, zz, d, None, (dy, z), 2).wait_send()
        copy(3, pay, zz, dx, 0, (dy, z), 3).wait_send()
        copy(4, pay, zz, dy, 1, (dx, z), 4).wait_send()
        copy(5, pay, zz, d, None, (dc, z), 5).wait_send()
        copy(6, pay, zz, dx, None, (dc, z), 6).wait_send()
        copy(7, pay, zz, dy, None, (dc, z), 7).wait_send()
        copy(8, pay, zz, dxy, 0, (dc, z), 8).wait_send()
        copy(9, pay, zz, dxy, 1, (dc, z), 9).wait_send()

    ffn = (2, 3, 1)
    ffn = (2, 3, 1)

    def set_out(pay):
        src = shards.get(pay)
        pl.when(z < 3)(lambda: up(pay, z, src).start())
        pl.when(z > 0)(lambda: down(pay, z, src).start())

    stage1(0, 0, own0)
    for pay in (0, 4, 5):
        set_out(pay)
    stage2(0, 0)
    for pay in (4, 5, 0):
        along(pay, 1)
    stage1(0, 1)
    stage3(0, 0)
    for pay in (4, 5):
        along(pay, 2)
    for pay in ffn:
        set_out(pay)
    for pay in (4, 5):
        along(pay, 3)
    stage1(2, 0, wi_s)
    for g in range(4):
        lanes = slice(256 * g, 256 * g + 256)
        for ref, o in ((pk, 0), (pv, 32)):
            parts = [pre[i, o : o + 32, lanes].astype(f32)[:24] for i in range(4)]
            ref[g] = jnp.concatenate(parts, axis=0).astype(bf16)
    for c in xin + local:
        c.wait()

    def outs(zz):
        q = [pltpu.make_async_copy(qb.at[r], qkv.at[r, zz], osem.at[r]) for r in range(2)]
        c = [
            pltpu.make_async_copy(cb.at[r], ctx.at[r, :, pl.ds(pl.multiple_of(256 * zz, 256), 256)], osem.at[2 + r])
            for r in range(2)
        ]
        return q, c

    def project(r, zz, slot):
        y = nn(x[r], wbuf[slot]) + vec[zz, :, 0:768]
        qb[r, :, 0:256] = (y[:, :256].astype(bf16) * 0.125).astype(bf16)
        kv = y[:, 256:].astype(bf16)
        qb[r, :, 256:] = kv
        vt[r, :, :L] = kv[:, 256:].T
        vt[r, :, L:] = pv[zz].T

    def attend(t, zz):
        jobs = []
        for tt in (t, L // BLK - 1 - t):
            first = max(0, tt - SPAN // BLK)
            stop = min(L // BLK, tt + SPAN // BLK + 1)
            k = slice(first * BLK, stop * BLK)
            q = slice(tt * BLK, tt * BLK + BLK)
            for r in range(2):
                seen = segk[r, k, :] == segq[r, :, q]
                for p in range(2):
                    lanes = slice(128 * p, 128 * p + 128)
                    q2 = stack_heads(qb[r, q, lanes])
                    s = nt(qb[r, k, 256 + 128 * p : 384 + 128 * p], q2)
                    jobs.append((r, p, q, k, lanes, seen, s, nt(pk[zz, :, lanes], q2)))
        stage = []
        for r, p, q, k, lanes, seen, s, sp in jobs:
            s = jnp.concatenate([jnp.where(seen, s[:, :128], NEG), jnp.where(seen, s[:, 128:], NEG)], axis=1)
            top = jnp.maximum(jnp.max(s, axis=0, keepdims=True), jnp.max(sp, axis=0, keepdims=True))
            stage.append((s, sp, top))
        probs = []
        for s, sp, top in stage:
            e = jnp.exp(s - top)
            ep = jnp.exp(sp - top)
            total = jnp.sum(e, axis=0, keepdims=True) + jnp.sum(ep, axis=0, keepdims=True)
            probs.append((e.astype(bf16), ep.astype(bf16), total, top))
        res = []
        for (r, p, q, k, lanes, _, _, _), (e, ep, total, top) in zip(jobs, probs):
            res.append(nn(vt[r, lanes, k], e) + nn(vt[r, lanes, L : L + PRE], ep))
        for (r, p, q, k, lanes, _, _, _), (e, ep, total, top), o in zip(jobs, probs, res):
            o = o * (1.0 / total)
            o = jnp.concatenate([o[:64, :128], o[64:, 128:]], axis=0)
            cb[r, q, lanes] = o.T.astype(bf16)
            lt = top + jnp.log(total)
            lse[r, zz, 2 * p : 2 * p + 1, q] = lt[:, :128]
            lse[r, zz, 2 * p + 1 : 2 * p + 2, q] = lt[:, 128:]

    plan = {
        (0, 0): [("z", 0, 2), (1, 0, 2)],
        (0, 1): [(2, 0, 1)],
        (0, 2): [("z", 0, 3), (1, 0, 3)],
        (0, 3): [(3, 0, 1), (2, 0, 2), (1, 3, 0)],
        (0, 4): [(1, 6, 0), (1, 1, 0)],
        (0, 5): [(2, 0, 3)],
        (1, 0): [(3, 0, 2), ("z", 2, 1), ("z", 3, 1), ("z", 1, 1), (1, 2, 1)],
        (1, 1): [(2, 2, 0), (1, 3, 1)],
        (1, 2): [(3, 0, 3), (1, 1, 1)],
        (1, 3): [(2, 3, 0), (2, 6, 0)],
        (1, 4): [(2, 1, 0)],
        (1, 5): [("z", 2, 2), ("z", 3, 2), ("z", 1, 2), (1, 2, 2), (1, 3, 2)],
        (2, 0): [(3, 2, 0), (3, 3, 0), (3, 6, 0)],
        (2, 1): [(2, 2, 1), (1, 1, 2), ("h", 6, 0)],
        (2, 2): [(2, 3, 1), (3, 1, 0)],
        (2, 3): [(2, 1, 1)],
        (2, 4): [("z", 2, 3), ("z", 3, 3), ("z", 1, 3), (1, 2, 3), (1, 3, 3), (1, 1, 3)],
        (2, 5): [(3, 2, 1), (3, 3, 1)],
        (3, 0): [("h", 6, 1), (2, 2, 2), (3, 1, 1)],
        (3, 1): [(2, 3, 2)],
        (3, 2): [(2, 1, 2)],
        (3, 3): [("h", 6, 2), (3, 2, 2)],
        (3, 4): [(2, 2, 3)],
        (3, 5): [(3, 3, 2), (3, 1, 2)],
        (4, 0): [(2, 3, 3), (2, 1, 3), ("h", 6, 3), (3, 2, 3), (3, 3, 3), (3, 1, 3)],
    }

    def act(what, pay, k):
        if what == "z":
            along(pay, k)
        elif what == "h" and k == 0:
            stage4(6, 0)
            pl.when(z < 3)(lambda: haul(z, 1, 10).start())
            pl.when(z > 0)(lambda: haul(z, -1, 0).start())
        elif what == "h":
            haul_on(k)
        elif what == 1:
            stage1(pay, k, shards[pay] if k == 0 else None)
        else:
            (stage2, stage3)[what - 2](pay, k)

    def group(s, carry):
        zz = block(s)

        def pump(slot):
            for i in range(4):

                @pl.when(s == i)
                def _():
                    for step in plan[i, slot]:
                        act(*step)

        def weights(k):
            return pltpu.make_async_copy(wqkv.at[block(k)], wbuf.at[k % 2], xsem.at[2 + k % 2])

        @pl.when(s == 0)
        def _():
            stage4(0, 0)
            weights(0).start()

        before = outs(block(s - 1))

        @pl.when(s > 0)
        def _():
            for o in before[0]:
                o.wait()

        weights(s).wait()
        project(0, zz, s % 2)
        pump(0)
        project(1, zz, s % 2)
        q, c = outs(zz)
        for o in q:
            o.start()
        pump(1)

        @pl.when(s > 0)
        def _():
            for o in before[1]:
                o.wait()

        for t in range(4):
            attend(t, zz)
            pump(2 + t)
            if t == 2:

                @pl.when(s < 3)
                def _():
                    stage4(0, s + 1)
                    weights(s + 1).start()

        for o in c:
            o.start()
        return carry

    lax.fori_loop(0, 4, group, 0)
    for step in plan[4, 0]:
        act(*step)
    q, c = outs(block(3))
    for o in q + c:
        o.wait()

    def finish(k, done):
        for pay in (1, 2, 3):
            stage4(pay, k)
        for pay in range(6):
            drain(pay, k)

        @pl.when(k == z)
        def _():
            drain(6, k)

        @pl.when(k != z)
        def _():
            share(k, 1 - core).wait_recv()
            share(k, core).wait_send()

        pl.when((k <= z) & (z < 3))(lambda: haul(k, 1, 10).wait_send())
        pl.when((k >= z) & (z > 0))(lambda: haul(k, -1, 0).wait_send())
        return done

    lax.fori_loop(0, 4, finish, 0)


def front(hid, seg, msk, pk, pv, bq, bk, bv, bi, wq, wk, wv, wo, wi, wu):
    any_ = pl.BlockSpec(memory_space=pl.ANY)
    vmem = pl.BlockSpec(memory_space=pltpu.VMEM)
    shape = jax.ShapeDtypeStruct
    return pl.pallas_call(
        front_kernel,
        in_specs=[any_] + [vmem] * 14,
        out_specs=[any_] * 6 + [vmem] * 7,
        out_shape=[
            shape((4, D, 768), bf16),
            shape((D, D), bf16),
            shape((4, D, D), bf16),
            shape((4 * D, D), bf16),
            shape((2, 4, L, 768), bf16),
            shape((2, L, D), bf16),
            shape((2, 4, 4, L), f32),
            shape((4, PRE, 256), bf16),
            shape((4, PRE, 256), bf16),
            shape((4, 1, 1792), f32),
            shape((2, L, 128), f32),
            shape((2, 1, L), f32),
            shape((2, 16, 128), jnp.int32),
        ],
        scratch_shapes=[
            pltpu.VMEM((128, 768), bf16),
            pltpu.VMEM((2, L, D), bf16),
            pltpu.VMEM((2, D, 768), bf16),
            pltpu.VMEM((2, L, 768), bf16),
            pltpu.VMEM((2, 256, L + PRE), bf16),
            pltpu.VMEM((2, L, 256), bf16),
            pltpu.VMEM((4, 64, D), bf16),
            pltpu.SemaphoreType.DMA((4,)),
            pltpu.SemaphoreType.DMA((5,)),
            pltpu.SemaphoreType.DMA((4,)),
            pltpu.SemaphoreType.DMA((28, KINDS + 1)),
            pltpu.SemaphoreType.DMA((28, KINDS)),
        ],
        compiler_params=pltpu.CompilerParams(
            collective_id=0, has_side_effects=True, vmem_limit_bytes=60 << 20
        ),
        name="front",
    )(hid, seg, msk, pk, pv, bq, bk, bv, bi, wq, wk, wv, wo, wi, wu)


def front_plain(rows, hid, seg, msk, pk, pv, bq, bk, bv, bi, wq, wk, wv, wo, wi, wu):
    over = lambda v, axis, at: lax.all_gather(v, axis, axis=at, tiled=True)
    each = lambda v: lax.all_gather(v, "prefix")
    wqkv = each(jnp.concatenate([over(w, "dp", 0) for w in (wq, wk, wv)], axis=1))
    vec = each(jnp.concatenate([bq, bk, bv, bi], axis=1))
    by_group = lambda p: over(p, "prefix", 0).reshape(PRE, 4, 256).transpose(1, 0, 2)
    pk, pv = by_group(pk), by_group(pv)
    segk = jnp.broadcast_to(jnp.where(msk == 1, seg, -1)[rows][:, :, None], (2, L, 128)).astype(f32)
    segq = seg[rows][:, None, :].astype(f32)
    win = windows(seg[rows])
    qkv, ctx, lse = attn_fwd(rows, win, hid, wqkv, vec[:, :, :768], pk, pv, segk, segq)
    wins = jnp.broadcast_to(jnp.concatenate([win[..., 0], win[..., 1]], axis=1)[:, :, None], (2, 16, 128))
    return (
        wqkv, over(over(wo, "dp", 1), "prefix", 0), each(over(wi, "dp", 0)), over(over(wu, "dp", 1), "prefix", 0),
        qkv, ctx, lse, pk, pv, vec, segk, segq, wins,
    )


def total_kernel(uniq, shared, came, key, value, other, mine, half, slots, osem, ssem, rsem):
    d = lax.axis_index("dp")
    z = lax.axis_index("prefix")
    core, chip = d % 2, d // 2
    xx, yy = chip % 2, chip // 2
    dc = d + 1 - 2 * core
    peers = [((d + 2 - 4 * xx), chip + 1 - 2 * xx), ((d + 4 - 8 * yy), chip + 2 - 4 * yy)]
    peers.append((peers[0][0] + peers[1][0] - d, 3 - chip))
    bar = pltpu.get_barrier_semaphore()
    for dd in (dc, *(p for p, _ in peers)):
        pl.semaphore_signal(bar, inc=1, device_id=(dd, z), device_id_type=pl.DeviceIdType.MESH)
    n = key.shape[0]
    r0 = pl.multiple_of(z * n, 8)
    theirs = pltpu.make_async_copy(came.at[pl.ds(L, 2 * n)], other, osem)
    theirs.start()
    theirs.wait()
    add = other[...].astype(f32)
    for i in range(2):
        mine[i] = uniq[i, pl.ds(r0, n), :] + shared[i, pl.ds(r0, n), :] + add[i * n : i * n + n]
    pl.semaphore_wait(bar, 4)

    def send(src, dst, i, dd):
        return pltpu.make_async_remote_copy(
            src_ref=src, dst_ref=dst, send_sem=ssem.at[i], recv_sem=rsem.at[i],
            device_id=(dd, z), device_id_type=pl.DeviceIdType.MESH,
        )

    first = send(mine.at[1 - core], half, 0, dc)
    first.start()
    first.wait()
    slots[chip] = mine[core] + half[...]
    copies = [send(slots.at[chip], slots.at[chip], 1 + i, dd) for i, (dd, _) in enumerate(peers)]
    for c in copies:
        c.start()
    for c in copies:
        c.wait()
    total = (slots[0] + slots[1]) + (slots[2] + slots[3])

    @pl.when(core == 0)
    def _():
        key[...] = total
        last = send(key, key, 4, dc)
        last.start()
        last.wait_send()
        send(value, value, 5, dc).wait_recv()

    @pl.when(core == 1)
    def _():
        value[...] = total
        last = send(value, value, 5, dc)
        last.start()
        last.wait_send()
        send(key, key, 4, dc).wait_recv()


def total_grads(uniq, shared, came):
    n = PRE // 4
    vmem = pl.BlockSpec(memory_space=pltpu.VMEM)
    return pl.pallas_call(
        total_kernel,
        in_specs=[vmem, vmem, pl.BlockSpec(memory_space=pl.ANY)],
        out_specs=[vmem] * 2,
        out_shape=[jax.ShapeDtypeStruct((n, D), f32)] * 2,
        scratch_shapes=[
            pltpu.VMEM((2 * n, D), bf16),
            pltpu.VMEM((2, n, D), f32),
            pltpu.VMEM((n, D), f32),
            pltpu.VMEM((4, n, D), f32),
            pltpu.SemaphoreType.DMA,
            pltpu.SemaphoreType.DMA((6,)),
            pltpu.SemaphoreType.DMA((6,)),
        ],
        compiler_params=pltpu.CompilerParams(collective_id=1, has_side_effects=True),
        name="total_grads",
    )(uniq, shared, came)


def body(
    hidden_in, cotangent, segment_ids, key_mask, prefix_keys, prefix_values,
    w_query, b_query, w_key, b_key, w_value, b_value, w_attn_out, b_attn_out, gain_attn, shift_attn,
    w_ffn_in, b_ffn_in, w_ffn_out, b_ffn_out, gain_ffn, shift_ffn,
):
    z = lax.axis_index("prefix")
    side = z % 2
    info = jnp.stack([2 * side, jnp.ones_like(side), side, 1 - side, z + 1 - 2 * side]).astype(jnp.int32)
    line = lambda v: v.reshape(1, -1)
    small = lax.axis_size("dp") == 8 and lax.axis_size("prefix") == 4
    start = front if small else functools.partial(front_plain, info[:2])
    w_qkv, w_out, w_up, w_down, qkv, ctx, lse, pk, pv, vec, segk, segq, win = start(
        hidden_in, segment_ids, key_mask, prefix_keys, prefix_values,
        line(b_query), line(b_key), line(b_value), line(b_ffn_in),
        w_query, w_key, w_value, w_attn_out, w_ffn_in, w_ffn_out,
    )
    weights = (
        w_out, w_up, w_down, line(b_attn_out), line(gain_attn), line(shift_attn),
        vec, line(b_ffn_out), line(gain_ffn), line(shift_ffn),
    )
    pairs = [(i, i + 1 - 2 * (i % 2)) for i in range(lax.axis_size("prefix"))]
    swap = lambda v: lax.ppermute(v, "prefix", pairs)
    tie = lax.optimization_barrier
    args = (info, ctx, hidden_in, cotangent, *weights)
    out, out_s, gf_s = tokens(True, *args)
    out_s_other, gf_s_other = swap(out_s), swap(gf_s)
    out, out_u, gf_u = tokens(False, *args, into=out)
    out, out_s_other, gf_s_other, gf_u = tie((out, out_s_other, gf_s_other, gf_u))
    out_u_other = swap(out_u)
    parts = PRE // lax.axis_size("prefix")
    common = (pk, pv, segk, segq, w_out, w_qkv)
    gin, gin_own, uniq = attn_bwd(0, parts, info, win, qkv, ctx, lse, gf_u, *common)
    gin, out_u_other = tie((gin, out_u_other))
    came = swap(gin_own)
    gin, out, shared = attn_bwd(
        1, parts, info, win, qkv, ctx, lse, gf_s, *common, more=(gf_s_other, out_u_other, out_s_other, gin, out)
    )
    if small:
        keys, values = total_grads(uniq, shared, came)
    else:
        own = lax.dynamic_slice_in_dim(uniq + shared, z * parts, parts, 1)
        keys, values = lax.psum(own + came[L:].reshape(2, parts, D).astype(f32), "dp")
    gin = lax.dynamic_update_slice(gin, came[None, :L], (2 - info[0], 0, 0))
    return out, gin, keys, values


def solution(mesh):
    return jax.shard_map(
        body,
        mesh=mesh,
        in_specs=(
            P("dp", None, None), P("dp", None, None), P("dp", None), P("dp", None),
            P("prefix", None), P("prefix", None),
            P("dp", "prefix"), P("prefix"), P("dp", "prefix"), P("prefix"), P("dp", "prefix"), P("prefix"),
            P("prefix", "dp"), P(), P(), P(),
            P("dp", "prefix"), P("prefix"), P("prefix", "dp"), P(), P(), P(),
        ),
        out_specs=(P("dp", None, None), P("dp", None, None), P("prefix", None), P("prefix", None)),
        check_vma=False,
    )
```

```python
import functools
import jax
import jax.numpy as jnp
from jax import lax
from jax.experimental import pallas as pl
from jax.experimental.pallas import tpu as pltpu
from jax.sharding import PartitionSpec as P

L = 1024
D = 1024
PRE = 96
BLK = 128
NEG = -1e30
CLASSES = (2, 3, 4, 5, 6, 8)
bf16 = jnp.bfloat16
f32 = jnp.float32


def nt(a, b):
    return lax.dot_general(a, b, (((1,), (1,)), ((), ())), preferred_element_type=f32)


def nn(a, b):
    return jnp.dot(a, b, preferred_element_type=f32)


def stack_heads(tile):
    lane = lax.broadcasted_iota(jnp.int32, tile.shape, 1)
    zero = jnp.zeros_like(tile)
    return jnp.concatenate([jnp.where(lane < 64, tile, zero), jnp.where(lane >= 64, tile, zero)], axis=0)


def windows(seg):
    tiles = seg.shape[-1] // BLK
    first = seg[..., ::BLK]
    last = seg[..., BLK - 1 :: BLK]
    start = jnp.sum((seg[..., None, :] < first[..., :, None]).astype(jnp.int32), axis=-1) // BLK
    stop = (jnp.sum((seg[..., None, :] <= last[..., :, None]).astype(jnp.int32), axis=-1) + BLK - 1) // BLK
    need = stop - start
    size = jnp.full_like(need, CLASSES[-1])
    for n in reversed(CLASSES[:-1]):
        size = jnp.where(need <= n, n, size)
    start = jnp.minimum(start, tiles - size)
    return jnp.stack([start, size], axis=-1)


NP = 8


def attn_fwd_kernel(rows, win, x, w, b, pk, pv, segk, segq, qkv, ctx, lse, vt):
    row = pl.program_id(0)
    for g in range(4):
        y = nn(x[0], w[g]) + b[g]
        q = (y[:, :256].astype(bf16) * 0.125).astype(bf16)
        qkv[0, g, :, :256] = q
        kv = y[:, 256:].astype(bf16)
        qkv[0, g, :, 256:] = kv
        vt[256 * g : 256 * g + 256, :L] = kv[:, 256:].T
        vt[256 * g : 256 * g + 256, L:] = pv[g].T

    def tile(t, carry):
        start = win[row, t, 0]
        size = win[row, t, 1]
        q0 = pl.multiple_of(t * BLK, BLK)
        k0 = pl.multiple_of(start * BLK, BLK)

        def run(n):
            W = n * BLK
            mask = segk[0, pl.ds(k0, W), :] == segq[0, :, pl.ds(q0, BLK)]

            def batch(i, carry):
                jobs = []
                for j in range(NP):
                    p = i * NP + j
                    g, half = p // 2, j % 2
                    lanes = slice(128 * half, 128 * half + 128)
                    klanes = slice(256 + 128 * half, 384 + 128 * half)
                    q2 = stack_heads(qkv[0, g, pl.ds(q0, BLK), lanes])
                    jobs.append((p, g, half, nt(qkv[0, g, pl.ds(k0, W), klanes], q2), nt(pk[g, :, lanes], q2)))
                stage = []
                for p, g, half, s, sp in jobs:
                    s = jnp.concatenate([jnp.where(mask, s[:, :128], NEG), jnp.where(mask, s[:, 128:], NEG)], axis=1)
                    top = jnp.maximum(jnp.max(s, axis=0, keepdims=True), jnp.max(sp, axis=0, keepdims=True))
                    stage.append((s, sp, top))
                probs = []
                for s, sp, top in stage:
                    e = jnp.exp(s - top)
                    ep = jnp.exp(sp - top)
                    total = jnp.sum(e, axis=0, keepdims=True) + jnp.sum(ep, axis=0, keepdims=True)
                    probs.append((e.astype(bf16), ep.astype(bf16), total, top))
                outs = []
                for (p, g, half, _, _), (e, ep, total, top) in zip(jobs, probs):
                    r0 = pl.multiple_of(p * 128, 128)
                    outs.append(nn(vt[pl.ds(r0, 128), pl.ds(k0, W)], e) + nn(vt[pl.ds(r0, 128), L : L + PRE], ep))
                for (p, g, half, _, _), (e, ep, total, top), o in zip(jobs, probs, outs):
                    o = o * (1.0 / total)
                    o = jnp.concatenate([o[:64, :128], o[64:, 128:]], axis=0)
                    r0 = pl.multiple_of(p * 128, 128)
                    ctx[0, pl.ds(q0, BLK), pl.ds(r0, 128)] = o.T.astype(bf16)
                    lt = top + jnp.log(total)
                    lse[0, g, 2 * half : 2 * half + 1, pl.ds(q0, BLK)] = lt[:, :128]
                    lse[0, g, 2 * half + 1 : 2 * half + 2, pl.ds(q0, BLK)] = lt[:, 128:]
                return carry

            lax.fori_loop(0, 8 // NP, batch, 0)

        for n in CLASSES:
            pl.when(size == n)(functools.partial(run, n))
        return carry

    lax.fori_loop(0, L // BLK, tile, 0)


def attn_fwd(rows, win, x, w, b, pk, pv, segk, segq):
    R = rows.shape[0]
    row = lambda r, *_: (r, 0, 0)
    all_ = lambda r, *_: (0, 0, 0)
    return pl.pallas_call(
        attn_fwd_kernel,
        grid_spec=pltpu.PrefetchScalarGridSpec(
            num_scalar_prefetch=2,
            grid=(R,),
            in_specs=[
                pl.BlockSpec((1, L, D), lambda r, rows, win: (rows[r], 0, 0)),
                pl.BlockSpec((4, D, 768), all_),
                pl.BlockSpec((4, 1, 768), all_),
                pl.BlockSpec((4, PRE, 256), all_),
                pl.BlockSpec((4, PRE, 256), all_),
                pl.BlockSpec((1, L, 128), row),
                pl.BlockSpec((1, 1, L), row),
            ],
            out_specs=[
                pl.BlockSpec((1, 4, L, 768), lambda r, *_: (r, 0, 0, 0)),
                pl.BlockSpec((1, L, D), row),
                pl.BlockSpec((1, 4, 4, L), lambda r, *_: (r, 0, 0, 0)),
            ],
            scratch_shapes=[pltpu.VMEM((D, L + PRE), bf16)],
        ),
        out_shape=[
            jax.ShapeDtypeStruct((R, 4, L, 768), bf16),
            jax.ShapeDtypeStruct((R, L, D), bf16),
            jax.ShapeDtypeStruct((R, 4, 4, L), f32),
        ],
        compiler_params=pltpu.CompilerParams(vmem_limit_bytes=60 << 20),
        name="attn_fwd",
    )(rows, win, x, w, b, pk, pv, segk, segq)


NB = 8


def split3(v, index):
    high = v.astype(bf16)
    rest = v - high.astype(f32)
    mid = rest.astype(bf16)
    low = (rest - mid.astype(f32)).astype(bf16)
    return jnp.where(index % 3 == 0, high.astype(f32), jnp.where(index % 3 == 1, mid.astype(f32), low.astype(f32)))


def attn_bwd_kernel(
    row, parts, info, win, qkv_h, ctx_h, lse, gf_a, pk, pv, qcol, krow, wo_h, w_h, *rest
):
    qa, da, qt, dt, dq, dkt, dvt, qkv, gfirst, w, sem = rest[-11:]
    wo, ctx = dkt, dvt
    half = L // 2
    if row == 0:
        gin, own, pgrad = rest[-14:-11]
        moves = [(gf_a, gfirst)]
    else:
        gf_s, out_u, out_s = rest[:3]
        gin, out, pgrad, stage, osem = rest[-16:-11]
        moves = [
            (gf_a, gfirst.at[pl.ds(pl.multiple_of(info[2] * half, half), half)]),
            (gf_s, gfirst.at[pl.ds(pl.multiple_of(info[3] * half, half), half)]),
        ]
    moves += [(wo_h, wo), (ctx_h.at[row], ctx), (qkv_h.at[row], qkv), (w_h, w)]
    moves = [pltpu.make_async_copy(src, dst, sem.at[i]) for i, (src, dst) in enumerate(moves)]
    for c in moves:
        c.start()
    if row == 1:
        arrived = [
            pltpu.make_async_copy(out_u, stage.at[0:L], osem.at[0]),
            pltpu.make_async_copy(out_s, stage.at[L : L + TM], osem.at[1]),
        ]
        placed = [
            pltpu.make_async_copy(stage.at[0:L], out.at[2 - info[0]], osem.at[2]),
            pltpu.make_async_copy(
                stage.at[L : L + TM], out.at[1, pl.ds(pl.multiple_of(info[3] * TM, TM), TM)], osem.at[3]
            ),
        ]
        for c in arrived:
            c.start()
    for c in moves[:-2]:
        c.wait()

    at = lambda i, n: (i % 64 < 6) & (i // 64 * 2 + i % 64 // 3 == n)
    for g in range(4):
        cols = slice(256 * g, 256 * g + 256)
        part = nt(gfirst[...], wo[cols, :]).astype(bf16)
        prod = part.astype(f32) * ctx[:, cols].astype(f32)
        high = prod.astype(bf16)
        low = (prod - high.astype(f32)).astype(bf16)
        r = lax.broadcasted_iota(jnp.int32, (256, 128), 0)
        c = lax.broadcasted_iota(jnp.int32, (256, 128), 1)
        pick = jnp.where(at(c, r // 64), 1.0, 0.0).astype(bf16)
        sums = nn(high, pick) + nn(low, pick)
        da[g, :, 0:128] = part[:, :128]
        da[g, :, 128:256] = split3(sums, lax.broadcasted_iota(jnp.int32, (L, 128), 1) % 64).astype(bf16)
        da[g, :, 256:384] = part[:, 128:]
        dt[cols, :] = part.T
    moves[-2].wait()
    for g in range(4):
        index = lax.broadcasted_iota(jnp.int32, (128, L), 0)
        logs = jnp.zeros((128, L), f32)
        for n in range(4):
            logs = jnp.where(at(index, n), lse[0, g, n : n + 1, :], logs)
        qa[g, :, 0:128] = qkv[g, :, 0:128]
        qa[g, :, 128:256] = split3(logs, index % 64).T.astype(bf16)
        qa[g, :, 256:384] = qkv[g, :, 128:256]
        qt[256 * g : 256 * g + 256, :] = qkv[g, :, 0:256].T

    def widen(tile, side):
        r = lax.broadcasted_iota(jnp.int32, (256, 128), 0)
        c = lax.broadcasted_iota(jnp.int32, (256, 128), 1)
        minus = jnp.where(at(c, 2 * side + r // 128), -1.0, 0.0).astype(bf16)
        two = stack_heads(tile)
        return two, jnp.concatenate([two, minus] if side == 0 else [minus, two], axis=1)

    def blocks(jobs, mask, q0, W, first):
        here = pl.ds(q0, W)
        stage_ = []
        for p, g, side, kt, vt in jobs:
            lanes = slice(128 * side, 128 * side + 256)
            k2, ka = widen(kt, side)
            stage_.append((k2, nt(qa[g, here, lanes], ka), nt(da[g, here, lanes], widen(vt, side)[1])))
        probs = []
        for k2, s, dp in stage_:
            e = [jnp.exp(jnp.where(mask, s[:, 128 * h : 128 * h + 128], NEG)) for h in range(2)]
            ds = [(e[h] * dp[:, 128 * h : 128 * h + 128]).astype(bf16) for h in range(2)]
            probs.append((jnp.concatenate([v.astype(bf16) for v in e], axis=1), jnp.concatenate(ds, axis=1)))
        res = []
        for (p, g, side, _, _), (pb, db) in zip(jobs, probs):
            r0 = pl.ds(pl.multiple_of(p * 128, 128), 128)
            dv = nn(dt[r0, here], pb)
            dk = nn(qt[r0, here], db)
            res.append([jnp.concatenate([v[:64, :128], v[64:, 128:]], axis=0) for v in (dk, dv)])
        for (p, g, side, _, _), (k2, _, _), (pb, db) in zip(jobs, stage_, probs):
            r0 = pl.ds(pl.multiple_of(p * 128, 128), 128)
            part = nn(db, k2)
            if first:
                dq[here, r0] = part
            else:
                dq[here, r0] += part
        return res

    def prefix(i, carry):
        jobs = []
        pad = jnp.zeros((128 - PRE, 128), bf16)
        for j in range(NB):
            p = i * NB + j
            g, side = p // 2, j % 2
            lanes = slice(128 * side, 128 * side + 128)
            jobs.append((p, g, side, *(jnp.concatenate([v[g, :, lanes], pad], axis=0) for v in (pk, pv))))
        total = None
        for c in range(2):
            real = lax.broadcasted_iota(jnp.int32, (half, 128), 1) < PRE
            part = blocks(jobs, real, c * half, half, True)
            total = part if total is None else [[a + b for a, b in zip(u, v)] for u, v in zip(total, part)]
        for (p, *_), both in zip(jobs, total):
            for n in range(2):
                pgrad[n, :, pl.ds(pl.multiple_of(p * 128, 128), 128)] = both[n].T[:PRE]
        return carry

    lax.fori_loop(0, 8 // NB, prefix, 0)
    if row == 0:
        r0 = pl.multiple_of(info[4] * parts, 8)
        own[L:] = jnp.concatenate([pgrad[0, pl.ds(r0, parts), :], pgrad[1, pl.ds(r0, parts), :]], axis=0).astype(bf16)
    else:
        for c, d in zip(arrived, placed):
            c.wait()
            d.start()

    def tile(t, carry):
        start = win[row, t, 0]
        size = win[row, 8 + t, 0]
        k0 = pl.multiple_of(t * BLK, BLK)
        q0 = pl.multiple_of(start * BLK, BLK)

        def run(n):
            W = n * BLK
            mask = qcol[0, pl.ds(q0, W), :] == krow[0, :, pl.ds(k0, BLK)]

            many = NB if n <= 5 else NB // 2

            def batch(i, carry):
                jobs = []
                for j in range(many):
                    p = i * many + j
                    g, side = p // 2, j % 2
                    kt = qkv[g, pl.ds(k0, BLK), 256 + 128 * side : 384 + 128 * side]
                    vt = qkv[g, pl.ds(k0, BLK), 512 + 128 * side : 640 + 128 * side]
                    jobs.append((p, g, side, kt, vt))
                for (p, *_), (dk, dv) in zip(jobs, blocks(jobs, mask, q0, W, False)):
                    r0 = pl.ds(pl.multiple_of(p * 128, 128), 128)
                    dkt[r0, pl.ds(k0, BLK)] = dk.astype(bf16)
                    dvt[r0, pl.ds(k0, BLK)] = dv.astype(bf16)
                return carry

            lax.fori_loop(0, 8 // many, batch, 0)

        for n in CLASSES:
            pl.when(size == n)(functools.partial(run, n))
        return carry

    lax.fori_loop(0, L // BLK, tile, 0)
    moves[-1].wait()
    for g in range(4):
        cols = slice(256 * g, 256 * g + 256)
        qkv[g, :, 0:256] = (dq[:, cols] * 0.125).astype(bf16)
        qkv[g, :, 256:512] = dkt[cols, :].T
        qkv[g, :, 512:768] = dvt[cols, :].T
    for c in range(2):
        cols = slice(512 * c, 512 * c + 512)
        acc = gfirst[:, cols].astype(f32)
        for i in range(4):
            acc = acc + nt(qkv[i], w[i, cols, :])
        low = acc.astype(bf16)
        gin[0, :, cols] = low
        if row == 0:
            own[:L, cols] = low
    if row == 1:
        for c in placed:
            c.wait()


def attn_bwd(r, parts, info, win, qkv, ctx, lse, gf, pk, pv, qcol, krow, wo, w, more=()):
    row = lambda i, *_: (r, 0, 0)
    row4 = lambda i, *_: (r, 0, 0, 0)
    all_ = lambda i, *_: (0, 0, 0)
    any_ = pl.BlockSpec(memory_space=pl.ANY)
    shape = jax.ShapeDtypeStruct
    rows = pl.BlockSpec((1, L, D), lambda i, info, win: (info[r], 0, 0))
    grads = pl.BlockSpec((2, PRE, D), all_)
    if r == 0:
        out_specs = [rows, pl.BlockSpec((L + 2 * parts, D), lambda i, *_: (0, 0)), grads]
        out_shape = [shape((3, L, D), bf16), shape((L + 2 * parts, D), bf16), shape((2, PRE, D), f32)]
        scratch = []
    else:
        out_specs = [rows, any_, grads]
        out_shape = [shape((3, L, D), bf16), shape((3, L, D), bf16), shape((2, PRE, D), f32)]
        scratch = [pltpu.VMEM((L + TM, D), bf16), pltpu.SemaphoreType.DMA((4,))]
    return pl.pallas_call(
        functools.partial(attn_bwd_kernel, r, parts),
        grid_spec=pltpu.PrefetchScalarGridSpec(
            num_scalar_prefetch=2,
            grid=(1,),
            in_specs=[
                any_,
                any_,
                pl.BlockSpec((1, 4, 4, L), row4),
                any_,
                pl.BlockSpec((4, PRE, 256), all_),
                pl.BlockSpec((4, PRE, 256), all_),
                pl.BlockSpec((1, L, 128), row),
                pl.BlockSpec((1, 1, L), row),
                any_,
                any_,
            ]
            + [any_ for _ in more],
            out_specs=out_specs,
            scratch_shapes=scratch
            + [
                pltpu.VMEM((4, L, 384), bf16),
                pltpu.VMEM((4, L, 384), bf16),
                pltpu.VMEM((D, L), bf16),
                pltpu.VMEM((D, L), bf16),
                pltpu.VMEM((L, D), f32),
                pltpu.VMEM((D, L), bf16),
                pltpu.VMEM((D, L), bf16),
                pltpu.VMEM((4, L, 768), bf16),
                pltpu.VMEM((L, D), bf16),
                pltpu.VMEM((4, D, 768), bf16),
                pltpu.SemaphoreType.DMA((6,)),
            ],
        ),
        out_shape=out_shape,
        input_output_aliases={15: 0, 16: 1} if more else {},
        compiler_params=pltpu.CompilerParams(vmem_limit_bytes=60 << 20),
        cost_estimate=pl.CostEstimate(flops=40 * 10**9, bytes_accessed=32 << 20, transcendentals=0),
        name="attn_bwd",
    )(info, win, qkv, ctx, lse, gf, pk, pv, qcol, krow, wo, w, *more)


HC = 512
TM = 512
EPS = 1e-5


ERF = (0.797881942323396, 0.036345746572412886, -4.589167395636408e-05, -5.002340812775584e-05,
       3.05428266992555e-06, -6.449413176560626e-08)


def gelu_parts(v):
    u = v * v
    w = jnp.minimum(u, 31.36)
    p = ERF[5] * w + ERF[4]
    for c in ERF[3::-1]:
        p = p * w + c
    phi = 0.5 * jnp.tanh(v * p) + 0.5
    return v * phi, phi


def norm_stats(z):
    mean = jnp.mean(z, axis=1, keepdims=True)
    c = z - mean
    var = jnp.mean(c * c, axis=1, keepdims=True)
    r = lax.rsqrt(var + EPS)
    return c * r, r


def tokens_kernel(shared, info, ctx_h, x_h, cot_h, wo_h, win_h, wout_h, bo, g1, s1, bi, b2, g2, s2, *rest):
    out, own, gf, ctx, x, cot, wo, win, wout, xhat, zbuf, low, act, gp, rs, vb, wsem, tsem = rest[-18:]
    tiles = own.shape[0] // TM
    r, row = (1, info[1]) if shared else (0, info[0])
    at = pl.multiple_of(info[2] * TM, TM) if shared else 0
    M = TM
    fetch_o = pltpu.make_async_copy(wo_h, wo, wsem.at[0])
    fetch_i = [pltpu.make_async_copy(win_h.at[i], win.at[i], wsem.at[1 + i]) for i in range(4)]
    fetch_u = [
        pltpu.make_async_copy(wout_h.at[pl.ds(1024 * i, 1024)], wout.at[pl.ds(1024 * i, 1024)], wsem.at[5 + i])
        for i in range(4)
    ]
    part = lambda j: slice(j * TM, j * TM + TM)
    fetch = lambda src, k, dst, j, i: pltpu.make_async_copy(
        src.at[k, pl.ds(at + j * TM, TM)], dst.at[part(j)], tsem.at[4 * j + i]
    )
    fetch_c = [fetch(ctx_h, r, ctx, j, 0) for j in range(tiles)]
    fetch_x = [fetch(x_h, row, x, j, 1) for j in range(tiles)]
    fetch_t = [fetch(cot_h, row, cot, j, 2) for j in range(tiles)]
    result = [
        pltpu.make_async_copy(own.at[part(j)], out.at[row, pl.ds(at + j * TM, TM)], tsem.at[4 * j + 3])
        for j in range(tiles)
    ]
    for c in [fetch_c[0], fetch_o, fetch_x[0]] + fetch_i + [fetch_t[0]] + fetch_u + fetch_c[1:] + fetch_x[1:] + fetch_t[1:]:
        c.start()

    for j in range(tiles):
        at_j = part(j)
        if j == 0:
            fetch_o.wait()
        fetch_c[j].wait()
        fetch_x[j].wait()
        for c0 in range(0, D, 256):
            cols = slice(c0, c0 + 256)
            zbuf[:, cols] = nn(ctx[at_j], wo[:, cols]) + x[at_j, cols].astype(f32)

        n, r_ = norm_stats(zbuf[...] + bo[...])
        xhat[...] = n
        rs[...] = jnp.broadcast_to(r_, (M, 128))
        y = n * g1[...] + s1[...]
        zbuf[...] = y
        low[...] = y.astype(bf16)

        early = fetch_i if tiles > 1 else fetch_i + fetch_u + fetch_t
        if j == 0:
            for c in early:
                c.wait()
        for i in range(8):
            z, c = i // 2, i % 2
            cols = slice(i * HC, i * HC + HC)
            h = nn(low[...], win[z, :, c * HC : c * HC + HC]) + bi[z, :, 768 + c * HC : 768 + c * HC + HC]
            a, phi = gelu_parts(h)
            act[:, cols] = a.astype(bf16)
            gp[:, cols] = phi.astype(bf16)
            vb[:, cols] = h.astype(bf16)

        if j == 0 and tiles > 1:
            for c in fetch_u:
                c.wait()
        for c0 in range(0, D, 256):
            cols = slice(c0, c0 + 256)
            zbuf[:, cols] += nn(act[...], wout[:, cols])

        if tiles > 1:
            fetch_t[j].wait()
        n, r_ = norm_stats(zbuf[...] + b2[...])
        own[at_j] = (n * g2[...] + s2[...]).astype(bf16)
        result[j].start()
        g = cot[at_j].astype(f32) * g2[...]
        m1 = jnp.mean(g, axis=1, keepdims=True)
        m2 = jnp.mean(g * n, axis=1, keepdims=True)
        d = (g - m1 - n * m2) * r_
        zbuf[...] = d
        low[...] = d.astype(bf16)

        for i in range(8):
            cols = slice(i * HC, i * HC + HC)
            d = nt(low[...], wout[cols, :])
            v = vb[:, cols].astype(f32)
            slope = gp[:, cols].astype(f32) + v * (jnp.exp(-0.5 * v * v) * 0.3989422804014327)
            act[:, cols] = (d * slope).astype(bf16)

        for c0 in range(0, D, 256):
            cols = slice(c0, c0 + 256)
            acc = zbuf[:, cols]
            for z in range(4):
                acc = acc + nt(act[:, 1024 * z : 1024 * z + 1024], win[z, cols, :])
            zbuf[:, cols] = acc

        n = xhat[...]
        g = zbuf[...] * g1[...]
        m1 = jnp.mean(g, axis=1, keepdims=True)
        m2 = jnp.mean(g * n, axis=1, keepdims=True)
        gf[at_j] = ((g - m1 - n * m2) * rs[:, 0:1]).astype(bf16)
    for c in result:
        c.wait()


def tokens(shared, info, ctx, x, cot, wo, win, wout, bo, g1, s1, bi, b2, g2, s2, into=None):
    n = TM if shared else L
    any_ = pl.BlockSpec(memory_space=pl.ANY)
    whole = lambda a: pl.BlockSpec(a.shape, lambda i, info: (0,) * a.ndim)
    block = pl.BlockSpec((n, D), lambda i, info: (0, 0))
    vectors = (bo, g1, s1, bi, b2, g2, s2)
    extra = [] if into is None else [into]
    return pl.pallas_call(
        functools.partial(tokens_kernel, shared),
        grid_spec=pltpu.PrefetchScalarGridSpec(
            num_scalar_prefetch=1,
            grid=(1,),
            in_specs=[any_] * 6 + [whole(a) for a in vectors] + [any_ for _ in extra],
            out_specs=[any_, block, block],
            scratch_shapes=[
                pltpu.VMEM((n, D), bf16),
                pltpu.VMEM((n, D), bf16),
                pltpu.VMEM((n, D), bf16),
                pltpu.VMEM((D, D), bf16),
                pltpu.VMEM((4, D, D), bf16),
                pltpu.VMEM((4 * D, D), bf16),
                pltpu.VMEM((TM, D), f32),
                pltpu.VMEM((TM, D), f32),
                pltpu.VMEM((TM, D), bf16),
                pltpu.VMEM((TM, 4 * D), bf16),
                pltpu.VMEM((TM, 4 * D), bf16),
                pltpu.VMEM((TM, 128), f32),
                pltpu.VMEM((TM, 4 * D), bf16),
                pltpu.SemaphoreType.DMA((9,)),
                pltpu.SemaphoreType.DMA((8,)),
            ],
        ),
        out_shape=[
            jax.ShapeDtypeStruct((3, L, D), bf16),
            jax.ShapeDtypeStruct((n, D), bf16),
            jax.ShapeDtypeStruct((n, D), bf16),
        ],
        input_output_aliases={14: 0} if extra else {},
        compiler_params=pltpu.CompilerParams(vmem_limit_bytes=60 << 20),
        cost_estimate=pl.CostEstimate(flops=(n // TM) * 25 * 10**9, bytes_accessed=24 << 20, transcendentals=0),
        name="tokens",
    )(info, ctx, x, cot, wo, win, wout, *vectors, *extra)


SPAN = 512
KINDS = 10


def front_kernel(
    hid, seg, msk, pk_s, pv_s, bq, bk, bv, bi, wq, wk, wv, wo_s, wi_s, wu_s,
    wqkv, wo, wi, wu, qkv, ctx, lse, pk, pv, vec, segk, segq, wins, qcol, krow,
    own0, x, wbuf, qb, vt, cb, pre, xsem, lsem, osem, ssem, rsem,
):
    d = lax.axis_index("dp")
    z = lax.axis_index("prefix")
    core, xx, yy = d % 2, (d // 2) % 2, d // 4
    dc = d + 1 - 2 * core
    dx = d + 2 - 4 * xx
    dy = d + 4 - 8 * yy
    dxy = dx + dy - d
    unique = 2 * (z % 2)
    MESH = pl.DeviceIdType.MESH

    def region(pay, zz, dd, half=None):
        if pay in (4, 5):
            return (pre, vec)[pay - 4].at[zz]
        if pay == 0:
            n, ref = 128, lambda o, s: wqkv.at[zz, pl.ds(128 * dd + o, s), :]
        elif pay == 1:
            n, ref = 256, lambda o, s: wo.at[pl.ds(256 * zz + o, s), pl.ds(128 * dd, 128)]
        elif pay == 2:
            n, ref = 128, lambda o, s: wi.at[zz, pl.ds(128 * dd + o, s), :]
        else:
            o0 = 0 if pay == 3 else 512
            n, ref = 512, lambda o, s: wu.at[pl.ds(1024 * zz + o0 + o, s), pl.ds(128 * dd, 128)]
        return ref(0, n) if half is None else ref(half * (n // 2), n // 2)

    def rows_of(zz, c):
        return wu.at[pl.ds(1024 * zz + 512 + 256 * c, 256), :]

    own0[:, 0:256] = wq[...]
    own0[:, 256:512] = wk[...]
    own0[:, 512:768] = wv[...]
    shards = {0: own0, 1: wo_s, 2: wi_s, 3: wu_s.at[0:512], 6: wu_s.at[512:1024]}
    xin = [pltpu.make_async_copy(hid.at[unique], x.at[0], xsem.at[0]), pltpu.make_async_copy(hid.at[1], x.at[1], xsem.at[1])]
    for c in xin:
        c.start()

    bar = pltpu.get_barrier_semaphore()

    def hello(dev):
        pl.semaphore_signal(bar, inc=1, device_id=dev, device_id_type=MESH)

    for dd in (dc, dx, dy):
        hello((dd, z))
    pl.when(z > 0)(lambda: hello((d, z - 1)))
    pl.when(z < 3)(lambda: hello((d, z + 1)))

    pre[z, 0:24, :] = pk_s[...]
    pre[z, 32:56, :] = pv_s[...]
    vec[z, :, 0:256] = bq[...]
    vec[z, :, 256:512] = bk[...]
    vec[z, :, 512:768] = bv[...]
    vec[z, :, 768:] = bi[...]
    for r in range(2):
        own = seg[pl.ds(unique, 1), :] if r == 0 else seg[1:2, :]
        real = msk[pl.ds(unique, 1), :] if r == 0 else msk[1:2, :]
        segq[r] = own.astype(f32)
        keys = jnp.where(real == 1, own, -1).astype(f32)
        segk[r] = jnp.broadcast_to(keys, (128, L)).T
        qcol[r] = jnp.broadcast_to(own.astype(f32), (128, L)).T
        krow[r] = keys
        line = own.astype(f32)
        for t in range(L // BLK):
            first, last = line[:, t * BLK : t * BLK + 1], line[:, t * BLK + BLK - 1 : t * BLK + BLK]
            begin = jnp.floor(jnp.sum(jnp.where(line < first, 1.0, 0.0), axis=1, keepdims=True) / BLK)
            stop = jnp.floor((jnp.sum(jnp.where(line <= last, 1.0, 0.0), axis=1, keepdims=True) + (BLK - 1)) / BLK)
            size = jnp.full_like(begin, float(CLASSES[-1]))
            for n in reversed(CLASSES[:-1]):
                size = jnp.where(stop - begin <= n, float(n), size)
            begin = jnp.minimum(begin, L // BLK - size)
            wins[r, t : t + 1, :] = jnp.broadcast_to(begin, (1, 128)).astype(jnp.int32)
            wins[r, 8 + t : 9 + t, :] = jnp.broadcast_to(size, (1, 128)).astype(jnp.int32)

    local = [pltpu.make_async_copy(src, region(p, z, d), lsem.at[i]) for i, (p, src) in enumerate(shards.items())]
    for c in local:
        c.start()
    peers = jnp.where(z > 0, 1, 0) + jnp.where(z < 3, 1, 0)
    pl.semaphore_wait(bar, 3 + peers)

    def copy(kind, pay, zz, dd, half, dev, skind, src=None):
        r = region(pay, zz, dd, half)
        return pltpu.make_async_remote_copy(
            src_ref=r if src is None else src, dst_ref=r, send_sem=ssem.at[pay * 4 + zz, skind], recv_sem=rsem.at[pay * 4 + zz, kind],
            device_id=dev, device_id_type=MESH,
        )

    def block(k):
        second = jnp.where(z == 0, 1, z - 1)
        third = jnp.where(z == 0, 2, jnp.where(z == 3, 1, z + 1))
        last = jnp.where(z <= 1, 3, 0)
        return jnp.where(k == 0, z, jnp.where(k == 1, second, jnp.where(k == 2, third, last)))

    def up(pay, zz, src=None):
        return copy(0, pay, zz, d, None, (d, z + 1), 10, src)

    def down(pay, zz, src=None):
        return copy(0, pay, zz, d, None, (d, z - 1), 0, src)

    def along(pay, h):
        @pl.when(z >= h)
        def _():
            up(pay, z - h).wait_recv()
            pl.when(z < 3)(lambda: up(pay, z - h).start())

        @pl.when(z + h <= 3)
        def _():
            down(pay, z + h).wait_recv()
            pl.when(z > 0)(lambda: down(pay, z + h).start())

    def stage1(pay, k, src=None):
        zz = block(k)
        copy(1, pay, zz, d, None, (dx, z), 1, src).start()
        copy(2, pay, zz, d, None, (dy, z), 2, src).start()
        copy(5, pay, zz, d, None, (dc, z), 5, src).start()

    def stage2(pay, k):
        zz = block(k)
        copy(1, pay, zz, dx, None, (dx, z), 1).wait_recv()
        copy(3, pay, zz, dx, 0, (dy, z), 3).start()
        copy(6, pay, zz, dx, None, (dc, z), 6).start()
        copy(2, pay, zz, dy, None, (dy, z), 2).wait_recv()
        copy(4, pay, zz, dy, 1, (dx, z), 4).start()
        copy(7, pay, zz, dy, None, (dc, z), 7).start()

    def stage3(pay, k):
        zz = block(k)
        copy(3, pay, zz, dxy, 0, (dy, z), 3).wait_recv()
        copy(8, pay, zz, dxy, 0, (dc, z), 8).start()
        copy(4, pay, zz, dxy, 1, (dx, z), 4).wait_recv()
        copy(9, pay, zz, dxy, 1, (dc, z), 9).start()

    def stage4(pay, k):
        zz = block(k)
        o = dc - d
        copy(5, pay, zz, d + o, None, (dc, z), 5).wait_recv()
        copy(6, pay, zz, dx + o, None, (dc, z), 6).wait_recv()
        copy(7, pay, zz, dy + o, None, (dc, z), 7).wait_recv()
        copy(8, pay, zz, dxy + o, 0, (dc, z), 8).wait_recv()
        copy(9, pay, zz, dxy + o, 1, (dc, z), 9).wait_recv()

    def haul(zz, dz, kind):
        r = rows_of(zz, core)
        return pltpu.make_async_remote_copy(
            src_ref=r, dst_ref=r, send_sem=ssem.at[24 + zz, kind], recv_sem=rsem.at[24 + zz, 0],
            device_id=(d, z + dz), device_id_type=MESH,
        )

    def share(zz, c):
        r = rows_of(zz, c)
        return pltpu.make_async_remote_copy(
            src_ref=r, dst_ref=r, send_sem=ssem.at[24 + zz, 5], recv_sem=rsem.at[24 + zz, 5],
            device_id=(dc, z), device_id_type=MESH,
        )

    def haul_on(h):
        @pl.when(z >= h)
        def _():
            haul(z - h, 1, 10).wait_recv()
            pl.when(z < 3)(lambda: haul(z - h, 1, 10).start())
            share(z - h, core).start()

        @pl.when(z + h <= 3)
        def _():
            haul(z + h, -1, 0).wait_recv()
            pl.when(z > 0)(lambda: haul(z + h, -1, 0).start())
            share(z + h, core).start()

    def drain(pay, zz):
        if pay != 6:
            pl.when((zz <= z) & (z < 3))(lambda: up(pay, zz).wait_send())
            pl.when((zz >= z) & (z > 0))(lambda: down(pay, zz).wait_send())
        if pay in (4, 5):
            return
        copy(1, pay, zz, d, None, (dx, z), 1).wait_send()
        copy(2, pay, zz, d, None, (dy, z), 2).wait_send()
        copy(3, pay, zz, dx, 0, (dy, z), 3).wait_send()
        copy(4, pay, zz, dy, 1, (dx, z), 4).wait_send()
        copy(5, pay, zz, d, None, (dc, z), 5).wait_send()
        copy(6, pay, zz, dx, None, (dc, z), 6).wait_send()
        copy(7, pay, zz, dy, None, (dc, z), 7).wait_send()
        copy(8, pay, zz, dxy, 0, (dc, z), 8).wait_send()
        copy(9, pay, zz, dxy, 1, (dc, z), 9).wait_send()

    ffn = (2, 3, 1)
    ffn = (2, 3, 1)

    def set_out(pay):
        src = shards.get(pay)
        pl.when(z < 3)(lambda: up(pay, z, src).start())
        pl.when(z > 0)(lambda: down(pay, z, src).start())

    stage1(0, 0, own0)
    for pay in (0, 4, 5):
        set_out(pay)
    stage2(0, 0)
    for pay in (4, 5, 0):
        along(pay, 1)
    stage1(0, 1)
    stage3(0, 0)
    for pay in (4, 5):
        along(pay, 2)
    for pay in ffn:
        set_out(pay)
    for pay in (4, 5):
        along(pay, 3)
    stage1(2, 0, wi_s)
    for g in range(4):
        lanes = slice(256 * g, 256 * g + 256)
        for ref, o in ((pk, 0), (pv, 32)):
            parts = [pre[i, o : o + 32, lanes].astype(f32)[:24] for i in range(4)]
            ref[g] = jnp.concatenate(parts, axis=0).astype(bf16)
    for c in xin + local:
        c.wait()

    def outs(zz):
        q = [pltpu.make_async_copy(qb.at[r], qkv.at[r, zz], osem.at[r]) for r in range(2)]
        c = [
            pltpu.make_async_copy(cb.at[r], ctx.at[r, :, pl.ds(pl.multiple_of(256 * zz, 256), 256)], osem.at[2 + r])
            for r in range(2)
        ]
        return q, c

    def project(r, zz, slot):
        y = nn(x[r], wbuf[slot]) + vec[zz, :, 0:768]
        qb[r, :, 0:256] = (y[:, :256].astype(bf16) * 0.125).astype(bf16)
        kv = y[:, 256:].astype(bf16)
        qb[r, :, 256:] = kv
        vt[r, :, :L] = kv[:, 256:].T
        vt[r, :, L:] = pv[zz].T

    def attend(t, zz):
        jobs = []
        for tt in (t, L // BLK - 1 - t):
            first = max(0, tt - SPAN // BLK)
            stop = min(L // BLK, tt + SPAN // BLK + 1)
            k = slice(first * BLK, stop * BLK)
            q = slice(tt * BLK, tt * BLK + BLK)
            for r in range(2):
                seen = segk[r, k, :] == segq[r, :, q]
                for p in range(2):
                    lanes = slice(128 * p, 128 * p + 128)
                    q2 = stack_heads(qb[r, q, lanes])
                    s = nt(qb[r, k, 256 + 128 * p : 384 + 128 * p], q2)
                    jobs.append((r, p, q, k, lanes, seen, s, nt(pk[zz, :, lanes], q2)))
        stage = []
        for r, p, q, k, lanes, seen, s, sp in jobs:
            s = jnp.concatenate([jnp.where(seen, s[:, :128], NEG), jnp.where(seen, s[:, 128:], NEG)], axis=1)
            top = jnp.maximum(jnp.max(s, axis=0, keepdims=True), jnp.max(sp, axis=0, keepdims=True))
            stage.append((s, sp, top))
        probs = []
        for s, sp, top in stage:
            e = jnp.exp(s - top)
            ep = jnp.exp(sp - top)
            total = jnp.sum(e, axis=0, keepdims=True) + jnp.sum(ep, axis=0, keepdims=True)
            probs.append((e.astype(bf16), ep.astype(bf16), total, top))
        res = []
        for (r, p, q, k, lanes, _, _, _), (e, ep, total, top) in zip(jobs, probs):
            res.append(nn(vt[r, lanes, k], e) + nn(vt[r, lanes, L : L + PRE], ep))
        for (r, p, q, k, lanes, _, _, _), (e, ep, total, top), o in zip(jobs, probs, res):
            o = o * (1.0 / total)
            o = jnp.concatenate([o[:64, :128], o[64:, 128:]], axis=0)
            cb[r, q, lanes] = o.T.astype(bf16)
            lt = top + jnp.log(total)
            lse[r, zz, 2 * p : 2 * p + 1, q] = lt[:, :128]
            lse[r, zz, 2 * p + 1 : 2 * p + 2, q] = lt[:, 128:]

    plan = {
        (0, 0): [("z", 0, 2), (1, 0, 2)],
        (0, 1): [(2, 0, 1)],
        (0, 2): [("z", 0, 3), (1, 0, 3)],
        (0, 3): [(3, 0, 1), (2, 0, 2), (1, 3, 0)],
        (0, 4): [(1, 6, 0), (1, 1, 0)],
        (0, 5): [(2, 0, 3)],
        (1, 0): [(3, 0, 2), ("z", 2, 1), ("z", 3, 1), ("z", 1, 1), (1, 2, 1)],
        (1, 1): [(2, 2, 0), (1, 3, 1)],
        (1, 2): [(3, 0, 3), (1, 1, 1)],
        (1, 3): [(2, 3, 0), (2, 6, 0)],
        (1, 4): [(2, 1, 0)],
        (1, 5): [("z", 2, 2), ("z", 3, 2), ("z", 1, 2), (1, 2, 2), (1, 3, 2)],
        (2, 0): [(3, 2, 0), (3, 3, 0), (3, 6, 0)],
        (2, 1): [(2, 2, 1), (1, 1, 2), ("h", 6, 0)],
        (2, 2): [(2, 3, 1), (3, 1, 0)],
        (2, 3): [(2, 1, 1)],
        (2, 4): [("z", 2, 3), ("z", 3, 3), ("z", 1, 3), (1, 2, 3), (1, 3, 3), (1, 1, 3)],
        (2, 5): [(3, 2, 1), (3, 3, 1)],
        (3, 0): [("h", 6, 1), (2, 2, 2), (3, 1, 1)],
        (3, 1): [(2, 3, 2)],
        (3, 2): [(2, 1, 2)],
        (3, 3): [("h", 6, 2), (3, 2, 2)],
        (3, 4): [(2, 2, 3)],
        (3, 5): [(3, 3, 2), (3, 1, 2)],
        (4, 0): [(2, 3, 3), (2, 1, 3), ("h", 6, 3), (3, 2, 3), (3, 3, 3), (3, 1, 3)],
    }

    def act(what, pay, k):
        if what == "z":
            along(pay, k)
        elif what == "h" and k == 0:
            stage4(6, 0)
            pl.when(z < 3)(lambda: haul(z, 1, 10).start())
            pl.when(z > 0)(lambda: haul(z, -1, 0).start())
        elif what == "h":
            haul_on(k)
        elif what == 1:
            stage1(pay, k, shards[pay] if k == 0 else None)
        else:
            (stage2, stage3)[what - 2](pay, k)

    def group(s, carry):
        zz = block(s)

        def pump(slot):
            for i in range(4):

                @pl.when(s == i)
                def _():
                    for step in plan[i, slot]:
                        act(*step)

        def weights(k):
            return pltpu.make_async_copy(wqkv.at[block(k)], wbuf.at[k % 2], xsem.at[2 + k % 2])

        @pl.when(s == 0)
        def _():
            stage4(0, 0)
            weights(0).start()

        before = outs(block(s - 1))

        @pl.when(s > 0)
        def _():
            for o in before[0]:
                o.wait()

        weights(s).wait()
        project(0, zz, s % 2)
        pump(0)
        project(1, zz, s % 2)
        q, c = outs(zz)
        for o in q:
            o.start()
        pump(1)

        @pl.when(s > 0)
        def _():
            for o in before[1]:
                o.wait()

        for t in range(4):
            attend(t, zz)
            pump(2 + t)
            if t == 2:

                @pl.when(s < 3)
                def _():
                    stage4(0, s + 1)
                    weights(s + 1).start()

        for o in c:
            o.start()
        return carry

    lax.fori_loop(0, 4, group, 0)
    for step in plan[4, 0]:
        act(*step)
    q, c = outs(block(3))
    for o in q + c:
        o.wait()

    def finish(k, done):
        for pay in (1, 2, 3):
            stage4(pay, k)
        for pay in range(6):
            drain(pay, k)

        @pl.when(k == z)
        def _():
            drain(6, k)

        @pl.when(k != z)
        def _():
            share(k, 1 - core).wait_recv()
            share(k, core).wait_send()

        pl.when((k <= z) & (z < 3))(lambda: haul(k, 1, 10).wait_send())
        pl.when((k >= z) & (z > 0))(lambda: haul(k, -1, 0).wait_send())
        return done

    lax.fori_loop(0, 4, finish, 0)


def front(hid, seg, msk, pk, pv, bq, bk, bv, bi, wq, wk, wv, wo, wi, wu):
    any_ = pl.BlockSpec(memory_space=pl.ANY)
    vmem = pl.BlockSpec(memory_space=pltpu.VMEM)
    shape = jax.ShapeDtypeStruct
    return pl.pallas_call(
        front_kernel,
        in_specs=[any_] + [vmem] * 14,
        out_specs=[any_] * 6 + [vmem] * 9,
        out_shape=[
            shape((4, D, 768), bf16),
            shape((D, D), bf16),
            shape((4, D, D), bf16),
            shape((4 * D, D), bf16),
            shape((2, 4, L, 768), bf16),
            shape((2, L, D), bf16),
            shape((2, 4, 4, L), f32),
            shape((4, PRE, 256), bf16),
            shape((4, PRE, 256), bf16),
            shape((4, 1, 1792), f32),
            shape((2, L, 128), f32),
            shape((2, 1, L), f32),
            shape((2, 16, 128), jnp.int32),
            shape((2, L, 128), f32),
            shape((2, 1, L), f32),
        ],
        scratch_shapes=[
            pltpu.VMEM((128, 768), bf16),
            pltpu.VMEM((2, L, D), bf16),
            pltpu.VMEM((2, D, 768), bf16),
            pltpu.VMEM((2, L, 768), bf16),
            pltpu.VMEM((2, 256, L + PRE), bf16),
            pltpu.VMEM((2, L, 256), bf16),
            pltpu.VMEM((4, 64, D), bf16),
            pltpu.SemaphoreType.DMA((4,)),
            pltpu.SemaphoreType.DMA((5,)),
            pltpu.SemaphoreType.DMA((4,)),
            pltpu.SemaphoreType.DMA((28, KINDS + 1)),
            pltpu.SemaphoreType.DMA((28, KINDS)),
        ],
        compiler_params=pltpu.CompilerParams(
            collective_id=0, has_side_effects=True, vmem_limit_bytes=60 << 20
        ),
        name="front",
    )(hid, seg, msk, pk, pv, bq, bk, bv, bi, wq, wk, wv, wo, wi, wu)


def front_plain(rows, hid, seg, msk, pk, pv, bq, bk, bv, bi, wq, wk, wv, wo, wi, wu):
    over = lambda v, axis, at: lax.all_gather(v, axis, axis=at, tiled=True)
    each = lambda v: lax.all_gather(v, "prefix")
    wqkv = each(jnp.concatenate([over(w, "dp", 0) for w in (wq, wk, wv)], axis=1))
    vec = each(jnp.concatenate([bq, bk, bv, bi], axis=1))
    by_group = lambda p: over(p, "prefix", 0).reshape(PRE, 4, 256).transpose(1, 0, 2)
    pk, pv = by_group(pk), by_group(pv)
    segk = jnp.broadcast_to(jnp.where(msk == 1, seg, -1)[rows][:, :, None], (2, L, 128)).astype(f32)
    segq = seg[rows][:, None, :].astype(f32)
    win = windows(seg[rows])
    qkv, ctx, lse = attn_fwd(rows, win, hid, wqkv, vec[:, :, :768], pk, pv, segk, segq)
    wins = jnp.broadcast_to(jnp.concatenate([win[..., 0], win[..., 1]], axis=1)[:, :, None], (2, 16, 128))
    return (
        wqkv, over(over(wo, "dp", 1), "prefix", 0), each(over(wi, "dp", 0)), over(over(wu, "dp", 1), "prefix", 0),
        qkv, ctx, lse, pk, pv, vec, segk, segq, wins,
        jnp.broadcast_to(segq[:, 0, :, None], (2, L, 128)), segk[:, None, :, 0],
    )


def total_kernel(uniq, shared, came, key, value, other, both, mine, half, slots, osem, ssem, rsem):
    d = lax.axis_index("dp")
    z = lax.axis_index("prefix")
    core, chip = d % 2, d // 2
    xx, yy = chip % 2, chip // 2
    dc = d + 1 - 2 * core
    peers = [((d + 2 - 4 * xx), chip + 1 - 2 * xx), ((d + 4 - 8 * yy), chip + 2 - 4 * yy)]
    peers.append((peers[0][0] + peers[1][0] - d, 3 - chip))
    bar = pltpu.get_barrier_semaphore()
    for dd in (dc, *(p for p, _ in peers)):
        pl.semaphore_signal(bar, inc=1, device_id=(dd, z), device_id_type=pl.DeviceIdType.MESH)
    n = key.shape[0]
    r0 = pl.multiple_of(z * n, 8)
    fetch = [
        pltpu.make_async_copy(came.at[pl.ds(L, 2 * n)], other, osem.at[0]),
        pltpu.make_async_copy(uniq.at[:, pl.ds(r0, n), :], both.at[0], osem.at[1]),
        pltpu.make_async_copy(shared.at[:, pl.ds(r0, n), :], both.at[1], osem.at[2]),
    ]
    for c in fetch:
        c.start()
    for c in fetch:
        c.wait()
    add = other[...].astype(f32)
    for i in range(2):
        mine[i] = both[0, i] + both[1, i] + add[i * n : i * n + n]
    pl.semaphore_wait(bar, 4)

    def send(src, dst, i, dd):
        return pltpu.make_async_remote_copy(
            src_ref=src, dst_ref=dst, send_sem=ssem.at[i], recv_sem=rsem.at[i],
            device_id=(dd, z), device_id_type=pl.DeviceIdType.MESH,
        )

    first = send(mine.at[1 - core], half, 0, dc)
    first.start()
    first.wait()
    slots[chip] = mine[core] + half[...]
    copies = [send(slots.at[chip], slots.at[chip], 1 + i, dd) for i, (dd, _) in enumerate(peers)]
    for c in copies:
        c.start()
    for c in copies:
        c.wait()
    total = (slots[0] + slots[1]) + (slots[2] + slots[3])

    @pl.when(core == 0)
    def _():
        key[...] = total
        last = send(key, key, 4, dc)
        last.start()
        last.wait_send()
        send(value, value, 5, dc).wait_recv()

    @pl.when(core == 1)
    def _():
        value[...] = total
        last = send(value, value, 5, dc)
        last.start()
        last.wait_send()
        send(key, key, 4, dc).wait_recv()


def total_grads(uniq, shared, came):
    n = PRE // 4
    vmem = pl.BlockSpec(memory_space=pltpu.VMEM)
    return pl.pallas_call(
        total_kernel,
        in_specs=[pl.BlockSpec(memory_space=pl.ANY)] * 3,
        out_specs=[vmem] * 2,
        out_shape=[jax.ShapeDtypeStruct((n, D), f32)] * 2,
        scratch_shapes=[
            pltpu.VMEM((2 * n, D), bf16),
            pltpu.VMEM((2, 2, n, D), f32),
            pltpu.VMEM((2, n, D), f32),
            pltpu.VMEM((n, D), f32),
            pltpu.VMEM((4, n, D), f32),
            pltpu.SemaphoreType.DMA((3,)),
            pltpu.SemaphoreType.DMA((6,)),
            pltpu.SemaphoreType.DMA((6,)),
        ],
        compiler_params=pltpu.CompilerParams(collective_id=1, has_side_effects=True),
        name="total_grads",
    )(uniq, shared, came)


def body(
    hidden_in, cotangent, segment_ids, key_mask, prefix_keys, prefix_values,
    w_query, b_query, w_key, b_key, w_value, b_value, w_attn_out, b_attn_out, gain_attn, shift_attn,
    w_ffn_in, b_ffn_in, w_ffn_out, b_ffn_out, gain_ffn, shift_ffn,
):
    z = lax.axis_index("prefix")
    side = z % 2
    info = jnp.stack([2 * side, jnp.ones_like(side), side, 1 - side, z + 1 - 2 * side]).astype(jnp.int32)
    line = lambda v: v.reshape(1, -1)
    small = lax.axis_size("dp") == 8 and lax.axis_size("prefix") == 4
    start = front if small else functools.partial(front_plain, info[:2])
    w_qkv, w_out, w_up, w_down, qkv, ctx, lse, pk, pv, vec, _, _, win, qcol, krow = start(
        hidden_in, segment_ids, key_mask, prefix_keys, prefix_values,
        line(b_query), line(b_key), line(b_value), line(b_ffn_in),
        w_query, w_key, w_value, w_attn_out, w_ffn_in, w_ffn_out,
    )
    weights = (
        w_out, w_up, w_down, line(b_attn_out), line(gain_attn), line(shift_attn),
        vec, line(b_ffn_out), line(gain_ffn), line(shift_ffn),
    )
    pairs = [(i, i + 1 - 2 * (i % 2)) for i in range(lax.axis_size("prefix"))]
    swap = lambda v: lax.ppermute(v, "prefix", pairs)
    tie = lax.optimization_barrier
    args = (info, ctx, hidden_in, cotangent, *weights)
    out, out_s, gf_s = tokens(True, *args)
    out_s_other, gf_s_other = swap(out_s), swap(gf_s)
    out, out_u, gf_u = tokens(False, *args, into=out)
    out, out_s_other, gf_s_other, gf_u = tie((out, out_s_other, gf_s_other, gf_u))
    out_u_other = swap(out_u)
    parts = PRE // lax.axis_size("prefix")
    common = (pk, pv, qcol, krow, w_out, w_qkv)
    gin, gin_own, uniq = attn_bwd(0, parts, info, win, qkv, ctx, lse, gf_u, *common)
    gin, out_u_other = tie((gin, out_u_other))
    came = swap(gin_own)
    gin, out, shared = attn_bwd(
        1, parts, info, win, qkv, ctx, lse, gf_s, *common, more=(gf_s_other, out_u_other, out_s_other, gin, out)
    )
    if small:
        keys, values = total_grads(uniq, shared, came)
    else:
        own = lax.dynamic_slice_in_dim(uniq + shared, z * parts, parts, 1)
        keys, values = lax.psum(own + came[L:].reshape(2, parts, D).astype(f32), "dp")
    gin = lax.dynamic_update_slice(gin, came[None, :L], (2 - info[0], 0, 0))
    return out, gin, keys, values


def solution(mesh):
    return jax.shard_map(
        body,
        mesh=mesh,
        in_specs=(
            P("dp", None, None), P("dp", None, None), P("dp", None), P("dp", None),
            P("prefix", None), P("prefix", None),
            P("dp", "prefix"), P("prefix"), P("dp", "prefix"), P("prefix"), P("dp", "prefix"), P("prefix"),
            P("prefix", "dp"), P(), P(), P(),
            P("dp", "prefix"), P("prefix"), P("prefix", "dp"), P(), P(), P(),
        ),
        out_specs=(P("dp", None, None), P("dp", None, None), P("prefix", None), P("prefix", None)),
        check_vma=False,
    )
```

```python
import functools
import jax
import jax.numpy as jnp
from jax import lax
from jax.experimental import pallas as pl
from jax.experimental.pallas import tpu as pltpu
from jax.sharding import PartitionSpec as P

L = 1024
D = 1024
PRE = 96
BLK = 128
NEG = -1e30
CLASSES = (2, 3, 4, 5, 6, 8)
bf16 = jnp.bfloat16
f32 = jnp.float32


def nt(a, b):
    return lax.dot_general(a, b, (((1,), (1,)), ((), ())), preferred_element_type=f32)


def nn(a, b):
    return jnp.dot(a, b, preferred_element_type=f32)


def stack_heads(tile):
    lane = lax.broadcasted_iota(jnp.int32, tile.shape, 1)
    zero = jnp.zeros_like(tile)
    return jnp.concatenate([jnp.where(lane < 64, tile, zero), jnp.where(lane >= 64, tile, zero)], axis=0)


def windows(seg):
    tiles = seg.shape[-1] // BLK
    first = seg[..., ::BLK]
    last = seg[..., BLK - 1 :: BLK]
    start = jnp.sum((seg[..., None, :] < first[..., :, None]).astype(jnp.int32), axis=-1) // BLK
    stop = (jnp.sum((seg[..., None, :] <= last[..., :, None]).astype(jnp.int32), axis=-1) + BLK - 1) // BLK
    need = stop - start
    size = jnp.full_like(need, CLASSES[-1])
    for n in reversed(CLASSES[:-1]):
        size = jnp.where(need <= n, n, size)
    start = jnp.minimum(start, tiles - size)
    return jnp.stack([start, size], axis=-1)


NP = 8


def attn_fwd_kernel(rows, win, x, w, b, pk, pv, segk, segq, qkv, ctx, lse, vt):
    row = pl.program_id(0)
    for g in range(4):
        y = nn(x[0], w[g]) + b[g]
        q = (y[:, :256].astype(bf16) * 0.125).astype(bf16)
        qkv[0, g, :, :256] = q
        kv = y[:, 256:].astype(bf16)
        qkv[0, g, :, 256:] = kv
        vt[256 * g : 256 * g + 256, :L] = kv[:, 256:].T
        vt[256 * g : 256 * g + 256, L:] = pv[g].T

    def tile(t, carry):
        start = win[row, t, 0]
        size = win[row, t, 1]
        q0 = pl.multiple_of(t * BLK, BLK)
        k0 = pl.multiple_of(start * BLK, BLK)

        def run(n):
            W = n * BLK
            mask = segk[0, pl.ds(k0, W), :] == segq[0, :, pl.ds(q0, BLK)]

            def batch(i, carry):
                jobs = []
                for j in range(NP):
                    p = i * NP + j
                    g, half = p // 2, j % 2
                    lanes = slice(128 * half, 128 * half + 128)
                    klanes = slice(256 + 128 * half, 384 + 128 * half)
                    q2 = stack_heads(qkv[0, g, pl.ds(q0, BLK), lanes])
                    jobs.append((p, g, half, nt(qkv[0, g, pl.ds(k0, W), klanes], q2), nt(pk[g, :, lanes], q2)))
                stage = []
                for p, g, half, s, sp in jobs:
                    s = jnp.concatenate([jnp.where(mask, s[:, :128], NEG), jnp.where(mask, s[:, 128:], NEG)], axis=1)
                    top = jnp.maximum(jnp.max(s, axis=0, keepdims=True), jnp.max(sp, axis=0, keepdims=True))
                    stage.append((s, sp, top))
                probs = []
                for s, sp, top in stage:
                    e = jnp.exp(s - top)
                    ep = jnp.exp(sp - top)
                    total = jnp.sum(e, axis=0, keepdims=True) + jnp.sum(ep, axis=0, keepdims=True)
                    probs.append((e.astype(bf16), ep.astype(bf16), total, top))
                outs = []
                for (p, g, half, _, _), (e, ep, total, top) in zip(jobs, probs):
                    r0 = pl.multiple_of(p * 128, 128)
                    outs.append(nn(vt[pl.ds(r0, 128), pl.ds(k0, W)], e) + nn(vt[pl.ds(r0, 128), L : L + PRE], ep))
                for (p, g, half, _, _), (e, ep, total, top), o in zip(jobs, probs, outs):
                    o = o * (1.0 / total)
                    o = jnp.concatenate([o[:64, :128], o[64:, 128:]], axis=0)
                    r0 = pl.multiple_of(p * 128, 128)
                    ctx[0, pl.ds(q0, BLK), pl.ds(r0, 128)] = o.T.astype(bf16)
                    lt = top + jnp.log(total)
                    lse[0, g, 2 * half : 2 * half + 1, pl.ds(q0, BLK)] = lt[:, :128]
                    lse[0, g, 2 * half + 1 : 2 * half + 2, pl.ds(q0, BLK)] = lt[:, 128:]
                return carry

            lax.fori_loop(0, 8 // NP, batch, 0)

        for n in CLASSES:
            pl.when(size == n)(functools.partial(run, n))
        return carry

    lax.fori_loop(0, L // BLK, tile, 0)


def attn_fwd(rows, win, x, w, b, pk, pv, segk, segq):
    R = rows.shape[0]
    row = lambda r, *_: (r, 0, 0)
    all_ = lambda r, *_: (0, 0, 0)
    return pl.pallas_call(
        attn_fwd_kernel,
        grid_spec=pltpu.PrefetchScalarGridSpec(
            num_scalar_prefetch=2,
            grid=(R,),
            in_specs=[
                pl.BlockSpec((1, L, D), lambda r, rows, win: (rows[r], 0, 0)),
                pl.BlockSpec((4, D, 768), all_),
                pl.BlockSpec((4, 1, 768), all_),
                pl.BlockSpec((4, PRE, 256), all_),
                pl.BlockSpec((4, PRE, 256), all_),
                pl.BlockSpec((1, L, 128), row),
                pl.BlockSpec((1, 1, L), row),
            ],
            out_specs=[
                pl.BlockSpec((1, 4, L, 768), lambda r, *_: (r, 0, 0, 0)),
                pl.BlockSpec((1, L, D), row),
                pl.BlockSpec((1, 4, 4, L), lambda r, *_: (r, 0, 0, 0)),
            ],
            scratch_shapes=[pltpu.VMEM((D, L + PRE), bf16)],
        ),
        out_shape=[
            jax.ShapeDtypeStruct((R, 4, L, 768), bf16),
            jax.ShapeDtypeStruct((R, L, D), bf16),
            jax.ShapeDtypeStruct((R, 4, 4, L), f32),
        ],
        compiler_params=pltpu.CompilerParams(vmem_limit_bytes=60 << 20),
        name="attn_fwd",
    )(rows, win, x, w, b, pk, pv, segk, segq)


NB = 8


def split3(v, index):
    high = v.astype(bf16)
    rest = v - high.astype(f32)
    mid = rest.astype(bf16)
    low = (rest - mid.astype(f32)).astype(bf16)
    return jnp.where(index % 3 == 0, high.astype(f32), jnp.where(index % 3 == 1, mid.astype(f32), low.astype(f32)))


def attn_bwd_kernel(
    row, parts, info, win, qkv_h, ctx_h, lse, gf_a, pk, pv, qcol, krow, wo_h, w_h, *rest
):
    qa, da, qt, dt, dq, dkt, dvt, qkv, gfirst, w, sem = rest[-11:]
    wo, ctx = dkt, dvt
    half = L // 2
    if row == 0:
        gin, own, pgrad = rest[-14:-11]
        moves = [(gf_a, gfirst)]
    else:
        gf_s, out_u, out_s = rest[:3]
        gin, out, pgrad, stage, osem = rest[-16:-11]
        moves = [
            (gf_a, gfirst.at[pl.ds(pl.multiple_of(info[2] * half, half), half)]),
            (gf_s, gfirst.at[pl.ds(pl.multiple_of(info[3] * half, half), half)]),
        ]
    moves += [(wo_h, wo), (ctx_h.at[row], ctx), (qkv_h.at[row], qkv), (w_h, w)]
    moves = [pltpu.make_async_copy(src, dst, sem.at[i]) for i, (src, dst) in enumerate(moves)]
    for c in moves:
        c.start()
    if row == 1:
        arrived = [
            pltpu.make_async_copy(out_u, stage.at[0:L], osem.at[0]),
            pltpu.make_async_copy(out_s, stage.at[L : L + TM], osem.at[1]),
        ]
        placed = [
            pltpu.make_async_copy(stage.at[0:L], out.at[2 - info[0]], osem.at[2]),
            pltpu.make_async_copy(
                stage.at[L : L + TM], out.at[1, pl.ds(pl.multiple_of(info[3] * TM, TM), TM)], osem.at[3]
            ),
        ]
        for c in arrived:
            c.start()
    for c in moves[:-2]:
        c.wait()

    at = lambda i, n: (i % 64 < 6) & (i // 64 * 2 + i % 64 // 3 == n)
    for g in range(4):
        cols = slice(256 * g, 256 * g + 256)
        part = nt(gfirst[...], wo[cols, :]).astype(bf16)
        prod = part.astype(f32) * ctx[:, cols].astype(f32)
        high = prod.astype(bf16)
        low = (prod - high.astype(f32)).astype(bf16)
        r = lax.broadcasted_iota(jnp.int32, (256, 128), 0)
        c = lax.broadcasted_iota(jnp.int32, (256, 128), 1)
        pick = jnp.where(at(c, r // 64), 1.0, 0.0).astype(bf16)
        sums = nn(high, pick) + nn(low, pick)
        da[g, :, 0:128] = part[:, :128]
        da[g, :, 128:256] = split3(sums, lax.broadcasted_iota(jnp.int32, (L, 128), 1) % 64).astype(bf16)
        da[g, :, 256:384] = part[:, 128:]
        dt[cols, :] = part.T
    moves[-2].wait()
    for g in range(4):
        index = lax.broadcasted_iota(jnp.int32, (128, L), 0)
        logs = jnp.zeros((128, L), f32)
        for n in range(4):
            logs = jnp.where(at(index, n), lse[0, g, n : n + 1, :], logs)
        qa[g, :, 0:128] = qkv[g, :, 0:128]
        qa[g, :, 128:256] = split3(logs, index % 64).T.astype(bf16)
        qa[g, :, 256:384] = qkv[g, :, 128:256]
        qt[256 * g : 256 * g + 256, :] = qkv[g, :, 0:256].T

    def widen(tile, side):
        r = lax.broadcasted_iota(jnp.int32, (256, 128), 0)
        c = lax.broadcasted_iota(jnp.int32, (256, 128), 1)
        minus = jnp.where(at(c, 2 * side + r // 128), -1.0, 0.0).astype(bf16)
        two = stack_heads(tile)
        return two, jnp.concatenate([two, minus] if side == 0 else [minus, two], axis=1)

    def blocks(jobs, mask, q0, W, first):
        here = pl.ds(q0, W)
        stage_ = []
        for p, g, side, kt, vt in jobs:
            lanes = slice(128 * side, 128 * side + 256)
            k2, ka = widen(kt, side)
            stage_.append((k2, nt(qa[g, here, lanes], ka), nt(da[g, here, lanes], widen(vt, side)[1])))
        probs = []
        for k2, s, dp in stage_:
            e = [jnp.exp(jnp.where(mask, s[:, 128 * h : 128 * h + 128], NEG)) for h in range(2)]
            ds = [(e[h] * dp[:, 128 * h : 128 * h + 128]).astype(bf16) for h in range(2)]
            probs.append((jnp.concatenate([v.astype(bf16) for v in e], axis=1), jnp.concatenate(ds, axis=1)))
        res = []
        for (p, g, side, _, _), (pb, db) in zip(jobs, probs):
            r0 = pl.ds(pl.multiple_of(p * 128, 128), 128)
            dv = nn(dt[r0, here], pb)
            dk = nn(qt[r0, here], db)
            res.append([jnp.concatenate([v[:64, :128], v[64:, 128:]], axis=0) for v in (dk, dv)])
        for (p, g, side, _, _), (k2, _, _), (pb, db) in zip(jobs, stage_, probs):
            r0 = pl.ds(pl.multiple_of(p * 128, 128), 128)
            part = nn(db, k2)
            if first:
                dq[here, r0] = part
            else:
                dq[here, r0] += part
        return res

    def prefix(i, carry):
        jobs = []
        pad = jnp.zeros((128 - PRE, 128), bf16)
        for j in range(NB):
            p = i * NB + j
            g, side = p // 2, j % 2
            lanes = slice(128 * side, 128 * side + 128)
            jobs.append((p, g, side, *(jnp.concatenate([v[g, :, lanes], pad], axis=0) for v in (pk, pv))))
        total = None
        for c in range(2):
            real = lax.broadcasted_iota(jnp.int32, (half, 128), 1) < PRE
            part = blocks(jobs, real, c * half, half, True)
            total = part if total is None else [[a + b for a, b in zip(u, v)] for u, v in zip(total, part)]
        for (p, *_), both in zip(jobs, total):
            for n in range(2):
                pgrad[n, :, pl.ds(pl.multiple_of(p * 128, 128), 128)] = both[n].T[:PRE]
        return carry

    lax.fori_loop(0, 8 // NB, prefix, 0)
    if row == 0:
        r0 = pl.multiple_of(info[4] * parts, 8)
        own[L:] = jnp.concatenate([pgrad[0, pl.ds(r0, parts), :], pgrad[1, pl.ds(r0, parts), :]], axis=0).astype(bf16)
    else:
        for c, d in zip(arrived, placed):
            c.wait()
            d.start()

    def tile(t, carry):
        start = win[row, t, 0]
        size = win[row, 8 + t, 0]
        k0 = pl.multiple_of(t * BLK, BLK)
        q0 = pl.multiple_of(start * BLK, BLK)

        def run(n):
            W = n * BLK
            mask = qcol[0, pl.ds(q0, W), :] == krow[0, :, pl.ds(k0, BLK)]

            many = NB if n <= 5 else NB // 2

            def batch(i, carry):
                jobs = []
                for j in range(many):
                    p = i * many + j
                    g, side = p // 2, j % 2
                    kt = qkv[g, pl.ds(k0, BLK), 256 + 128 * side : 384 + 128 * side]
                    vt = qkv[g, pl.ds(k0, BLK), 512 + 128 * side : 640 + 128 * side]
                    jobs.append((p, g, side, kt, vt))
                for (p, *_), (dk, dv) in zip(jobs, blocks(jobs, mask, q0, W, False)):
                    r0 = pl.ds(pl.multiple_of(p * 128, 128), 128)
                    dkt[r0, pl.ds(k0, BLK)] = dk.astype(bf16)
                    dvt[r0, pl.ds(k0, BLK)] = dv.astype(bf16)
                return carry

            lax.fori_loop(0, 8 // many, batch, 0)

        for n in CLASSES:
            pl.when(size == n)(functools.partial(run, n))
        return carry

    lax.fori_loop(0, L // BLK, tile, 0)
    moves[-1].wait()
    for g in range(4):
        cols = slice(256 * g, 256 * g + 256)
        qkv[g, :, 0:256] = (dq[:, cols] * 0.125).astype(bf16)
        qkv[g, :, 256:512] = dkt[cols, :].T
        qkv[g, :, 512:768] = dvt[cols, :].T
    for c in range(2):
        cols = slice(512 * c, 512 * c + 512)
        acc = gfirst[:, cols].astype(f32)
        for i in range(4):
            acc = acc + nt(qkv[i], w[i, cols, :])
        low = acc.astype(bf16)
        gin[0, :, cols] = low
        if row == 0:
            own[:L, cols] = low
    if row == 1:
        for c in placed:
            c.wait()


def attn_bwd(r, parts, info, win, qkv, ctx, lse, gf, pk, pv, qcol, krow, wo, w, more=()):
    row = lambda i, *_: (r, 0, 0)
    row4 = lambda i, *_: (r, 0, 0, 0)
    all_ = lambda i, *_: (0, 0, 0)
    any_ = pl.BlockSpec(memory_space=pl.ANY)
    shape = jax.ShapeDtypeStruct
    rows = pl.BlockSpec((1, L, D), lambda i, info, win: (info[r], 0, 0))
    grads = pl.BlockSpec((2, PRE, D), all_)
    if r == 0:
        out_specs = [rows, pl.BlockSpec((L + 2 * parts, D), lambda i, *_: (0, 0)), grads]
        out_shape = [shape((3, L, D), bf16), shape((L + 2 * parts, D), bf16), shape((2, PRE, D), f32)]
        scratch = []
    else:
        out_specs = [rows, any_, grads]
        out_shape = [shape((3, L, D), bf16), shape((3, L, D), bf16), shape((2, PRE, D), f32)]
        scratch = [pltpu.VMEM((L + TM, D), bf16), pltpu.SemaphoreType.DMA((4,))]
    return pl.pallas_call(
        functools.partial(attn_bwd_kernel, r, parts),
        grid_spec=pltpu.PrefetchScalarGridSpec(
            num_scalar_prefetch=2,
            grid=(1,),
            in_specs=[
                any_,
                any_,
                pl.BlockSpec((1, 4, 4, L), row4),
                any_,
                pl.BlockSpec((4, PRE, 256), all_),
                pl.BlockSpec((4, PRE, 256), all_),
                pl.BlockSpec((1, L, 128), row),
                pl.BlockSpec((1, 1, L), row),
                any_,
                any_,
            ]
            + [any_ for _ in more],
            out_specs=out_specs,
            scratch_shapes=scratch
            + [
                pltpu.VMEM((4, L, 384), bf16),
                pltpu.VMEM((4, L, 384), bf16),
                pltpu.VMEM((D, L), bf16),
                pltpu.VMEM((D, L), bf16),
                pltpu.VMEM((L, D), f32),
                pltpu.VMEM((D, L), bf16),
                pltpu.VMEM((D, L), bf16),
                pltpu.VMEM((4, L, 768), bf16),
                pltpu.VMEM((L, D), bf16),
                pltpu.VMEM((4, D, 768), bf16),
                pltpu.SemaphoreType.DMA((6,)),
            ],
        ),
        out_shape=out_shape,
        input_output_aliases={15: 0, 16: 1} if more else {},
        compiler_params=pltpu.CompilerParams(vmem_limit_bytes=60 << 20),
        cost_estimate=pl.CostEstimate(flops=40 * 10**9, bytes_accessed=32 << 20, transcendentals=0),
        name="attn_bwd",
    )(info, win, qkv, ctx, lse, gf, pk, pv, qcol, krow, wo, w, *more)


HC = 512
TM = 512
EPS = 1e-5


ERF = (0.797881942323396, 0.036345746572412886, -4.589167395636408e-05, -5.002340812775584e-05,
       3.05428266992555e-06, -6.449413176560626e-08)


def gelu_parts(v):
    u = v * v
    w = jnp.minimum(u, 31.36)
    p = ERF[5] * w + ERF[4]
    for c in ERF[3::-1]:
        p = p * w + c
    phi = 0.5 * jnp.tanh(v * p) + 0.5
    return v * phi, phi


def norm_stats(z):
    mean = jnp.mean(z, axis=1, keepdims=True)
    c = z - mean
    var = jnp.mean(c * c, axis=1, keepdims=True)
    r = lax.rsqrt(var + EPS)
    return c * r, r


def tokens_kernel(shared, info, ctx_h, x_h, cot_h, wo_h, win_h, wout_h, bo, g1, s1, bi, b2, g2, s2, *rest):
    out, own, gf, ctx, x, cot, wo, win, wout, xhat, zbuf, low, act, gp, rs, vb, wsem, tsem = rest[-18:]
    tiles = own.shape[0] // TM
    r, row = (1, info[1]) if shared else (0, info[0])
    at = pl.multiple_of(info[2] * TM, TM) if shared else 0
    M = TM
    fetch_o = pltpu.make_async_copy(wo_h, wo, wsem.at[0])
    fetch_i = [pltpu.make_async_copy(win_h.at[i], win.at[i], wsem.at[1 + i]) for i in range(4)]
    fetch_u = [
        pltpu.make_async_copy(wout_h.at[pl.ds(1024 * i, 1024)], wout.at[pl.ds(1024 * i, 1024)], wsem.at[5 + i])
        for i in range(4)
    ]
    part = lambda j: slice(j * TM, j * TM + TM)
    fetch = lambda src, k, dst, j, i: pltpu.make_async_copy(
        src.at[k, pl.ds(at + j * TM, TM)], dst.at[part(j)], tsem.at[4 * j + i]
    )
    fetch_c = [fetch(ctx_h, r, ctx, j, 0) for j in range(tiles)]
    fetch_x = [fetch(x_h, row, x, j, 1) for j in range(tiles)]
    fetch_t = [fetch(cot_h, row, cot, j, 2) for j in range(tiles)]
    result = [
        pltpu.make_async_copy(own.at[part(j)], out.at[row, pl.ds(at + j * TM, TM)], tsem.at[4 * j + 3])
        for j in range(tiles)
    ]
    for c in [fetch_c[0], fetch_o, fetch_x[0]] + fetch_i + [fetch_t[0]] + fetch_u + fetch_c[1:] + fetch_x[1:] + fetch_t[1:]:
        c.start()

    for j in range(tiles):
        at_j = part(j)
        if j == 0:
            fetch_o.wait()
        fetch_c[j].wait()
        fetch_x[j].wait()
        for c0 in range(0, D, 256):
            cols = slice(c0, c0 + 256)
            zbuf[:, cols] = nn(ctx[at_j], wo[:, cols]) + x[at_j, cols].astype(f32)

        n, r_ = norm_stats(zbuf[...] + bo[...])
        xhat[...] = n
        rs[...] = jnp.broadcast_to(r_, (M, 128))
        y = n * g1[...] + s1[...]
        zbuf[...] = y
        low[...] = y.astype(bf16)

        early = fetch_i if tiles > 1 else fetch_i + fetch_u + fetch_t
        if j == 0:
            for c in early:
                c.wait()
        for i in range(8):
            z, c = i // 2, i % 2
            cols = slice(i * HC, i * HC + HC)
            h = nn(low[...], win[z, :, c * HC : c * HC + HC]) + bi[z, :, 768 + c * HC : 768 + c * HC + HC]
            a, phi = gelu_parts(h)
            act[:, cols] = a.astype(bf16)
            gp[:, cols] = phi.astype(bf16)
            vb[:, cols] = h.astype(bf16)

        if j == 0 and tiles > 1:
            for c in fetch_u:
                c.wait()
        for c0 in range(0, D, 256):
            cols = slice(c0, c0 + 256)
            zbuf[:, cols] += nn(act[...], wout[:, cols])

        if tiles > 1:
            fetch_t[j].wait()
        n, r_ = norm_stats(zbuf[...] + b2[...])
        own[at_j] = (n * g2[...] + s2[...]).astype(bf16)
        result[j].start()
        g = cot[at_j].astype(f32) * g2[...]
        m1 = jnp.mean(g, axis=1, keepdims=True)
        m2 = jnp.mean(g * n, axis=1, keepdims=True)
        d = (g - m1 - n * m2) * r_
        zbuf[...] = d
        low[...] = d.astype(bf16)

        for i in range(8):
            cols = slice(i * HC, i * HC + HC)
            d = nt(low[...], wout[cols, :])
            v = vb[:, cols].astype(f32)
            slope = gp[:, cols].astype(f32) + v * (jnp.exp(-0.5 * v * v) * 0.3989422804014327)
            act[:, cols] = (d * slope).astype(bf16)

        for c0 in range(0, D, 256):
            cols = slice(c0, c0 + 256)
            acc = zbuf[:, cols]
            for z in range(4):
                acc = acc + nt(act[:, 1024 * z : 1024 * z + 1024], win[z, cols, :])
            zbuf[:, cols] = acc

        n = xhat[...]
        g = zbuf[...] * g1[...]
        m1 = jnp.mean(g, axis=1, keepdims=True)
        m2 = jnp.mean(g * n, axis=1, keepdims=True)
        gf[at_j] = ((g - m1 - n * m2) * rs[:, 0:1]).astype(bf16)
    for c in result:
        c.wait()


def tokens(shared, info, ctx, x, cot, wo, win, wout, bo, g1, s1, bi, b2, g2, s2, into=None):
    n = TM if shared else L
    any_ = pl.BlockSpec(memory_space=pl.ANY)
    whole = lambda a: pl.BlockSpec(a.shape, lambda i, info: (0,) * a.ndim)
    block = pl.BlockSpec((n, D), lambda i, info: (0, 0))
    vectors = (bo, g1, s1, bi, b2, g2, s2)
    extra = [] if into is None else [into]
    return pl.pallas_call(
        functools.partial(tokens_kernel, shared),
        grid_spec=pltpu.PrefetchScalarGridSpec(
            num_scalar_prefetch=1,
            grid=(1,),
            in_specs=[any_] * 6 + [whole(a) for a in vectors] + [any_ for _ in extra],
            out_specs=[any_, block, block],
            scratch_shapes=[
                pltpu.VMEM((n, D), bf16),
                pltpu.VMEM((n, D), bf16),
                pltpu.VMEM((n, D), bf16),
                pltpu.VMEM((D, D), bf16),
                pltpu.VMEM((4, D, D), bf16),
                pltpu.VMEM((4 * D, D), bf16),
                pltpu.VMEM((TM, D), f32),
                pltpu.VMEM((TM, D), f32),
                pltpu.VMEM((TM, D), bf16),
                pltpu.VMEM((TM, 4 * D), bf16),
                pltpu.VMEM((TM, 4 * D), bf16),
                pltpu.VMEM((TM, 128), f32),
                pltpu.VMEM((TM, 4 * D), bf16),
                pltpu.SemaphoreType.DMA((9,)),
                pltpu.SemaphoreType.DMA((8,)),
            ],
        ),
        out_shape=[
            jax.ShapeDtypeStruct((3, L, D), bf16),
            jax.ShapeDtypeStruct((n, D), bf16),
            jax.ShapeDtypeStruct((n, D), bf16),
        ],
        input_output_aliases={14: 0} if extra else {},
        compiler_params=pltpu.CompilerParams(vmem_limit_bytes=60 << 20),
        cost_estimate=pl.CostEstimate(flops=(n // TM) * 25 * 10**9, bytes_accessed=24 << 20, transcendentals=0),
        name="tokens",
    )(info, ctx, x, cot, wo, win, wout, *vectors, *extra)


SPAN = 512
KINDS = 10


def front_kernel(
    hid, seg, msk, pk_s, pv_s, bq, bk, bv, bi, wq, wk, wv, wo_s, wi_s, wu_s,
    wqkv, wo, wi, wu, qkv, ctx, lse, pk, pv, vec, segk, segq, wins, qcol, krow,
    own0, x, wbuf, qb, vt, cb, pre, xsem, lsem, osem, ssem, rsem,
):
    d = lax.axis_index("dp")
    z = lax.axis_index("prefix")
    core, xx, yy = d % 2, (d // 2) % 2, d // 4
    dc = d + 1 - 2 * core
    dx = d + 2 - 4 * xx
    dy = d + 4 - 8 * yy
    dxy = dx + dy - d
    unique = 2 * (z % 2)
    MESH = pl.DeviceIdType.MESH

    def region(pay, zz, dd, half=None):
        if pay in (4, 5):
            return (pre, vec)[pay - 4].at[zz]
        if pay == 0:
            n, ref = 128, lambda o, s: wqkv.at[zz, pl.ds(128 * dd + o, s), :]
        elif pay == 1:
            n, ref = 256, lambda o, s: wo.at[pl.ds(256 * zz + o, s), pl.ds(128 * dd, 128)]
        elif pay == 2:
            n, ref = 128, lambda o, s: wi.at[zz, pl.ds(128 * dd + o, s), :]
        else:
            o0 = 0 if pay == 3 else 512
            n, ref = 512, lambda o, s: wu.at[pl.ds(1024 * zz + o0 + o, s), pl.ds(128 * dd, 128)]
        return ref(0, n) if half is None else ref(half * (n // 2), n // 2)

    def rows_of(zz, c):
        return wu.at[pl.ds(1024 * zz + 512 + 256 * c, 256), :]

    own0[:, 0:256] = wq[...]
    own0[:, 256:512] = wk[...]
    own0[:, 512:768] = wv[...]
    shards = {0: own0, 1: wo_s, 2: wi_s, 3: wu_s.at[0:512], 6: wu_s.at[512:1024]}
    xin = [pltpu.make_async_copy(hid.at[unique], x.at[0], xsem.at[0]), pltpu.make_async_copy(hid.at[1], x.at[1], xsem.at[1])]
    for c in xin:
        c.start()

    bar = pltpu.get_barrier_semaphore()

    def hello(dev):
        pl.semaphore_signal(bar, inc=1, device_id=dev, device_id_type=MESH)

    for dd in (dc, dx, dy):
        hello((dd, z))
    pl.when(z > 0)(lambda: hello((d, z - 1)))
    pl.when(z < 3)(lambda: hello((d, z + 1)))

    pre[z, 0:24, :] = pk_s[...]
    pre[z, 32:56, :] = pv_s[...]
    vec[z, :, 0:256] = bq[...]
    vec[z, :, 256:512] = bk[...]
    vec[z, :, 512:768] = bv[...]
    vec[z, :, 768:] = bi[...]
    for r in range(2):
        own = seg[pl.ds(unique, 1), :] if r == 0 else seg[1:2, :]
        real = msk[pl.ds(unique, 1), :] if r == 0 else msk[1:2, :]
        segq[r] = own.astype(f32)
        keys = jnp.where(real == 1, own, -1).astype(f32)
        segk[r] = jnp.broadcast_to(keys, (128, L)).T
        qcol[r] = jnp.broadcast_to(own.astype(f32), (128, L)).T
        krow[r] = keys
        line = own.astype(f32)
        for t in range(L // BLK):
            first, last = line[:, t * BLK : t * BLK + 1], line[:, t * BLK + BLK - 1 : t * BLK + BLK]
            begin = jnp.floor(jnp.sum(jnp.where(line < first, 1.0, 0.0), axis=1, keepdims=True) / BLK)
            stop = jnp.floor((jnp.sum(jnp.where(line <= last, 1.0, 0.0), axis=1, keepdims=True) + (BLK - 1)) / BLK)
            size = jnp.full_like(begin, float(CLASSES[-1]))
            for n in reversed(CLASSES[:-1]):
                size = jnp.where(stop - begin <= n, float(n), size)
            begin = jnp.minimum(begin, L // BLK - size)
            wins[r, t : t + 1, :] = jnp.broadcast_to(begin, (1, 128)).astype(jnp.int32)
            wins[r, 8 + t : 9 + t, :] = jnp.broadcast_to(size, (1, 128)).astype(jnp.int32)

    local = [pltpu.make_async_copy(src, region(p, z, d), lsem.at[i]) for i, (p, src) in enumerate(shards.items())]
    for c in local:
        c.start()
    peers = jnp.where(z > 0, 1, 0) + jnp.where(z < 3, 1, 0)
    pl.semaphore_wait(bar, 3 + peers)

    def copy(kind, pay, zz, dd, half, dev, skind, src=None):
        r = region(pay, zz, dd, half)
        return pltpu.make_async_remote_copy(
            src_ref=r if src is None else src, dst_ref=r, send_sem=ssem.at[pay * 4 + zz, skind], recv_sem=rsem.at[pay * 4 + zz, kind],
            device_id=dev, device_id_type=MESH,
        )

    def block(k):
        second = jnp.where(z == 0, 1, z - 1)
        third = jnp.where(z == 0, 2, jnp.where(z == 3, 1, z + 1))
        last = jnp.where(z <= 1, 3, 0)
        return jnp.where(k == 0, z, jnp.where(k == 1, second, jnp.where(k == 2, third, last)))

    def up(pay, zz, src=None):
        return copy(0, pay, zz, d, None, (d, z + 1), 10, src)

    def down(pay, zz, src=None):
        return copy(0, pay, zz, d, None, (d, z - 1), 0, src)

    def along(pay, h):
        @pl.when(z >= h)
        def _():
            up(pay, z - h).wait_recv()
            pl.when(z < 3)(lambda: up(pay, z - h).start())

        @pl.when(z + h <= 3)
        def _():
            down(pay, z + h).wait_recv()
            pl.when(z > 0)(lambda: down(pay, z + h).start())

    def stage1(pay, k, src=None):
        zz = block(k)
        copy(1, pay, zz, d, None, (dx, z), 1, src).start()
        copy(2, pay, zz, d, None, (dy, z), 2, src).start()
        copy(5, pay, zz, d, None, (dc, z), 5, src).start()

    def stage2(pay, k):
        zz = block(k)
        copy(1, pay, zz, dx, None, (dx, z), 1).wait_recv()
        copy(3, pay, zz, dx, 0, (dy, z), 3).start()
        copy(6, pay, zz, dx, None, (dc, z), 6).start()
        copy(2, pay, zz, dy, None, (dy, z), 2).wait_recv()
        copy(4, pay, zz, dy, 1, (dx, z), 4).start()
        copy(7, pay, zz, dy, None, (dc, z), 7).start()

    def stage3(pay, k):
        zz = block(k)
        copy(3, pay, zz, dxy, 0, (dy, z), 3).wait_recv()
        copy(8, pay, zz, dxy, 0, (dc, z), 8).start()
        copy(4, pay, zz, dxy, 1, (dx, z), 4).wait_recv()
        copy(9, pay, zz, dxy, 1, (dc, z), 9).start()

    def stage4(pay, k):
        zz = block(k)
        o = dc - d
        copy(5, pay, zz, d + o, None, (dc, z), 5).wait_recv()
        copy(6, pay, zz, dx + o, None, (dc, z), 6).wait_recv()
        copy(7, pay, zz, dy + o, None, (dc, z), 7).wait_recv()
        copy(8, pay, zz, dxy + o, 0, (dc, z), 8).wait_recv()
        copy(9, pay, zz, dxy + o, 1, (dc, z), 9).wait_recv()

    def haul(zz, dz, kind):
        r = rows_of(zz, core)
        return pltpu.make_async_remote_copy(
            src_ref=r, dst_ref=r, send_sem=ssem.at[24 + zz, kind], recv_sem=rsem.at[24 + zz, 0],
            device_id=(d, z + dz), device_id_type=MESH,
        )

    def share(zz, c):
        r = rows_of(zz, c)
        return pltpu.make_async_remote_copy(
            src_ref=r, dst_ref=r, send_sem=ssem.at[24 + zz, 5], recv_sem=rsem.at[24 + zz, 5],
            device_id=(dc, z), device_id_type=MESH,
        )

    def haul_on(h):
        @pl.when(z >= h)
        def _():
            haul(z - h, 1, 10).wait_recv()
            pl.when(z < 3)(lambda: haul(z - h, 1, 10).start())
            share(z - h, core).start()

        @pl.when(z + h <= 3)
        def _():
            haul(z + h, -1, 0).wait_recv()
            pl.when(z > 0)(lambda: haul(z + h, -1, 0).start())
            share(z + h, core).start()

    def drain(pay, zz):
        if pay != 6:
            pl.when((zz <= z) & (z < 3))(lambda: up(pay, zz).wait_send())
            pl.when((zz >= z) & (z > 0))(lambda: down(pay, zz).wait_send())
        if pay in (4, 5):
            return
        copy(1, pay, zz, d, None, (dx, z), 1).wait_send()
        copy(2, pay, zz, d, None, (dy, z), 2).wait_send()
        copy(3, pay, zz, dx, 0, (dy, z), 3).wait_send()
        copy(4, pay, zz, dy, 1, (dx, z), 4).wait_send()
        copy(5, pay, zz, d, None, (dc, z), 5).wait_send()
        copy(6, pay, zz, dx, None, (dc, z), 6).wait_send()
        copy(7, pay, zz, dy, None, (dc, z), 7).wait_send()
        copy(8, pay, zz, dxy, 0, (dc, z), 8).wait_send()
        copy(9, pay, zz, dxy, 1, (dc, z), 9).wait_send()

    ffn = (2, 3, 1)
    ffn = (2, 3, 1)

    def set_out(pay):
        src = shards.get(pay)
        pl.when(z < 3)(lambda: up(pay, z, src).start())
        pl.when(z > 0)(lambda: down(pay, z, src).start())

    stage1(0, 0, own0)
    for pay in (0, 4, 5):
        set_out(pay)
    stage2(0, 0)
    for pay in (4, 5, 0):
        along(pay, 1)
    stage1(0, 1)
    stage3(0, 0)
    for pay in (4, 5):
        along(pay, 2)
    for pay in ffn:
        set_out(pay)
    for pay in (4, 5):
        along(pay, 3)
    stage1(2, 0, wi_s)
    for g in range(4):
        lanes = slice(256 * g, 256 * g + 256)
        for ref, o in ((pk, 0), (pv, 32)):
            parts = [pre[i, o : o + 32, lanes].astype(f32)[:24] for i in range(4)]
            ref[g] = jnp.concatenate(parts, axis=0).astype(bf16)
    for c in xin + local:
        c.wait()

    def outs(zz):
        q = [pltpu.make_async_copy(qb.at[r], qkv.at[r, zz], osem.at[r]) for r in range(2)]
        c = [
            pltpu.make_async_copy(cb.at[r], ctx.at[r, :, pl.ds(pl.multiple_of(256 * zz, 256), 256)], osem.at[2 + r])
            for r in range(2)
        ]
        return q, c

    def project(r, zz, slot):
        y = nn(x[r], wbuf[slot]) + vec[zz, :, 0:768]
        qb[r, :, 0:256] = (y[:, :256].astype(bf16) * 0.125).astype(bf16)
        kv = y[:, 256:].astype(bf16)
        qb[r, :, 256:] = kv
        vt[r, :, :L] = kv[:, 256:].T
        vt[r, :, L:] = pv[zz].T

    def attend(t, zz):
        jobs = []
        for tt in (t, L // BLK - 1 - t):
            first = max(0, tt - SPAN // BLK)
            stop = min(L // BLK, tt + SPAN // BLK + 1)
            k = slice(first * BLK, stop * BLK)
            q = slice(tt * BLK, tt * BLK + BLK)
            for r in range(2):
                seen = segk[r, k, :] == segq[r, :, q]
                for p in range(2):
                    lanes = slice(128 * p, 128 * p + 128)
                    q2 = stack_heads(qb[r, q, lanes])
                    s = nt(qb[r, k, 256 + 128 * p : 384 + 128 * p], q2)
                    jobs.append((r, p, q, k, lanes, seen, s, nt(pk[zz, :, lanes], q2)))
        stage = []
        for r, p, q, k, lanes, seen, s, sp in jobs:
            s = jnp.concatenate([jnp.where(seen, s[:, :128], NEG), jnp.where(seen, s[:, 128:], NEG)], axis=1)
            top = jnp.maximum(jnp.max(s, axis=0, keepdims=True), jnp.max(sp, axis=0, keepdims=True))
            stage.append((s, sp, top))
        probs = []
        for s, sp, top in stage:
            e = jnp.exp(s - top)
            ep = jnp.exp(sp - top)
            total = jnp.sum(e, axis=0, keepdims=True) + jnp.sum(ep, axis=0, keepdims=True)
            probs.append((e.astype(bf16), ep.astype(bf16), total, top))
        res = []
        for (r, p, q, k, lanes, _, _, _), (e, ep, total, top) in zip(jobs, probs):
            res.append(nn(vt[r, lanes, k], e) + nn(vt[r, lanes, L : L + PRE], ep))
        for (r, p, q, k, lanes, _, _, _), (e, ep, total, top), o in zip(jobs, probs, res):
            o = o * (1.0 / total)
            o = jnp.concatenate([o[:64, :128], o[64:, 128:]], axis=0)
            cb[r, q, lanes] = o.T.astype(bf16)
            lt = top + jnp.log(total)
            lse[r, zz, 2 * p : 2 * p + 1, q] = lt[:, :128]
            lse[r, zz, 2 * p + 1 : 2 * p + 2, q] = lt[:, 128:]

    plan = {
        (0, 0): [("z", 0, 2), (1, 0, 2)],
        (0, 1): [(2, 0, 1)],
        (0, 2): [("z", 0, 3), (1, 0, 3)],
        (0, 3): [(3, 0, 1), (2, 0, 2), (1, 3, 0)],
        (0, 4): [(1, 6, 0), (1, 1, 0)],
        (0, 5): [(2, 0, 3)],
        (1, 0): [(3, 0, 2), ("z", 2, 1), ("z", 3, 1), ("z", 1, 1), (1, 2, 1)],
        (1, 1): [(2, 2, 0), (1, 3, 1)],
        (1, 2): [(3, 0, 3), (1, 1, 1)],
        (1, 3): [(2, 3, 0), (2, 6, 0)],
        (1, 4): [(2, 1, 0)],
        (1, 5): [("z", 2, 2), ("z", 3, 2), ("z", 1, 2), (1, 2, 2), (1, 3, 2)],
        (2, 0): [(3, 2, 0), (3, 3, 0), (3, 6, 0)],
        (2, 1): [(2, 2, 1), (1, 1, 2), ("h", 6, 0)],
        (2, 2): [(2, 3, 1), (3, 1, 0)],
        (2, 3): [(2, 1, 1)],
        (2, 4): [("z", 2, 3), ("z", 3, 3), ("z", 1, 3), (1, 2, 3), (1, 3, 3), (1, 1, 3)],
        (2, 5): [(3, 2, 1), (3, 3, 1)],
        (3, 0): [("h", 6, 1), (2, 2, 2), (3, 1, 1)],
        (3, 1): [(2, 3, 2)],
        (3, 2): [(2, 1, 2)],
        (3, 3): [("h", 6, 2), (3, 2, 2)],
        (3, 4): [(2, 2, 3)],
        (3, 5): [(3, 3, 2), (3, 1, 2)],
        (4, 0): [(2, 3, 3), (2, 1, 3), ("h", 6, 3), (3, 2, 3), (3, 3, 3), (3, 1, 3)],
    }

    def act(what, pay, k):
        if what == "z":
            along(pay, k)
        elif what == "h" and k == 0:
            stage4(6, 0)
            pl.when(z < 3)(lambda: haul(z, 1, 10).start())
            pl.when(z > 0)(lambda: haul(z, -1, 0).start())
        elif what == "h":
            haul_on(k)
        elif what == 1:
            stage1(pay, k, shards[pay] if k == 0 else None)
        else:
            (stage2, stage3)[what - 2](pay, k)

    def group(s, carry):
        zz = block(s)

        def pump(slot):
            for i in range(4):

                @pl.when(s == i)
                def _():
                    for step in plan[i, slot]:
                        act(*step)

        def weights(k):
            return pltpu.make_async_copy(wqkv.at[block(k)], wbuf.at[k % 2], xsem.at[2 + k % 2])

        @pl.when(s == 0)
        def _():
            stage4(0, 0)
            weights(0).start()

        before = outs(block(s - 1))

        @pl.when(s > 0)
        def _():
            for o in before[0]:
                o.wait()

        weights(s).wait()
        project(0, zz, s % 2)
        pump(0)
        project(1, zz, s % 2)
        q, c = outs(zz)
        for o in q:
            o.start()
        pump(1)

        @pl.when(s > 0)
        def _():
            for o in before[1]:
                o.wait()

        for t in range(4):
            attend(t, zz)
            pump(2 + t)
            if t == 2:

                @pl.when(s < 3)
                def _():
                    stage4(0, s + 1)
                    weights(s + 1).start()

        for o in c:
            o.start()
        return carry

    lax.fori_loop(0, 4, group, 0)
    for step in plan[4, 0]:
        act(*step)
    q, c = outs(block(3))
    for o in q + c:
        o.wait()

    def finish(k, done):
        for pay in (1, 2, 3):
            stage4(pay, k)
        for pay in range(6):
            drain(pay, k)

        @pl.when(k == z)
        def _():
            drain(6, k)

        @pl.when(k != z)
        def _():
            share(k, 1 - core).wait_recv()
            share(k, core).wait_send()

        pl.when((k <= z) & (z < 3))(lambda: haul(k, 1, 10).wait_send())
        pl.when((k >= z) & (z > 0))(lambda: haul(k, -1, 0).wait_send())
        return done

    lax.fori_loop(0, 4, finish, 0)


def front(hid, seg, msk, pk, pv, bq, bk, bv, bi, wq, wk, wv, wo, wi, wu):
    any_ = pl.BlockSpec(memory_space=pl.ANY)
    vmem = pl.BlockSpec(memory_space=pltpu.VMEM)
    shape = jax.ShapeDtypeStruct
    return pl.pallas_call(
        front_kernel,
        in_specs=[any_] + [vmem] * 14,
        out_specs=[any_] * 6 + [vmem] * 9,
        out_shape=[
            shape((4, D, 768), bf16),
            shape((D, D), bf16),
            shape((4, D, D), bf16),
            shape((4 * D, D), bf16),
            shape((2, 4, L, 768), bf16),
            shape((2, L, D), bf16),
            shape((2, 4, 4, L), f32),
            shape((4, PRE, 256), bf16),
            shape((4, PRE, 256), bf16),
            shape((4, 1, 1792), f32),
            shape((2, L, 128), f32),
            shape((2, 1, L), f32),
            shape((2, 16, 128), jnp.int32),
            shape((2, L, 128), f32),
            shape((2, 1, L), f32),
        ],
        scratch_shapes=[
            pltpu.VMEM((128, 768), bf16),
            pltpu.VMEM((2, L, D), bf16),
            pltpu.VMEM((2, D, 768), bf16),
            pltpu.VMEM((2, L, 768), bf16),
            pltpu.VMEM((2, 256, L + PRE), bf16),
            pltpu.VMEM((2, L, 256), bf16),
            pltpu.VMEM((4, 64, D), bf16),
            pltpu.SemaphoreType.DMA((4,)),
            pltpu.SemaphoreType.DMA((5,)),
            pltpu.SemaphoreType.DMA((4,)),
            pltpu.SemaphoreType.DMA((28, KINDS + 1)),
            pltpu.SemaphoreType.DMA((28, KINDS)),
        ],
        compiler_params=pltpu.CompilerParams(
            collective_id=0, has_side_effects=True, vmem_limit_bytes=60 << 20
        ),
        name="front",
    )(hid, seg, msk, pk, pv, bq, bk, bv, bi, wq, wk, wv, wo, wi, wu)


def front_plain(rows, hid, seg, msk, pk, pv, bq, bk, bv, bi, wq, wk, wv, wo, wi, wu):
    over = lambda v, axis, at: lax.all_gather(v, axis, axis=at, tiled=True)
    each = lambda v: lax.all_gather(v, "prefix")
    wqkv = each(jnp.concatenate([over(w, "dp", 0) for w in (wq, wk, wv)], axis=1))
    vec = each(jnp.concatenate([bq, bk, bv, bi], axis=1))
    by_group = lambda p: over(p, "prefix", 0).reshape(PRE, 4, 256).transpose(1, 0, 2)
    pk, pv = by_group(pk), by_group(pv)
    segk = jnp.broadcast_to(jnp.where(msk == 1, seg, -1)[rows][:, :, None], (2, L, 128)).astype(f32)
    segq = seg[rows][:, None, :].astype(f32)
    win = windows(seg[rows])
    qkv, ctx, lse = attn_fwd(rows, win, hid, wqkv, vec[:, :, :768], pk, pv, segk, segq)
    wins = jnp.broadcast_to(jnp.concatenate([win[..., 0], win[..., 1]], axis=1)[:, :, None], (2, 16, 128))
    return (
        wqkv, over(over(wo, "dp", 1), "prefix", 0), each(over(wi, "dp", 0)), over(over(wu, "dp", 1), "prefix", 0),
        qkv, ctx, lse, pk, pv, vec, segk, segq, wins,
        jnp.broadcast_to(segq[:, 0, :, None], (2, L, 128)), segk[:, None, :, 0],
    )


def total_kernel(uniq, shared, came, key, value, other, both, mine, half, slots, osem, ssem, rsem):
    d = lax.axis_index("dp")
    z = lax.axis_index("prefix")
    core, chip = d % 2, d // 2
    xx, yy = chip % 2, chip // 2
    dc = d + 1 - 2 * core
    peers = [((d + 2 - 4 * xx), chip + 1 - 2 * xx), ((d + 4 - 8 * yy), chip + 2 - 4 * yy)]
    peers.append((peers[0][0] + peers[1][0] - d, 3 - chip))
    bar = pltpu.get_barrier_semaphore()
    for dd in (dc, *(p for p, _ in peers)):
        pl.semaphore_signal(bar, inc=1, device_id=(dd, z), device_id_type=pl.DeviceIdType.MESH)
    n = key.shape[0]
    r0 = pl.multiple_of(z * n, 8)
    fetch = [
        pltpu.make_async_copy(came.at[pl.ds(L, 2 * n)], other, osem.at[0]),
        pltpu.make_async_copy(uniq.at[:, pl.ds(r0, n), :], both.at[0], osem.at[1]),
        pltpu.make_async_copy(shared.at[:, pl.ds(r0, n), :], both.at[1], osem.at[2]),
    ]
    for c in fetch:
        c.start()
    for c in fetch:
        c.wait()
    add = other[...].astype(f32)
    for i in range(2):
        mine[i] = both[0, i] + both[1, i] + add[i * n : i * n + n]
    pl.semaphore_wait(bar, 4)

    def send(src, dst, i, dd):
        return pltpu.make_async_remote_copy(
            src_ref=src, dst_ref=dst, send_sem=ssem.at[i], recv_sem=rsem.at[i],
            device_id=(dd, z), device_id_type=pl.DeviceIdType.MESH,
        )

    first = send(mine.at[1 - core], half, 0, dc)
    first.start()
    first.wait()
    slots[chip] = mine[core] + half[...]
    copies = [send(slots.at[chip], slots.at[chip], 1 + i, dd) for i, (dd, _) in enumerate(peers)]
    for c in copies:
        c.start()
    for c in copies:
        c.wait()
    total = (slots[0] + slots[1]) + (slots[2] + slots[3])

    @pl.when(core == 0)
    def _():
        key[...] = total
        last = send(key, key, 4, dc)
        last.start()
        last.wait_send()
        send(value, value, 5, dc).wait_recv()

    @pl.when(core == 1)
    def _():
        value[...] = total
        last = send(value, value, 5, dc)
        last.start()
        last.wait_send()
        send(key, key, 4, dc).wait_recv()


def total_grads(uniq, shared, came):
    n = PRE // 4
    vmem = pl.BlockSpec(memory_space=pltpu.VMEM)
    return pl.pallas_call(
        total_kernel,
        in_specs=[pl.BlockSpec(memory_space=pl.ANY)] * 3,
        out_specs=[vmem] * 2,
        out_shape=[jax.ShapeDtypeStruct((n, D), f32)] * 2,
        scratch_shapes=[
            pltpu.VMEM((2 * n, D), bf16),
            pltpu.VMEM((2, 2, n, D), f32),
            pltpu.VMEM((2, n, D), f32),
            pltpu.VMEM((n, D), f32),
            pltpu.VMEM((4, n, D), f32),
            pltpu.SemaphoreType.DMA((3,)),
            pltpu.SemaphoreType.DMA((6,)),
            pltpu.SemaphoreType.DMA((6,)),
        ],
        compiler_params=pltpu.CompilerParams(
            collective_id=1, has_side_effects=True, vmem_limit_bytes=60 << 20
        ),
        name="total_grads",
    )(uniq, shared, came)


def body(
    hidden_in, cotangent, segment_ids, key_mask, prefix_keys, prefix_values,
    w_query, b_query, w_key, b_key, w_value, b_value, w_attn_out, b_attn_out, gain_attn, shift_attn,
    w_ffn_in, b_ffn_in, w_ffn_out, b_ffn_out, gain_ffn, shift_ffn,
):
    z = lax.axis_index("prefix")
    side = z % 2
    info = jnp.stack([2 * side, jnp.ones_like(side), side, 1 - side, z + 1 - 2 * side]).astype(jnp.int32)
    line = lambda v: v.reshape(1, -1)
    small = lax.axis_size("dp") == 8 and lax.axis_size("prefix") == 4
    start = front if small else functools.partial(front_plain, info[:2])
    w_qkv, w_out, w_up, w_down, qkv, ctx, lse, pk, pv, vec, _, _, win, qcol, krow = start(
        hidden_in, segment_ids, key_mask, prefix_keys, prefix_values,
        line(b_query), line(b_key), line(b_value), line(b_ffn_in),
        w_query, w_key, w_value, w_attn_out, w_ffn_in, w_ffn_out,
    )
    weights = (
        w_out, w_up, w_down, line(b_attn_out), line(gain_attn), line(shift_attn),
        vec, line(b_ffn_out), line(gain_ffn), line(shift_ffn),
    )
    pairs = [(i, i + 1 - 2 * (i % 2)) for i in range(lax.axis_size("prefix"))]
    swap = lambda v: lax.ppermute(v, "prefix", pairs)
    tie = lax.optimization_barrier
    args = (info, ctx, hidden_in, cotangent, *weights)
    out, out_s, gf_s = tokens(True, *args)
    out_s_other, gf_s_other = swap(out_s), swap(gf_s)
    out, out_u, gf_u = tokens(False, *args, into=out)
    out, out_s_other, gf_s_other, gf_u = tie((out, out_s_other, gf_s_other, gf_u))
    out_u_other = swap(out_u)
    parts = PRE // lax.axis_size("prefix")
    common = (pk, pv, qcol, krow, w_out, w_qkv)
    gin, gin_own, uniq = attn_bwd(0, parts, info, win, qkv, ctx, lse, gf_u, *common)
    gin, out_u_other = tie((gin, out_u_other))
    came = swap(gin_own)
    gin, out, shared = attn_bwd(
        1, parts, info, win, qkv, ctx, lse, gf_s, *common, more=(gf_s_other, out_u_other, out_s_other, gin, out)
    )
    if small:
        keys, values = total_grads(uniq, shared, came)
    else:
        own = lax.dynamic_slice_in_dim(uniq + shared, z * parts, parts, 1)
        keys, values = lax.psum(own + came[L:].reshape(2, parts, D).astype(f32), "dp")
    gin = lax.dynamic_update_slice(gin, came[None, :L], (2 - info[0], 0, 0))
    return out, gin, keys, values


def solution(mesh):
    return jax.shard_map(
        body,
        mesh=mesh,
        in_specs=(
            P("dp", None, None), P("dp", None, None), P("dp", None), P("dp", None),
            P("prefix", None), P("prefix", None),
            P("dp", "prefix"), P("prefix"), P("dp", "prefix"), P("prefix"), P("dp", "prefix"), P("prefix"),
            P("prefix", "dp"), P(), P(), P(),
            P("dp", "prefix"), P("prefix"), P("prefix", "dp"), P(), P(), P(),
        ),
        out_specs=(P("dp", None, None), P("dp", None, None), P("prefix", None), P("prefix", None)),
        check_vma=False,
    )
```
